32 devices in a mesh: seq: 4 (over y, x), fsdp: 8 (over z, core).
Axes of the slice: x: 2, y: 2, z: 4, core: 2. Of those that a mesh axis runs over, the one named last changes fastest.
Arguments:
- tokens: bfloat16 [8, 1024, 2048], P('fsdp', 'seq'), may hold values from -6 to 6
- segment_ids: int32 [8, 1024], P('fsdp'), may hold values from 0 to 6, as said below
- input_gain: float32 [2048], replicated, may hold values from 0.5 to 1.5
- query_weight: bfloat16 [2048, 2048], P('fsdp'), may hold values from -0.125 to 0.125
- key_projection_weight: bfloat16 [2048, 1024], P('fsdp'), may hold values from -0.125 to 0.125
- value_projection_weight: bfloat16 [2048, 1024], P('fsdp'), may hold values from -0.125 to 0.125
- output_weight: bfloat16 [2048, 2048], P('fsdp'), may hold values from -2 to 2
- query_gain: float32 [128], replicated, may hold values from 0.25 to 1.75
- key_gain: float32 [128], replicated, may hold values from 0.25 to 1.75
- post_gain: float32 [2048], replicated, may hold values from 0.5 to 1.5
- gate_weight: bfloat16 [2048, 6144], P('fsdp'), may hold values from -0.125 to 0.125
- up_weight: bfloat16 [2048, 6144], P('fsdp'), may hold values from -0.125 to 0.125
- down_weight: bfloat16 [2048, 6144], P('fsdp'), may hold values from -0.078125 to 0.078125
- cotangent: bfloat16 [8, 1024, 2048], P('fsdp', 'seq'), may hold values from -6 to 6
Outputs:
- output: bfloat16 [8, 1024, 2048], P('fsdp', 'seq')
- input_grad: bfloat16 [8, 1024, 2048], P('fsdp', 'seq')
- input_gain_grad: float32 [2048], replicated
- query_weight_grad: float32 [2048, 2048], P('fsdp')
- key_weight_grad: float32 [2048, 1024], P('fsdp')
- value_weight_grad: float32 [2048, 1024], P('fsdp')
- output_weight_grad: float32 [2048, 2048], P('fsdp')
- query_gain_grad: float32 [128], replicated
- key_gain_grad: float32 [128], replicated
- post_gain_grad: float32 [2048], replicated
- gate_weight_grad: float32 [2048, 6144], P('fsdp')
- up_weight_grad: float32 [2048, 6144], P('fsdp')
- down_weight_grad: float32 [2048, 6144], P('fsdp')
The draws below stay inside these ranges and needn't reach their ends.
Inputs may be any that keep to these rules, and one draw needn't show every extreme that they name: `segment_ids`: along each sequence the ids start at 0, never fall, and rise by one from one document to the next; documents after a sequence's first hold 200 to 2000 tokens, except the last, which the sequence's end may cut short; the first holds at most 2000. In one sequence of the batch, which one drawn from the seed, every id is 0; in another, documents after the first (the last aside) hold exactly 200 tokens and the largest id is reached.
All inputs are finite; a program needn't handle non-finite values.
Results may differ from the reference program's by a relative error of at most 0.02.
Values may be sent and summed in bfloat16 or wider, within the bound.
No kernel may reach another device: no remote copies, remote signals or barrier semaphores. Data moves between devices by JAX's collectives and lax.ppermute only.
A program may use at most 640 MiB of HBM per device.

```python
import jax
import jax.numpy as jnp
from jax import lax

MODEL_WIDTH = 2048
QUERY_HEADS = 16
KEY_VALUE_HEADS = 8
HEAD_SIZE = 128
FF = 6144
DOC_LO = 200
DOC_HI = 2000
LENGTH = 1024
SEQS = 8


def draw_segment_ids(key, part):
    key = jax.random.fold_in(key, 7)
    key_len, key_shift, key_whole, key_dense = jax.random.split(key, 4)
    docs = LENGTH // DOC_LO + 1
    spans = jax.random.randint(key_len, (SEQS, docs), DOC_LO, DOC_HI + 1)
    shifts = jax.random.randint(key_shift, (SEQS, 1), 0, DOC_LO)
    whole = jax.random.randint(key_whole, (), 0, SEQS)
    offset = jax.random.randint(key_dense, (), 1, SEQS)
    dense = (whole + offset) % SEQS
    rows = jnp.arange(SEQS, dtype=jnp.int32)
    spans = jnp.where(rows[:, None] == dense, DOC_LO, spans)
    shifts = jnp.where(rows[:, None] == dense, DOC_LO - 1, shifts)
    ends = jnp.cumsum(spans, axis=1) - shifts
    places = jnp.arange(LENGTH, dtype=jnp.int32)
    labels = jnp.sum((places[None, :, None] >= ends[:, None, :]).astype(jnp.int32), axis=2)
    labels = jnp.where(rows[:, None] == whole, 0, labels)
    return labels.astype(jnp.int32)


def block_levels(rng, dims, pieces, least, largest):
    factor_of = 1.0
    for dim, shards_of in pieces:
        heights = jax.random.uniform(jax.random.fold_in(jax.random.fold_in(rng, 6), dim), (shards_of,), jnp.float32, least / len(pieces), largest / len(pieces))
        factor_of = factor_of * jnp.repeat(jnp.exp(heights), dims[dim] // shards_of).reshape((-1,) + (1,) * (len(dims) - 1 - dim))
    return factor_of


def noise(own_key, extent, deviation, reach, cuts=(), kind=jnp.bfloat16):
    drawn = deviation * jax.random.normal(own_key, extent, jnp.float32)
    if cuts:
        drawn = drawn * block_levels(own_key, extent, cuts, -0.22, 0.18)
    return jnp.clip(drawn, -reach, reach).astype(kind)


def setup_inputs(seed: int = 0) -> dict:
    seeds = jax.random.split(jax.random.key(seed), 15)
    tokens = noise(seeds[0], (SEQS, LENGTH, MODEL_WIDTH), 1.0, 6.0, ((0, 8), (1, 4)))
    segment_ids = draw_segment_ids(jax.random.fold_in(seeds[14], 71), 0)
    input_gain = jnp.clip(1.0 + 0.1 * jax.random.normal(seeds[2], (MODEL_WIDTH,), jnp.float32), 0.5, 1.5)
    query_weight = noise(seeds[3], (MODEL_WIDTH, QUERY_HEADS * HEAD_SIZE), MODEL_WIDTH ** -0.5, 0.125, ((0, 8),))
    key_projection_weight = noise(seeds[4], (MODEL_WIDTH, KEY_VALUE_HEADS * HEAD_SIZE), MODEL_WIDTH ** -0.5, 0.125, ((0, 8),))
    value_projection_weight = noise(seeds[5], (MODEL_WIDTH, KEY_VALUE_HEADS * HEAD_SIZE), MODEL_WIDTH ** -0.5, 0.125, ((0, 8),))
    output_weight = noise(seeds[6], (MODEL_WIDTH, QUERY_HEADS * HEAD_SIZE), (max(1, QUERY_HEADS * HEAD_SIZE // 256)) ** -0.5, 2.0, ((0, 8),))
    query_gain = jnp.clip(1.0 + 0.15 * jax.random.normal(seeds[7], (HEAD_SIZE,), jnp.float32), 0.25, 1.75)
    key_gain = jnp.clip(1.0 + 0.15 * jax.random.normal(seeds[8], (HEAD_SIZE,), jnp.float32), 0.25, 1.75)
    post_gain = jnp.clip(1.0 + 0.1 * jax.random.normal(seeds[9], (MODEL_WIDTH,), jnp.float32), 0.5, 1.5)
    gate_weight = noise(seeds[10], (MODEL_WIDTH, FF), MODEL_WIDTH ** -0.5, 0.125, ((0, 8),))
    up_weight = noise(seeds[11], (MODEL_WIDTH, FF), MODEL_WIDTH ** -0.5, 0.125, ((0, 8),))
    down_weight = noise(seeds[12], (MODEL_WIDTH, FF), FF ** -0.5, 0.078125, ((0, 8),))
    cotangent = noise(seeds[13], (SEQS, LENGTH, MODEL_WIDTH), 1.0, 6.0, ((0, 8), (1, 4)))
    return dict(tokens=tokens, segment_ids=segment_ids, input_gain=input_gain, query_weight=query_weight, key_projection_weight=key_projection_weight, value_projection_weight=value_projection_weight, output_weight=output_weight, query_gain=query_gain, key_gain=key_gain, post_gain=post_gain, gate_weight=gate_weight, up_weight=up_weight, down_weight=down_weight, cotangent=cotangent)


NORM_EPSILON = 1e-06
ROPE_BASE = 1000000.0
SCORE_FLOOR = -1e+30
PRECISION_TOP = lax.Precision.HIGHEST

@jax.custom_vjp
def reduced_precision(v):
    return lax.optimization_barrier(v.astype(jnp.bfloat16)).astype(jnp.float32)

@jax.custom_vjp
def reduced_backward(v):
    return v

def low_keep(v):
    return (reduced_precision(v), None)

def low_pass(kept, grad):
    return (grad,)

def back_keep(v):
    return (v, None)

def back_low(kept, grad):
    return (reduced_precision(grad),)
reduced_precision.defvjp(low_keep, low_pass)
reduced_backward.defvjp(back_keep, back_low)

def apply_norm(values_in, gain):
    return values_in * lax.rsqrt(lax.optimization_barrier(jnp.mean(values_in * values_in, axis=-1, keepdims=True)) + NORM_EPSILON) * gain

def positions(segments):
    index = jnp.arange(segments.shape[0], dtype=jnp.int32)
    first = jnp.concatenate([jnp.ones((1,), dtype=jnp.bool_), segments[1:] != segments[:-1]])
    starts = lax.cummax(jnp.where(first, index, jnp.zeros_like(index)), axis=0)
    return index - starts

def apply_rotary(values_in, position_index):
    size = values_in.shape[-1]
    half = size // 2
    freq = ROPE_BASE ** (-jnp.arange(half, dtype=jnp.float32) * 2.0 / size)
    angle = position_index.astype(jnp.float32)[:, None] * freq[None, :]
    shape = (values_in.shape[0],) + (1,) * (values_in.ndim - 2) + (size,)
    cosine = jnp.concatenate([jnp.cos(angle), jnp.cos(angle)], axis=-1).reshape(shape)
    sine = jnp.concatenate([jnp.sin(angle), jnp.sin(angle)], axis=-1).reshape(shape)
    turned = jnp.concatenate([-values_in[..., half:], values_in[..., :half]], axis=-1)
    return values_in * cosine + turned * sine

def layer(inputs, segments, params):
    in_gain, query_w, key_matrix, value_matrix, out_w, query_gain_local, key_g, post_g, gate_w, up_w, down_w = params
    length_total = inputs.shape[0]
    normalized_input = reduced_precision(apply_norm(inputs, in_gain))
    query_rows = reduced_backward(reduced_precision(jnp.dot(normalized_input, query_w, precision=PRECISION_TOP))).reshape(length_total, QUERY_HEADS, HEAD_SIZE)
    key_rows = reduced_backward(reduced_precision(jnp.dot(normalized_input, key_matrix, precision=PRECISION_TOP))).reshape(length_total, KEY_VALUE_HEADS, HEAD_SIZE)
    value_rows = reduced_backward(reduced_precision(jnp.dot(normalized_input, value_matrix, precision=PRECISION_TOP))).reshape(length_total, KEY_VALUE_HEADS, HEAD_SIZE)
    position_index = positions(segments)
    rotated_query = reduced_precision(apply_rotary(apply_norm(query_rows, query_gain_local), position_index)).reshape(length_total, KEY_VALUE_HEADS, QUERY_HEADS // KEY_VALUE_HEADS, HEAD_SIZE)
    key_rot = reduced_precision(apply_rotary(apply_norm(key_rows, key_g), position_index))
    raw = reduced_backward(jnp.einsum('qgrd,kgd->grqk', rotated_query, key_rot, precision=PRECISION_TOP))
    scores = raw * HEAD_SIZE ** (-0.5)
    index = jnp.arange(length_total, dtype=jnp.int32)
    allowed = (segments[:, None] == segments[None, :]) & (index[None, :] <= index[:, None])
    scores = jnp.where(allowed, scores, SCORE_FLOOR)
    probs = jax.nn.softmax(scores, axis=-1)
    attended = jnp.einsum('grqk,kgd->qgrd', reduced_precision(probs), value_rows, precision=PRECISION_TOP)
    attended = reduced_backward(reduced_precision(attended)).reshape(length_total, QUERY_HEADS * HEAD_SIZE)
    residual = inputs + reduced_backward(jnp.dot(attended, out_w.T, precision=PRECISION_TOP))
    normed_two = reduced_precision(apply_norm(residual, post_g))
    gate = reduced_backward(jnp.dot(normed_two, gate_w, precision=PRECISION_TOP))
    upper = reduced_backward(jnp.dot(normed_two, up_w, precision=PRECISION_TOP))
    hidden = reduced_precision(jax.nn.silu(gate) * upper)
    return residual + reduced_backward(jnp.dot(hidden, down_w.T, precision=PRECISION_TOP))

def reference(tokens, segment_ids, input_gain, query_weight, key_projection_weight, value_projection_weight, output_weight, query_gain, key_gain, post_gain, gate_weight, up_weight, down_weight, cotangent):
    params = (input_gain.astype(jnp.float32), query_weight.astype(jnp.float32), key_projection_weight.astype(jnp.float32), value_projection_weight.astype(jnp.float32), output_weight.astype(jnp.float32), query_gain.astype(jnp.float32), key_gain.astype(jnp.float32), post_gain.astype(jnp.float32), gate_weight.astype(jnp.float32), up_weight.astype(jnp.float32), down_weight.astype(jnp.float32))
    inputs = tokens.astype(jnp.float32)

    def forward(values_in, weights_in):

        def step_one(carry, item):
            return (carry, jax.checkpoint(layer)(item[0], item[1], weights_in))
        _, result = lax.scan(step_one, jnp.zeros((), jnp.float32), (values_in, segment_ids))
        return result
    output, pullback = jax.vjp(forward, inputs, params)
    d_inputs, d_params = pullback(cotangent.astype(jnp.float32))
    return (output.astype(jnp.bfloat16), d_inputs.astype(jnp.bfloat16), d_params[0], d_params[1], d_params[2], d_params[3], d_params[4], d_params[5], d_params[6], d_params[7], d_params[8], d_params[9], d_params[10])
```

```python
import jax
import jax.numpy as jnp
from jax import lax
from jax.sharding import PartitionSpec as P

QUERY_HEADS = 16
KEY_VALUE_HEADS = 8
HEAD_SIZE = 128
NORM_EPSILON = 1e-06
ROPE_BASE = 1000000.0
SCORE_FLOOR = -1e30
F32 = jnp.float32
BF16 = jnp.bfloat16


def dot(a, b):
    return jnp.dot(a, b, preferred_element_type=F32)


def dot_nt(a, b):
    return lax.dot_general(a, b, (((1,), (1,)), ((), ())), preferred_element_type=F32)


def dot_tn(a, b):
    return lax.dot_general(a, b, (((0,), (0,)), ((), ())), preferred_element_type=F32)


def inverse_rms(u):
    return lax.rsqrt(jnp.mean(u * u, axis=-1, keepdims=True) + NORM_EPSILON)


def norm_back(u, gain, e):
    w = inverse_rms(u)
    n = u * w
    t = e * gain
    du = w * (t - n * jnp.mean(n * t, axis=-1, keepdims=True))
    return du, e * n


def positions(segments):
    index = jnp.arange(segments.shape[0], dtype=jnp.int32)
    first = jnp.concatenate([jnp.ones((1,), dtype=jnp.bool_), segments[1:] != segments[:-1]])
    starts = lax.cummax(jnp.where(first, index, jnp.zeros_like(index)), axis=0)
    return index - starts


def rotary_tables(position_index):
    half = HEAD_SIZE // 2
    freq = ROPE_BASE ** (-jnp.arange(half, dtype=F32) * 2.0 / HEAD_SIZE)
    angle = position_index.astype(F32)[:, None] * freq[None, :]
    cosine = jnp.concatenate([jnp.cos(angle), jnp.cos(angle)], axis=-1)
    sine = jnp.concatenate([jnp.sin(angle), jnp.sin(angle)], axis=-1)
    return cosine[:, None, :], sine[:, None, :]


def rotate(u, cosine, sine):
    half = HEAD_SIZE // 2
    turned = jnp.concatenate([-u[..., half:], u[..., :half]], axis=-1)
    return u * cosine + turned * sine


def rotate_back(e, cosine, sine):
    half = HEAD_SIZE // 2
    es = e * sine
    return e * cosine + jnp.concatenate([es[..., half:], -es[..., :half]], axis=-1)


def by_neighbours(count):
    return count == 4


def swap(x, side):
    return lax.ppermute(x, "seq", [(s, s ^ side) for s in range(4)])


def gather_slots(x, count):
    half = x.shape[0] // 2
    a, b = x[:half], x[half:]
    bx, ay = swap(b, 1), swap(a, 2)
    ax, by = swap(a, 1), swap(b, 2)
    ad = swap(ay, 1)
    bd = swap(bx, 2)
    return [[a, b], [ax, bx], [ay, by], [ad, bd]]


def gather_rows(x, count):
    if not by_neighbours(count):
        return lax.all_gather(x, "seq", axis=0, tiled=True)
    rows = x.shape[0]
    me = lax.axis_index("seq")
    out = jnp.zeros((count * rows,) + x.shape[1:], x.dtype)
    for k, pieces in enumerate(gather_slots(x, count)):
        for j, piece in enumerate(pieces):
            out = lax.dynamic_update_slice(out, piece, ((me ^ k) * rows + j * (rows // 2), 0))
    return out


def gather_columns(x, count):
    if not by_neighbours(count):
        return lax.all_gather(x, "seq", axis=1, tiled=True).astype(F32)
    rows, c = x.shape
    me = lax.axis_index("seq")
    out = jnp.zeros((rows, count * c), F32)
    for k, pieces in enumerate(gather_slots(x, count)):
        for j, piece in enumerate(pieces):
            out = lax.dynamic_update_slice(out, piece.astype(F32), (j * (rows // 2), (me ^ k) * c))
    return out


def scatter_sum(partial, count):
    if not by_neighbours(count):
        return lax.psum_scatter(
            partial.astype(BF16), "seq", scatter_dimension=0, tiled=True
        ).astype(F32)
    rows = partial.shape[0] // count
    half = rows // 2
    me = lax.axis_index("seq")
    low = partial.astype(BF16)

    def block(k, start, size):
        return lax.dynamic_slice(low, ((me ^ k) * rows + start, 0), (size, low.shape[1]))

    tx = swap(block(3, 0, half), 1)
    ty = swap(block(3, half, half), 2)
    ya = swap((block(2, 0, half).astype(F32) + tx.astype(F32)).astype(BF16), 2)
    yb = swap(block(2, half, half), 2)
    xa = swap(block(1, 0, half), 1)
    xb = swap((block(1, half, half).astype(F32) + ty.astype(F32)).astype(BF16), 1)
    top = block(0, 0, half).astype(F32) + ya.astype(F32) + xa.astype(F32)
    low_half = block(0, half, half).astype(F32) + yb.astype(F32) + xb.astype(F32)
    return jnp.concatenate([top, low_half], axis=0)


def scores_of(query, key, segments):
    length = query.shape[0]
    index = jnp.arange(length, dtype=jnp.int32)
    allowed = (segments[:, None] == segments[None, :]) & (index[None, :] <= index[:, None])
    s = dot_nt(query, key) * HEAD_SIZE ** (-0.5)
    return jnp.where(allowed, s, SCORE_FLOOR)


def attend(query, key, value, segments, ratio):
    outs, lses = [], []
    for h in range(query.shape[0]):
        s = scores_of(query[h], key[h // ratio], segments)
        top = jnp.max(s, axis=-1, keepdims=True)
        weights = jnp.exp(s - top)
        total = jnp.sum(weights, axis=-1, keepdims=True)
        probs = (weights / total).astype(BF16)
        outs.append(dot(probs, value[h // ratio]).astype(BF16))
        lses.append(top + jnp.log(total))
    return jnp.stack(outs), jnp.stack(lses)


def attend_back(query, key, value, segments, lse, d_out, ratio):
    dqs, dks, dvs = [], [], []
    for g in range(key.shape[0]):
        dk = dv = 0.0
        for h in range(g * ratio, (g + 1) * ratio):
            s = scores_of(query[h], key[g], segments)
            probs = jnp.exp(s - lse[h])
            dp = dot_nt(d_out[h], value[g])
            delta = jnp.sum(probs * dp, axis=-1, keepdims=True)
            ds = (probs * (dp - delta) * HEAD_SIZE ** (-0.5)).astype(BF16)
            dqs.append(dot(ds, key[g]))
            dk = dk + dot_tn(ds, query[h])
            dv = dv + dot_tn(probs.astype(BF16), d_out[h])
        dks.append(dk)
        dvs.append(dv)
    return jnp.stack(dqs), jnp.stack(dks), jnp.stack(dvs)


def make_body(seq_count):
    def body(
        tokens,
        segment_ids,
        input_gain,
        query_weight,
        key_projection_weight,
        value_projection_weight,
        output_weight,
        query_gain,
        key_gain,
        post_gain,
        gate_weight,
        up_weight,
        down_weight,
        cotangent,
    ):
        me = lax.axis_index("seq")
        q_heads = QUERY_HEADS // seq_count
        kv_heads = KEY_VALUE_HEADS // seq_count
        ratio = QUERY_HEADS // KEY_VALUE_HEADS
        q_cols, kv_cols = q_heads * HEAD_SIZE, kv_heads * HEAD_SIZE
        f_cols = gate_weight.shape[1] // seq_count

        def share(w, cols):
            return lax.dynamic_slice(w, (0, me * cols), (w.shape[0], cols))

        def gather_weight(w):
            return lax.all_gather(w, "fsdp", axis=0, tiled=True)

        def reduce_weight(terms):
            return lax.psum_scatter(terms.astype(BF16), "fsdp", scatter_dimension=0, tiled=True)

        w_qkv = gather_weight(
            jnp.concatenate(
                [
                    share(query_weight, q_cols),
                    share(key_projection_weight, kv_cols),
                    share(value_projection_weight, kv_cols),
                ],
                axis=1,
            )
        )
        w_out = gather_weight(share(output_weight, q_cols))
        w_gate = gather_weight(share(gate_weight, f_cols))
        w_up = gather_weight(share(up_weight, f_cols))
        w_down = gather_weight(share(down_weight, f_cols))

        inputs = tokens[0].astype(F32)
        segments = segment_ids[0]
        length = segments.shape[0]
        xa = gather_rows((inputs * inverse_rms(inputs) * input_gain).astype(BF16), seq_count)
        dy = gather_rows(cotangent[0], seq_count)

        cosine, sine = rotary_tables(positions(segments))
        qkv = dot(xa, w_qkv).astype(BF16)
        q = qkv[:, :q_cols].reshape(length, q_heads, HEAD_SIZE).astype(F32)
        k = qkv[:, q_cols : q_cols + kv_cols].reshape(length, kv_heads, HEAD_SIZE).astype(F32)
        v = qkv[:, q_cols + kv_cols :].reshape(length, kv_heads, HEAD_SIZE).transpose(1, 0, 2)
        qr = rotate(q * inverse_rms(q) * query_gain, cosine, sine).astype(BF16).transpose(1, 0, 2)
        kr = rotate(k * inverse_rms(k) * key_gain, cosine, sine).astype(BF16).transpose(1, 0, 2)
        o_heads, lse = attend(qr, kr, v, segments, ratio)
        o = o_heads.transpose(1, 0, 2).reshape(length, q_cols)

        resid = inputs + scatter_sum(dot_nt(o, w_out), seq_count)
        xb = gather_rows((resid * inverse_rms(resid) * post_gain).astype(BF16), seq_count)

        gate = dot(xb, w_gate)
        upper = dot(xb, w_up)
        d_hidden = dot(dy, w_down)
        sigma = 1.0 / (1.0 + jnp.exp(-gate))
        silu = gate * sigma
        hidden = (silu * upper).astype(BF16)
        d_gate = (d_hidden * upper * sigma * (1.0 + gate * (1.0 - sigma))).astype(BF16)
        d_up = (d_hidden * silu).astype(BF16)

        d_xb = scatter_sum(dot_nt(d_gate, w_gate) + dot_nt(d_up, w_up), seq_count)
        out = resid + scatter_sum(dot_nt(hidden, w_down), seq_count)

        g_gate = reduce_weight(dot_tn(xb, d_gate))
        g_up = reduce_weight(dot_tn(xb, d_up))
        g_down = reduce_weight(dot_tn(dy, hidden))

        du, post_terms = norm_back(resid, post_gain, d_xb)
        d_resid = cotangent[0].astype(F32) + du
        drl = gather_rows(d_resid.astype(BF16), seq_count)
        d_o = dot(drl, w_out).astype(BF16)
        g_out = reduce_weight(dot_tn(drl, o))

        d_o_heads = d_o.reshape(length, q_heads, HEAD_SIZE).transpose(1, 0, 2)
        dqr, dkr, dv = attend_back(qr, kr, v, segments, lse, d_o_heads, ratio)
        dq, q_terms = norm_back(q, query_gain, rotate_back(dqr.transpose(1, 0, 2), cosine, sine))
        dk, k_terms = norm_back(k, key_gain, rotate_back(dkr.transpose(1, 0, 2), cosine, sine))
        d_qkv = jnp.concatenate(
            [
                dq.astype(BF16).reshape(length, q_cols),
                dk.astype(BF16).reshape(length, kv_cols),
                dv.astype(BF16).transpose(1, 0, 2).reshape(length, kv_cols),
            ],
            axis=1,
        )
        g_qkv = reduce_weight(dot_tn(xa, d_qkv))
        d_xa = scatter_sum(dot_nt(d_qkv, w_qkv), seq_count)
        du, in_terms = norm_back(inputs, input_gain, d_xa)
        d_inputs = d_resid + du

        gains = lax.psum(
            (
                jnp.sum(in_terms, axis=0),
                jnp.sum(q_terms, axis=(0, 1)),
                jnp.sum(k_terms, axis=(0, 1)),
                jnp.sum(post_terms, axis=0),
            ),
            ("seq", "fsdp"),
        )
        return (
            out.astype(BF16)[None],
            d_inputs.astype(BF16)[None],
            gains[0],
            gather_columns(g_qkv[:, :q_cols], seq_count),
            gather_columns(g_qkv[:, q_cols : q_cols + kv_cols], seq_count),
            gather_columns(g_qkv[:, q_cols + kv_cols :], seq_count),
            gather_columns(g_out, seq_count),
            gains[1],
            gains[2],
            gains[3],
            gather_columns(g_gate, seq_count),
            gather_columns(g_up, seq_count),
            gather_columns(g_down, seq_count),
        )

    return body


def solution(mesh):
    rows, acts = P("fsdp", None), P("fsdp", "seq", None)
    return jax.shard_map(
        make_body(mesh.shape["seq"]),
        mesh=mesh,
        in_specs=(
            acts, rows, P(), rows, rows, rows, rows, P(), P(), P(), rows, rows, rows, acts,
        ),
        out_specs=(acts, acts, P(), rows, rows, rows, rows, P(), P(), P(), rows, rows, rows),
        check_vma=False,
    )
```

```python
import functools

import jax
import jax.numpy as jnp
from jax import lax
from jax.experimental import pallas as pl
from jax.experimental.pallas import tpu as pltpu
from jax.sharding import PartitionSpec as P

QUERY_HEADS = 16
KEY_VALUE_HEADS = 8
HEAD_SIZE = 128
NORM_EPSILON = 1e-06
ROPE_BASE = 1000000.0
SCORE_FLOOR = -1e30
F32 = jnp.float32
BF16 = jnp.bfloat16
TINY = pl.CostEstimate(flops=1000, bytes_accessed=1000, transcendentals=0)


def dot(a, b):
    return jnp.dot(a, b, preferred_element_type=F32)


def dot_nt(a, b):
    return lax.dot_general(a, b, (((1,), (1,)), ((), ())), preferred_element_type=F32)


def dot_tn(a, b):
    return lax.dot_general(a, b, (((0,), (0,)), ((), ())), preferred_element_type=F32)


def inverse_rms(u):
    return lax.rsqrt(jnp.mean(u * u, axis=-1, keepdims=True) + NORM_EPSILON)


def norm_back(u, gain, e):
    w = inverse_rms(u)
    n = u * w
    t = e * gain
    du = w * (t - n * jnp.mean(n * t, axis=-1, keepdims=True))
    return du, e * n


def positions(segments):
    index = jnp.arange(segments.shape[0], dtype=jnp.int32)
    first = jnp.concatenate([jnp.ones((1,), dtype=jnp.bool_), segments[1:] != segments[:-1]])
    starts = lax.cummax(jnp.where(first, index, jnp.zeros_like(index)), axis=0)
    return index - starts


def rotary_tables(position_index):
    half = HEAD_SIZE // 2
    freq = ROPE_BASE ** (-jnp.arange(half, dtype=F32) * 2.0 / HEAD_SIZE)
    angle = position_index.astype(F32)[:, None] * freq[None, :]
    cosine, sine = jnp.cos(angle), jnp.sin(angle)
    return jnp.concatenate([cosine, cosine], axis=-1), jnp.concatenate([-sine, sine], axis=-1)


def by_neighbours(count):
    return count == 4


def swap(x, side):
    return lax.ppermute(x, "seq", [(s, s ^ side) for s in range(4)])


class Scatter:
    def __init__(self, partial, count):
        self.partial, self.count = partial, count
        self.square = by_neighbours(count)
        self.rows = partial.shape[0] // count
        self.me = lax.axis_index("seq")

    def block(self, k, start, size):
        at = ((self.me ^ k) * self.rows + start, 0)
        return lax.dynamic_slice(self.partial, at, (size, self.partial.shape[1]))

    def first(self):
        if not self.square:
            return [self.partial]
        half = self.rows // 2
        self.tx = swap(self.block(3, 0, half), 1)
        self.ty = swap(self.block(3, half, half), 2)
        return [self.tx, self.ty]

    def second(self, *others):
        if not self.square:
            self.sent = [self.partial]
            self.sum = lax.psum_scatter(self.partial, "seq", scatter_dimension=0, tiled=True)
            return [self.sum]
        zero = jnp.zeros((self.rows // 2, self.partial.shape[1]), F32)
        sx = self.block(1, 0, self.rows).astype(F32) + jnp.concatenate([zero, self.ty.astype(F32)])
        sy = self.block(2, 0, self.rows).astype(F32) + jnp.concatenate([self.tx.astype(F32), zero])
        sx, sy = sx.astype(BF16), sy.astype(BF16)
        if others:
            sx, sy, *_ = lax.optimization_barrier((sx, sy, *others))
        self.sent = [sx, sy]
        self.rx, self.ry = swap(sx, 1), swap(sy, 2)
        return [self.rx, self.ry]

    def finish(self):
        if not self.square:
            return self.sum.astype(F32)
        own = self.block(0, 0, self.rows).astype(F32)
        return own + self.rx.astype(F32) + self.ry.astype(F32)


class Gather:
    def __init__(self, x, count):
        self.x, self.count = x, count
        self.square = by_neighbours(count)
        self.me = lax.axis_index("seq")

    def first(self):
        if not self.square:
            return [self.x]
        self.bx, self.by = swap(self.x, 1), swap(self.x, 2)
        return [self.bx, self.by]

    def second(self, *others):
        if not self.square:
            self.sent = self.x
            return [self.x]
        half = self.x.shape[0] // 2
        ahead, below = self.by[:half], self.bx[half:]
        if others:
            ahead, below, *_ = lax.optimization_barrier((ahead, below, *others))
        self.sent = ahead
        self.ad, self.bd = swap(ahead, 1), swap(below, 2)
        return [self.ad, self.bd]

    def column(self):
        if not self.square:
            return lax.all_gather(self.x, "seq", axis=0, tiled=True)
        rows = self.x.shape[0]
        out = jnp.zeros((self.count * rows,) + self.x.shape[1:], self.x.dtype)
        pieces = (
            (0, 0, self.x),
            (1, 0, self.bx),
            (2, 0, self.by),
            (3, 0, self.ad),
            (3, rows // 2, self.bd),
        )
        for k, start, piece in pieces:
            out = lax.dynamic_update_slice(out, piece, ((self.me ^ k) * rows + start, 0))
        return out

    def slots(self):
        if not self.square:
            every = lax.all_gather(self.x, "seq", axis=0, tiled=False)
            return [every[k] for k in range(self.count)]
        return [self.x, self.bx, self.by, jnp.concatenate([self.ad, self.bd], axis=0)]


def after(x, *others):
    return lax.optimization_barrier((x, *others))[0]


def in_line(count):
    return count == 8


def gather_weight(w):
    return lax.all_gather(w, "fsdp", axis=0, tiled=True)


def terms_kernel(starts, order_ref, *refs):
    count = len(starts)
    x_refs, d_ref = refs[:count], refs[count]
    out_ref = refs[-1]
    j = pl.program_id(0)
    for n, x_ref in enumerate(x_refs):
        last = starts[n + 1] if n + 1 < count else pl.num_programs(0)

        @pl.when((j >= starts[n]) & (j < last))
        def _():
            total = dot_tn(x_ref[...], d_ref[...])
            if len(refs) == count + 3:
                total = total + refs[count + 1][0].astype(F32)
            out_ref[0] = total.astype(BF16)


def weight_terms(xs, d, rows, order, got=None):
    length, blocks = d.shape[0], order.shape[0]
    tiles = sum(n for _, n in xs)
    width = d.shape[1] // tiles
    starts = [sum(n for _, n in xs[:m]) for m in range(len(xs))]

    def x_map(first, n):
        def index(j, i, order_ref):
            here = (j >= first) & (j < first + n)
            return 0, order_ref[jnp.where(here, i, jnp.where(j < first, 0, blocks - 1))]

        return index

    def out_map(j, i, order_ref):
        return i, 0, j

    in_specs = [
        pl.BlockSpec((length, rows), x_map(first, n)) for first, (_, n) in zip(starts, xs)
    ] + [pl.BlockSpec((length, width), lambda j, i, order_ref: (0, j))]
    operands = [x for x, _ in xs] + [d]
    if got is not None:
        in_specs.append(pl.BlockSpec((1, rows, width), out_map))
        operands.append(got)
    return pl.pallas_call(
        functools.partial(terms_kernel, starts),
        grid_spec=pltpu.PrefetchScalarGridSpec(
            num_scalar_prefetch=1,
            grid=(tiles, blocks),
            in_specs=in_specs,
            out_specs=pl.BlockSpec((1, rows, width), out_map),
        ),
        out_shape=jax.ShapeDtypeStruct((blocks, rows, d.shape[1]), BF16),
        compiler_params=pltpu.CompilerParams(vmem_limit_bytes=40 << 20),
        cost_estimate=TINY,
        name="weight_terms",
    )(order, *operands)


def all_terms(xs, d, rows, count):
    terms = weight_terms(xs, d, rows, jnp.arange(count, dtype=jnp.int32))
    return terms.reshape(count * rows, d.shape[1])


def sum_terms(terms):
    return lax.psum_scatter(terms, "fsdp", scatter_dimension=0, tiled=True)


def sum_all(x, axis, count):
    if count & (count - 1):
        return lax.psum(x, axis)
    bit = 1
    while bit < count:
        x = x + lax.ppermute(x, axis, [(i, i ^ bit) for i in range(count)])
        bit *= 2
    return x


ROWS = 256
SCALE = HEAD_SIZE ** (-0.5)


def head_norm_rope(u, gain, cosine, sine):
    w = inverse_rms(u)
    t = u * w * gain
    return (t * cosine + pltpu.roll(t, HEAD_SIZE // 2, 1) * sine).astype(BF16)


def head_norm_rope_back(u, gain, cosine, sine, e):
    e = e * cosine - pltpu.roll(e, HEAD_SIZE // 2, 1) * sine
    return norm_back(u, gain, e)


def heads_of(refs, gains, cosine, sine, ratio):
    q_ref, k_ref = refs
    queries = [
        head_norm_rope(
            q_ref[:, h * HEAD_SIZE : (h + 1) * HEAD_SIZE].astype(F32), gains[0], cosine, sine
        )
        for h in range(ratio)
    ]
    return queries, head_norm_rope(k_ref[...].astype(F32), gains[1], cosine, sine)


def softmax_rows(queries, key, column, row, i, keys):
    stacked = jnp.concatenate([q[i * ROWS : (i + 1) * ROWS] for q in queries], axis=0)
    s = dot_nt(stacked, key[:keys]) * SCALE
    ids = jnp.concatenate([column[i * ROWS : (i + 1) * ROWS]] * len(queries), axis=0)
    place = lax.broadcasted_iota(jnp.int32, s.shape, 0) % ROWS + i * ROWS
    allowed = (ids == row[:, :keys]) & (lax.broadcasted_iota(jnp.int32, s.shape, 1) <= place)
    s = jnp.where(allowed, s, SCORE_FLOOR)
    p = jnp.exp(s - jnp.max(s, axis=-1, keepdims=True))
    return stacked, p * (1.0 / jnp.sum(p, axis=-1, keepdims=True))


def attend_kernel(
    ratio, q_ref, k_ref, v_ref, cos_ref, sin_ref, col_ref, row_ref, qg_ref, kg_ref, o_ref
):
    gains = qg_ref[...], kg_ref[...]
    queries, key = heads_of((q_ref, k_ref), gains, cos_ref[...], sin_ref[...], ratio)
    column, row = col_ref[...], row_ref[...]
    for i in range(q_ref.shape[0] // ROWS):
        keys = (i + 1) * ROWS
        _, p = softmax_rows(queries, key, column, row, i, keys)
        o = dot(p.astype(BF16), v_ref[:keys, :])
        for h in range(ratio):
            o_ref[i * ROWS : keys, h * HEAD_SIZE : (h + 1) * HEAD_SIZE] = o[
                h * ROWS : (h + 1) * ROWS
            ].astype(BF16)


def attend_back_kernel(
    ratio,
    q_ref,
    k_ref,
    v_ref,
    cos_ref,
    sin_ref,
    col_ref,
    row_ref,
    qg_ref,
    kg_ref,
    do_ref,
    dq_ref,
    dk_ref,
    dv_ref,
    qgg_ref,
    kgg_ref,
    dq_all,
    dk_all,
    dv_all,
):
    gains = qg_ref[...], kg_ref[...]
    cosine, sine = cos_ref[...], sin_ref[...]
    queries, key = heads_of((q_ref, k_ref), gains, cosine, sine, ratio)
    column, row = col_ref[...], row_ref[...]
    dk_all[...] = jnp.zeros_like(dk_all)
    dv_all[...] = jnp.zeros_like(dv_all)
    for i in range(q_ref.shape[0] // ROWS):
        keys = (i + 1) * ROWS
        stacked, p = softmax_rows(queries, key, column, row, i, keys)
        do = jnp.concatenate(
            [do_ref[i * ROWS : keys, h * HEAD_SIZE : (h + 1) * HEAD_SIZE] for h in range(ratio)],
            axis=0,
        )
        dp = dot_nt(do, v_ref[:keys, :])
        delta = jnp.sum(p * dp, axis=-1, keepdims=True)
        ds = (p * (dp - delta) * SCALE).astype(BF16)
        dq = dot(ds, key[:keys])
        for h in range(ratio):
            dq_all[h, i * ROWS : keys, :] = dq[h * ROWS : (h + 1) * ROWS]
        dk_all[:keys, :] += dot_tn(ds, stacked)
        dv_all[:keys, :] += dot_tn(p.astype(BF16), do)

    q_terms = jnp.zeros((1, HEAD_SIZE), F32)
    for h in range(ratio):
        columns = slice(h * HEAD_SIZE, (h + 1) * HEAD_SIZE)
        du, terms = head_norm_rope_back(
            q_ref[:, columns].astype(F32), gains[0], cosine, sine, dq_all[h]
        )
        dq_ref[:, columns] = du.astype(BF16)
        q_terms = q_terms + jnp.sum(terms, axis=0, keepdims=True)
    du, terms = head_norm_rope_back(k_ref[...].astype(F32), gains[1], cosine, sine, dk_all[...])
    dk_ref[...] = du.astype(BF16)
    dv_ref[...] = dv_all[...].astype(BF16)
    qgg_ref[0] = q_terms
    kgg_ref[0] = jnp.sum(terms, axis=0, keepdims=True)


def attention_specs(length, q_heads, kv_heads):
    ratio = q_heads // kv_heads
    wide = pl.BlockSpec((length, ratio * HEAD_SIZE), lambda g: (0, g))
    narrow = pl.BlockSpec((length, HEAD_SIZE), lambda g: (0, g))
    table = pl.BlockSpec((length, HEAD_SIZE), lambda g: (0, 0))
    gain = pl.BlockSpec((1, HEAD_SIZE), lambda g: (0, 0))
    inputs = [
        wide,
        pl.BlockSpec((length, HEAD_SIZE), lambda g: (0, q_heads + g)),
        pl.BlockSpec((length, HEAD_SIZE), lambda g: (0, q_heads + kv_heads + g)),
        table,
        table,
        pl.BlockSpec((length, 1), lambda g: (0, 0)),
        pl.BlockSpec((1, length), lambda g: (0, 0)),
        gain,
        gain,
    ]
    return ratio, wide, narrow, inputs


def attention_cost(length, q_heads, products):
    flops = products * q_heads * length * length * HEAD_SIZE
    return pl.CostEstimate(
        flops=flops, bytes_accessed=16 * length * q_heads * HEAD_SIZE, transcendentals=q_heads * length * length
    )


def attend(qkv, tables, ids, gains, q_heads, kv_heads):
    length = qkv.shape[0]
    ratio, wide, _, inputs = attention_specs(length, q_heads, kv_heads)
    return pl.pallas_call(
        functools.partial(attend_kernel, ratio),
        grid=(kv_heads,),
        in_specs=inputs,
        out_specs=wide,
        out_shape=jax.ShapeDtypeStruct((length, q_heads * HEAD_SIZE), BF16),
        compiler_params=pltpu.CompilerParams(vmem_limit_bytes=56 << 20),
        cost_estimate=TINY,
        name="attend",
    )(qkv, qkv, qkv, *tables, *ids, *gains)


def attend_back(qkv, tables, ids, gains, d_o, q_heads, kv_heads):
    length = qkv.shape[0]
    ratio, wide, narrow, inputs = attention_specs(length, q_heads, kv_heads)
    gain_spec = pl.BlockSpec((1, 1, HEAD_SIZE), lambda g: (g, 0, 0))
    gain_shape = jax.ShapeDtypeStruct((kv_heads, 1, HEAD_SIZE), F32)
    kv_shape = jax.ShapeDtypeStruct((length, kv_heads * HEAD_SIZE), BF16)
    return pl.pallas_call(
        functools.partial(attend_back_kernel, ratio),
        grid=(kv_heads,),
        in_specs=inputs + [wide],
        out_specs=(wide, narrow, narrow, gain_spec, gain_spec),
        out_shape=(
            jax.ShapeDtypeStruct((length, q_heads * HEAD_SIZE), BF16),
            kv_shape,
            kv_shape,
            gain_shape,
            gain_shape,
        ),
        scratch_shapes=[
            pltpu.VMEM((ratio, length, HEAD_SIZE), F32),
            pltpu.VMEM((length, HEAD_SIZE), F32),
            pltpu.VMEM((length, HEAD_SIZE), F32),
        ],
        compiler_params=pltpu.CompilerParams(vmem_limit_bytes=56 << 20),
        cost_estimate=TINY,
        name="attend_back",
    )(qkv, qkv, qkv, *tables, *ids, *gains, d_o)


def feed_forward_kernel(carried, piece, xb_ref, dy_ref, w_ref, *refs):
    sums = refs[:2] if carried else (None, None)
    d_ref, dxb_ref, out_ref = refs[-3:]
    xb, dy = xb_ref[...], dy_ref[...]
    gate = dot(xb, w_ref[:, :piece])
    upper = dot(xb, w_ref[:, piece : 2 * piece])
    d_hidden = dot(dy, w_ref[:, 2 * piece :])
    sigma = 1.0 / (1.0 + jnp.exp(-gate))
    silu = gate * sigma
    hidden = (silu * upper).astype(BF16)
    d_gate = (d_hidden * upper * sigma * (1.0 + gate * (1.0 - sigma))).astype(BF16)
    d_up = (d_hidden * silu).astype(BF16)
    d_ref[:, :piece] = d_gate
    d_ref[:, piece : 2 * piece] = d_up
    d_ref[:, 2 * piece :] = hidden
    d_xb = dot_nt(d_gate, w_ref[:, :piece]) + dot_nt(d_up, w_ref[:, piece : 2 * piece])
    out = dot_nt(hidden, w_ref[:, 2 * piece :])
    if carried:
        d_xb = d_xb + sums[0][...]
        out = out + sums[1][...]
    dxb_ref[...] = d_xb.astype(dxb_ref.dtype)
    out_ref[...] = out.astype(out_ref.dtype)


def feed_forward(xb, dy, w, sums, last):
    length, width = xb.shape
    piece = w.shape[1] // 3
    rows = pl.BlockSpec((ROWS, width), lambda i: (i, 0))
    whole = pl.BlockSpec(w.shape, lambda i: (0, 0), pipeline_mode=pl.Buffered(1))
    total = jax.ShapeDtypeStruct((length, width), BF16 if last else F32)
    return pl.pallas_call(
        functools.partial(feed_forward_kernel, bool(sums), piece),
        grid=(length // ROWS,),
        in_specs=[rows, rows, whole] + [rows] * len(sums),
        out_specs=(pl.BlockSpec((ROWS, 3 * piece), lambda i: (i, 0)), rows, rows),
        out_shape=(jax.ShapeDtypeStruct((length, 3 * piece), BF16), total, total),
        compiler_params=pltpu.CompilerParams(vmem_limit_bytes=60 << 20),
        cost_estimate=TINY,
        name="feed_forward",
    )(xb, dy, w, *sums)


def place_kernel(widths, tiles, me_ref, *refs):
    outs = refs[-len(widths) :]
    k, t = pl.program_id(0), pl.program_id(1)
    for n in range(pl.num_programs(0)):
        for m in range(tiles):

            @pl.when((k == n) & (t == m))
            def _():
                start = 0
                for out_ref, width in zip(outs, widths):
                    size = width // tiles
                    at = start + m * size
                    out_ref[...] = refs[n][:, at : at + size].astype(F32)
                    start += width


def place(slots, widths, tiles, first, every, outs, me, count):
    rows = slots[0].shape[0]
    square = by_neighbours(count)

    def out_map(k, t, me_ref):
        member = jnp.bitwise_xor(me_ref[0], k) if square else k
        return 0, member * every + first + t

    any_spec = pl.BlockSpec(memory_space=pl.ANY)
    n = len(slots)
    return pl.pallas_call(
        functools.partial(place_kernel, widths, tiles),
        grid_spec=pltpu.PrefetchScalarGridSpec(
            num_scalar_prefetch=1,
            grid=(count, tiles),
            in_specs=[pl.BlockSpec(s.shape, lambda k, t, me_ref: (0, 0)) for s in slots]
            + [any_spec] * len(outs),
            out_specs=[pl.BlockSpec((rows, w // tiles), out_map) for w in widths],
        ),
        out_shape=[
            jax.ShapeDtypeStruct((rows, w // tiles * every * count), F32) for w in widths
        ],
        input_output_aliases={1 + n + m: m for m in range(len(outs))},
        compiler_params=pltpu.CompilerParams(vmem_limit_bytes=40 << 20),
        name="place",
        cost_estimate=TINY,
    )(jnp.reshape(me, (1,)).astype(jnp.int32), *slots, *outs)


def make_body(counts):
    seq_count, fsdp_count = counts["seq"], counts["fsdp"]

    def body(
        tokens,
        segment_ids,
        input_gain,
        query_weight,
        key_projection_weight,
        value_projection_weight,
        output_weight,
        query_gain,
        key_gain,
        post_gain,
        gate_weight,
        up_weight,
        down_weight,
        cotangent,
    ):
        me = lax.axis_index("seq")
        rows = query_weight.shape[0]
        q_heads = QUERY_HEADS // seq_count
        kv_heads = KEY_VALUE_HEADS // seq_count
        ratio = QUERY_HEADS // KEY_VALUE_HEADS
        q_cols, kv_cols = q_heads * HEAD_SIZE, kv_heads * HEAD_SIZE
        qkv_cols = q_cols + 2 * kv_cols
        f_cols = gate_weight.shape[1] // seq_count
        pieces = (f_cols // 3 * 2, f_cols // 3)
        def share(w, cols, start=0, size=None):
            return lax.dynamic_slice(w, (0, me * cols + start), (rows, size or cols))

        w_attn = gather_weight(
            jnp.concatenate(
                [
                    share(query_weight, q_cols),
                    share(key_projection_weight, kv_cols),
                    share(value_projection_weight, kv_cols),
                    share(output_weight, q_cols),
                ],
                axis=1,
            )
        )
        w_qkv, w_out = w_attn[:, :qkv_cols], w_attn[:, qkv_cols:]
        w_mlp = [
            gather_weight(
                jnp.concatenate(
                    [share(w, f_cols, start, size) for w in (gate_weight, up_weight, down_weight)],
                    axis=1,
                )
            )
            for start, size in zip((0, pieces[0]), pieces)
        ]

        inputs = tokens[0].astype(F32)
        segments = segment_ids[0]
        get_dy = Gather(cotangent[0], seq_count)
        get_xa = Gather((inputs * inverse_rms(inputs) * input_gain).astype(BF16), seq_count)
        got = get_xa.first()
        get_dy.x = after(get_dy.x, *got)
        get_xa.second()
        get_dy.first()
        xa = get_xa.column()

        tables = rotary_tables(positions(segments))
        ids = segments[:, None], segments[None, :]
        head_gains = query_gain[None, :], key_gain[None, :]
        qkv = dot(xa, w_qkv).astype(BF16)
        get_dy.second(qkv)
        dy = get_dy.column()
        o = attend(qkv, tables, ids, head_gains, q_heads, kv_heads)
        sum_r = Scatter(dot_nt(after(o, dy), w_out).astype(BF16), seq_count)
        sum_r.first()
        sum_r.second()
        resid = inputs + sum_r.finish()
        get_xb = Gather((resid * inverse_rms(resid) * post_gain).astype(BF16), seq_count)
        get_xb.first()
        get_xb.second()
        xb = get_xb.column()

        d1, *sums = feed_forward(xb, dy, w_mlp[0], (), False)
        terms1 = all_terms([(xb, 2), (dy, 1)], d1, rows, fsdp_count)
        share1 = sum_terms(terms1)
        d2, d_xb, out = feed_forward(after(xb, terms1), dy, w_mlp[1], tuple(sums), True)
        sum_dxb = Scatter(d_xb, seq_count)
        sum_dxb.first()
        got = sum_dxb.second()
        terms2 = all_terms([(xb, 2), (dy, 1)], after(d2, *sum_dxb.sent), rows, fsdp_count)
        du, post_terms = norm_back(resid, post_gain, after(sum_dxb.finish(), terms2))
        d_resid = cotangent[0].astype(F32) + du
        get_drl = Gather(d_resid.astype(BF16), seq_count)
        get_drl.first()
        get_drl.second()
        drl = get_drl.column()
        sum_out = Scatter(after(out, drl), seq_count)
        sum_out.first()
        d_o = dot(drl, w_out).astype(BF16)
        got = sum_out.second(d_o)
        share2 = sum_terms(after(terms2, share1, *sum_out.sent))
        dq, dk, dv, q_terms, k_terms = attend_back(
            qkv, tables, ids, head_gains, after(d_o, *sum_out.sent), q_heads, kv_heads
        )
        d_attn = jnp.concatenate([dq, dk, dv, o], axis=1)
        out = resid + sum_out.finish()
        d_attn, out = lax.optimization_barrier((d_attn, out))
        sum_dxa = Scatter(dot_nt(d_attn[:, :qkv_cols], w_qkv).astype(BF16), seq_count)
        sum_dxa.first()
        sum_dxa.second()
        terms3 = all_terms([(xa, 2), (drl, 1)], after(d_attn, *sum_dxa.sent), rows, fsdp_count)
        share3 = sum_terms(after(terms3, share2))
        du, in_terms = norm_back(inputs, input_gain, after(sum_dxa.finish(), terms3))
        d_inputs = d_resid + du

        gains = jnp.concatenate(
            [
                jnp.sum(in_terms, axis=0),
                jnp.sum(post_terms, axis=0),
                jnp.sum(q_terms, axis=(0, 1)),
                jnp.sum(k_terms, axis=(0, 1)),
            ]
        )
        width = post_gain.shape[0]
        get1 = Gather(after(share1, in_terms), seq_count)
        get1.first()
        gains = sum_all(gains, "fsdp", fsdp_count)
        get1.second(gains)
        get2 = Gather(after(share2, *get1.slots()), seq_count)
        get2.first()
        mlp = place(get1.slots(), (pieces[0],) * 3, 2, 0, 3, (), me, seq_count)
        gains = sum_all(after(gains, *get1.slots()), "seq", seq_count)
        get2.second(gains, *mlp)
        mlp = place(get2.slots(), (pieces[1],) * 3, 1, 2, 3, mlp, me, seq_count)
        get3 = Gather(after(share3, *get2.slots()), seq_count)
        get3.first()
        get3.second(*mlp)
        widths = (q_cols, kv_cols, kv_cols, q_cols)
        g_q, g_k, g_v, g_out = place(get3.slots(), widths, 1, 0, 1, (), me, seq_count)
        return (
            out.astype(BF16)[None],
            d_inputs.astype(BF16)[None],
            gains[:width],
            g_q,
            g_k,
            g_v,
            g_out,
            gains[2 * width : 2 * width + HEAD_SIZE],
            gains[2 * width + HEAD_SIZE :],
            gains[width : 2 * width],
            *mlp,
        )

    return body


def solution(mesh):
    rows, acts = P("fsdp", None), P("fsdp", "seq", None)
    return jax.shard_map(
        make_body({"seq": mesh.shape["seq"], "fsdp": mesh.shape["fsdp"]}),
        mesh=mesh,
        in_specs=(
            acts, rows, P(), rows, rows, rows, rows, P(), P(), P(), rows, rows, rows, acts,
        ),
        out_specs=(acts, acts, P(), rows, rows, rows, rows, P(), P(), P(), rows, rows, rows),
        check_vma=False,
    )
```

```python
import functools

import jax
import jax.numpy as jnp
from jax import lax
from jax.experimental import pallas as pl
from jax.experimental.pallas import tpu as pltpu
from jax.sharding import PartitionSpec as P

QUERY_HEADS = 16
KEY_VALUE_HEADS = 8
HEAD_SIZE = 128
NORM_EPSILON = 1e-06
ROPE_BASE = 1000000.0
F32 = jnp.float32
BF16 = jnp.bfloat16
TINY = pl.CostEstimate(flops=1000, bytes_accessed=1000, transcendentals=0)


def dot(a, b):
    return jnp.dot(a, b, preferred_element_type=F32)


def dot_nt(a, b):
    return lax.dot_general(a, b, (((1,), (1,)), ((), ())), preferred_element_type=F32)


def dot_tn(a, b):
    return lax.dot_general(a, b, (((0,), (0,)), ((), ())), preferred_element_type=F32)


def inverse_rms(u):
    return lax.rsqrt(jnp.mean(u * u, axis=-1, keepdims=True) + NORM_EPSILON)


def norm_back(u, gain, e):
    w = inverse_rms(u)
    n = u * w
    t = e * gain
    du = w * (t - n * jnp.mean(n * t, axis=-1, keepdims=True))
    return du, e * n


def positions(segments):
    index = jnp.arange(segments.shape[0], dtype=jnp.int32)
    first = jnp.concatenate([jnp.ones((1,), dtype=jnp.bool_), segments[1:] != segments[:-1]])
    starts = lax.cummax(jnp.where(first, index, jnp.zeros_like(index)), axis=0)
    return index - starts


def rotary_tables(position_index):
    half = HEAD_SIZE // 2
    freq = ROPE_BASE ** (-jnp.arange(half, dtype=F32) * 2.0 / HEAD_SIZE)
    angle = position_index.astype(F32)[:, None] * freq[None, :]
    cosine, sine = jnp.cos(angle), jnp.sin(angle)
    return jnp.concatenate([cosine, cosine], axis=-1), jnp.concatenate([-sine, sine], axis=-1)


def by_neighbours(count):
    return count == 4


def swap(x, side):
    return lax.ppermute(x, "seq", [(s, s ^ side) for s in range(4)])


def put_rows_kernel(count, order_ref, *refs):
    for n in range(count):

        @pl.when(pl.program_id(0) == n)
        def _():
            refs[-1][...] = refs[n][...]


def put_rows(pieces, offsets, parts, out):
    me = lax.axis_index("seq")
    blocks = [(me ^ k) * parts + n % parts for n, k in enumerate(offsets)]
    rows, c = pieces[0].shape
    kept = [] if out is None else [out]
    return pl.pallas_call(
        functools.partial(put_rows_kernel, len(pieces)),
        grid_spec=pltpu.PrefetchScalarGridSpec(
            num_scalar_prefetch=1,
            grid=(len(pieces),),
            in_specs=[pl.BlockSpec((rows, c), lambda n, order: (0, 0))] * len(pieces)
            + [pl.BlockSpec(memory_space=pl.ANY)] * len(kept),
            out_specs=pl.BlockSpec((rows, c), lambda n, order: (order[n], 0)),
        ),
        out_shape=jax.ShapeDtypeStruct((4 * parts * rows, c), pieces[0].dtype),
        input_output_aliases={1 + len(pieces): 0} if kept else {},
        compiler_params=pltpu.CompilerParams(vmem_limit_bytes=60 << 20),
        cost_estimate=TINY,
        name="put_rows",
    )(jnp.stack(blocks).astype(jnp.int32), *pieces, *kept)


class Scatter:
    def __init__(self, count):
        self.square = by_neighbours(count)

    def first(self, last):
        if not self.square:
            return [last]
        half = last.shape[0] // 2
        self.tx, self.ty = swap(last[:half], 1), swap(last[half:], 2)
        return [self.tx, self.ty]

    def second(self, slots):
        self.slots = slots
        if not self.square:
            every = slots.reshape(-1, slots.shape[-1])
            self.sum = lax.psum_scatter(every, "seq", scatter_dimension=0, tiled=True)
            self.sent = [every]
            return [self.sum]
        half = self.tx.shape[0]
        top, low = slots[1, :half], slots[1, half:]
        sx = jnp.concatenate([top, add(low, self.ty)])
        top, low = slots[2, :half], slots[2, half:]
        sy = jnp.concatenate([add(top, self.tx), low])
        self.sent = [sx, sy]
        self.rx, self.ry = swap(sx, 1), swap(sy, 2)
        return [self.rx, self.ry]

    def finish(self):
        if not self.square:
            return self.sum.astype(F32)
        return self.slots[0].astype(F32) + self.rx.astype(F32) + self.ry.astype(F32)


def add(a, b):
    return (a.astype(F32) + b.astype(F32)).astype(BF16)


def slot_order(count):
    me = lax.axis_index("seq")
    members = [me ^ k if by_neighbours(count) else jnp.int32(k) for k in range(count)]
    return jnp.stack(members).astype(jnp.int32)


def slot_rows(x, order, count, slots):
    rows = x.shape[0] // count
    return jnp.concatenate(
        [lax.dynamic_slice_in_dim(x, order[k] * rows, rows, 0) for k in slots], axis=0
    )


def scattered_product(x, w, order, count, *others):
    total = Scatter(count)
    rows = x.shape[0] // count
    if not total.square:
        terms = dot_nt(x, w).astype(BF16)
        total.last = terms
        total.second(terms.reshape(count, rows, w.shape[0]))
        return total, [terms]
    total.last = dot_nt(slot_rows(x, order, count, (3,)), w).astype(BF16)
    got = total.first(total.last)
    rest = dot_nt(slot_rows(x, order, count, (0, 1, 2)), w).astype(BF16)
    total.second(after(rest, *others).reshape(3, rows, w.shape[0]))
    return total, got


class Gather:
    def __init__(self, x, count):
        self.x, self.count = x, count
        self.square = by_neighbours(count)
        self.me = lax.axis_index("seq")

    def first(self):
        if not self.square:
            return [self.x]
        self.bx, self.by = swap(self.x, 1), swap(self.x, 2)
        return [self.bx, self.by]

    def second(self, *others):
        if not self.square:
            self.sent = self.x
            return [self.x]
        half = self.x.shape[0] // 2
        ahead, below = self.by[:half], self.bx[half:]
        if others:
            ahead, below, *_ = lax.optimization_barrier((ahead, below, *others))
        self.sent = ahead
        self.ad, self.bd = swap(ahead, 1), swap(below, 2)
        return [self.ad, self.bd]

    def column(self):
        if not self.square:
            return lax.all_gather(self.x, "seq", axis=0, tiled=True)
        near = put_rows((self.x, self.bx, self.by), (0, 1, 2), 1, None)
        return put_rows((self.ad, self.bd), (3, 3), 2, near)

    def slots(self):
        if not self.square:
            every = lax.all_gather(self.x, "seq", axis=0, tiled=False)
            return [every[k] for k in range(self.count)]
        return [self.x, self.bx, self.by, jnp.concatenate([self.ad, self.bd], axis=0)]


def after(x, *others):
    return lax.optimization_barrier((x, *others))[0]


def in_line(count):
    return count == 8


def gather_weight(w):
    return lax.all_gather(w, "fsdp", axis=0, tiled=True)


def terms_kernel(starts, *refs):
    count = len(starts)
    x_refs, d_ref, out_ref = refs[:count], refs[count], refs[-1]
    j = pl.program_id(0)
    rows = 512
    for n, x_ref in enumerate(x_refs):
        last = starts[n + 1] if n + 1 < count else pl.num_programs(0)

        @pl.when((j >= starts[n]) & (j < last))
        def _():
            for at in range(0, out_ref.shape[0], rows):
                here = slice(at, at + rows)
                out_ref[here, :] = dot_tn(x_ref[:, here], d_ref[...]).astype(BF16)


def weight_terms(xs, d):
    length, columns = xs[0][0].shape
    tiles = sum(n for _, n in xs)
    width = d.shape[1] // tiles
    starts = [sum(n for _, n in xs[:m]) for m in range(len(xs))]
    whole = pl.BlockSpec((length, columns), lambda j: (0, 0), pipeline_mode=pl.Buffered(1))
    return pl.pallas_call(
        functools.partial(terms_kernel, starts),
        grid=(tiles,),
        in_specs=[whole] * len(xs) + [pl.BlockSpec((length, width), lambda j: (0, j))],
        out_specs=pl.BlockSpec((columns, width), lambda j: (0, j)),
        out_shape=jax.ShapeDtypeStruct((columns, d.shape[1]), BF16),
        compiler_params=pltpu.CompilerParams(vmem_limit_bytes=58 << 20),
        cost_estimate=TINY,
        name="weight_terms",
    )(*[x for x, _ in xs], d)


def sum_terms(terms):
    return lax.psum_scatter(terms, "fsdp", scatter_dimension=0, tiled=True)


def sum_all(x, axis, count):
    if count & (count - 1):
        return lax.psum(x, axis)
    bit = 1
    while bit < count:
        x = x + lax.ppermute(x, axis, [(i, i ^ bit) for i in range(count)])
        bit *= 2
    return x


ROWS = 256
FORWARD_ROWS = 128
SCALE = HEAD_SIZE ** (-0.5)
LOG2_E = 1.4426950408889634


def head_norm_rope(u, gain, cosine, sine):
    w = inverse_rms(u)
    t = u * w * gain
    return (t * cosine + pltpu.roll(t, HEAD_SIZE // 2, 1) * sine).astype(BF16)


def head_norm_rope_back(u, gain, cosine, sine, e):
    e = e * cosine - pltpu.roll(e, HEAD_SIZE // 2, 1) * sine
    return norm_back(u, gain, e)


def heads_of(refs, gains, cosine, sine, ratio):
    q_ref, k_ref = refs
    queries = [
        head_norm_rope(
            q_ref[:, h * HEAD_SIZE : (h + 1) * HEAD_SIZE].astype(F32), gains[0], cosine, sine
        )
        for h in range(ratio)
    ]
    return queries, head_norm_rope(k_ref[...].astype(F32), gains[1], cosine, sine)


def softmax_rows(queries, key, start, block, i):
    before, keys = i * block, (i + 1) * block
    stacked = jnp.concatenate([q[before:keys] for q in queries], axis=0)
    s = dot_nt(stacked, key[:keys]) * (SCALE * LOG2_E)
    first = jnp.concatenate([start[before:keys]] * len(queries), axis=0)
    here = (s.shape[0], block)
    place = lax.broadcasted_iota(jnp.int32, here, 0) % block
    index = lax.broadcasted_iota(jnp.int32, here, 1)
    allowed = (index <= place) & (index + before >= first)
    e = jnp.where(allowed, jnp.exp2(s[:, before:]), 0.0)
    if before:
        index = lax.broadcasted_iota(jnp.int32, (s.shape[0], before), 1)
        earlier = jnp.where(index >= first, jnp.exp2(s[:, :before]), 0.0)
        e = jnp.concatenate([earlier, e], axis=1)
    return stacked, e * (1.0 / jnp.sum(e, axis=-1, keepdims=True))


def attend_kernel(
    ratio, q_ref, k_ref, v_ref, cos_ref, sin_ref, start_ref, qg_ref, kg_ref, o_ref
):
    gains = qg_ref[...], kg_ref[...]
    queries, key = heads_of((q_ref, k_ref), gains, cos_ref[...], sin_ref[...], ratio)
    start, block = start_ref[...], FORWARD_ROWS
    for i in range(q_ref.shape[0] // block):
        keys = (i + 1) * block
        _, p = softmax_rows(queries, key, start, block, i)
        o = dot(p.astype(BF16), v_ref[:keys, :]).astype(BF16)
        for h in range(ratio):
            o_ref[i * block : keys, h * HEAD_SIZE : (h + 1) * HEAD_SIZE] = o[
                h * block : (h + 1) * block
            ]


def attend_back_kernel(
    ratio,
    q_ref,
    k_ref,
    v_ref,
    cos_ref,
    sin_ref,
    start_ref,
    qg_ref,
    kg_ref,
    do_ref,
    dq_ref,
    dk_ref,
    dv_ref,
    qgg_ref,
    kgg_ref,
    dq_all,
    dk_all,
    dv_all,
):
    gains = qg_ref[...], kg_ref[...]
    cosine, sine = cos_ref[...], sin_ref[...]
    queries, key = heads_of((q_ref, k_ref), gains, cosine, sine, ratio)
    start = start_ref[...]
    dk_all[...] = jnp.zeros_like(dk_all)
    dv_all[...] = jnp.zeros_like(dv_all)
    for i in range(q_ref.shape[0] // ROWS):
        keys = (i + 1) * ROWS
        stacked, p = softmax_rows(queries, key, start, ROWS, i)
        do = jnp.concatenate(
            [do_ref[i * ROWS : keys, h * HEAD_SIZE : (h + 1) * HEAD_SIZE] for h in range(ratio)],
            axis=0,
        )
        dp = dot_nt(do, v_ref[:keys, :])
        delta = jnp.sum(p * dp, axis=-1, keepdims=True)
        ds = (p * (dp - delta) * SCALE).astype(BF16)
        dq = dot(ds, key[:keys])
        for h in range(ratio):
            dq_all[h, i * ROWS : keys, :] = dq[h * ROWS : (h + 1) * ROWS]
        dk_all[:keys, :] += dot_tn(ds, stacked)
        dv_all[:keys, :] += dot_tn(p.astype(BF16), do)

    q_terms = jnp.zeros((1, HEAD_SIZE), F32)
    for h in range(ratio):
        columns = slice(h * HEAD_SIZE, (h + 1) * HEAD_SIZE)
        du, terms = head_norm_rope_back(
            q_ref[:, columns].astype(F32), gains[0], cosine, sine, dq_all[h]
        )
        dq_ref[:, columns] = du.astype(BF16)
        q_terms = q_terms + jnp.sum(terms, axis=0, keepdims=True)
    du, terms = head_norm_rope_back(k_ref[...].astype(F32), gains[1], cosine, sine, dk_all[...])
    dk_ref[...] = du.astype(BF16)
    dv_ref[...] = dv_all[...].astype(BF16)
    qgg_ref[0] = q_terms
    kgg_ref[0] = jnp.sum(terms, axis=0, keepdims=True)


def attention_specs(length, q_heads, kv_heads):
    ratio = q_heads // kv_heads
    wide = pl.BlockSpec((length, ratio * HEAD_SIZE), lambda g: (0, g))
    narrow = pl.BlockSpec((length, HEAD_SIZE), lambda g: (0, g))
    table = pl.BlockSpec((length, HEAD_SIZE), lambda g: (0, 0))
    gain = pl.BlockSpec((1, HEAD_SIZE), lambda g: (0, 0))
    inputs = [
        wide,
        pl.BlockSpec((length, HEAD_SIZE), lambda g: (0, q_heads + g)),
        pl.BlockSpec((length, HEAD_SIZE), lambda g: (0, q_heads + kv_heads + g)),
        table,
        table,
        pl.BlockSpec((length, 1), lambda g: (0, 0)),
        gain,
        gain,
    ]
    return ratio, wide, narrow, inputs


def attention_cost(length, q_heads, products):
    flops = products * q_heads * length * length * HEAD_SIZE
    return pl.CostEstimate(
        flops=flops, bytes_accessed=16 * length * q_heads * HEAD_SIZE, transcendentals=q_heads * length * length
    )


def attend(qkv, tables, start, gains, q_heads, kv_heads):
    length = qkv.shape[0]
    ratio, wide, _, inputs = attention_specs(length, q_heads, kv_heads)
    return pl.pallas_call(
        functools.partial(attend_kernel, ratio),
        grid=(kv_heads,),
        in_specs=inputs,
        out_specs=wide,
        out_shape=jax.ShapeDtypeStruct((length, q_heads * HEAD_SIZE), BF16),
        compiler_params=pltpu.CompilerParams(vmem_limit_bytes=56 << 20),
        cost_estimate=TINY,
        name="attend",
    )(qkv, qkv, qkv, *tables, start, *gains)


def attend_back(qkv, tables, start, gains, d_o, q_heads, kv_heads):
    length = qkv.shape[0]
    ratio, wide, narrow, inputs = attention_specs(length, q_heads, kv_heads)
    gain_spec = pl.BlockSpec((1, 1, HEAD_SIZE), lambda g: (g, 0, 0))
    gain_shape = jax.ShapeDtypeStruct((kv_heads, 1, HEAD_SIZE), F32)
    kv_shape = jax.ShapeDtypeStruct((length, kv_heads * HEAD_SIZE), BF16)
    return pl.pallas_call(
        functools.partial(attend_back_kernel, ratio),
        grid=(kv_heads,),
        in_specs=inputs + [wide],
        out_specs=(wide, narrow, narrow, gain_spec, gain_spec),
        out_shape=(
            jax.ShapeDtypeStruct((length, q_heads * HEAD_SIZE), BF16),
            kv_shape,
            kv_shape,
            gain_shape,
            gain_shape,
        ),
        scratch_shapes=[
            pltpu.VMEM((ratio, length, HEAD_SIZE), F32),
            pltpu.VMEM((length, HEAD_SIZE), F32),
            pltpu.VMEM((length, HEAD_SIZE), F32),
        ],
        compiler_params=pltpu.CompilerParams(vmem_limit_bytes=56 << 20),
        cost_estimate=TINY,
        name="attend_back",
    )(qkv, qkv, qkv, *tables, start, *gains, d_o)


def feed_forward_kernel(carried, piece, order_ref, xb_ref, dy_ref, w_ref, *refs):
    sums = refs[:2] if carried else (None, None)
    d_ref, dxb_ref, out_ref = refs[-3:]
    xb, dy = xb_ref[...], dy_ref[...]
    gate = dot(xb, w_ref[:, :piece])
    upper = dot(xb, w_ref[:, piece : 2 * piece])
    d_hidden = dot(dy, w_ref[:, 2 * piece :])
    sigma = 1.0 / (1.0 + jnp.exp(-gate))
    silu = gate * sigma
    hidden = (silu * upper).astype(BF16)
    d_gate = (d_hidden * upper * sigma * (1.0 + gate * (1.0 - sigma))).astype(BF16)
    d_up = (d_hidden * silu).astype(BF16)
    d_ref[:, :piece] = d_gate
    d_ref[:, piece : 2 * piece] = d_up
    d_ref[:, 2 * piece :] = hidden
    d_xb = dot_nt(d_gate, w_ref[:, :piece]) + dot_nt(d_up, w_ref[:, piece : 2 * piece])
    out = dot_nt(hidden, w_ref[:, 2 * piece :])
    if carried:
        d_xb = d_xb + sums[0][0]
        out = out + sums[1][0]
    dxb_ref[0] = d_xb.astype(dxb_ref.dtype)
    out_ref[0] = out.astype(out_ref.dtype)


def feed_forward(xb, dy, w, order, sums, kind):
    length, width = xb.shape
    piece = w.shape[1] // 3
    count = order.shape[0]
    block = length // count
    rows = pl.BlockSpec((block, width), lambda i, order: (order[i], 0))
    whole = pl.BlockSpec(w.shape, lambda i, order: (0, 0), pipeline_mode=pl.Buffered(1))
    summed = pl.BlockSpec((1, block, width), lambda i, order: (i, 0, 0))
    total = jax.ShapeDtypeStruct((count, block, width), kind)
    return pl.pallas_call(
        functools.partial(feed_forward_kernel, bool(sums), piece),
        grid_spec=pltpu.PrefetchScalarGridSpec(
            num_scalar_prefetch=1,
            grid=(count,),
            in_specs=[rows, rows, whole] + [summed] * len(sums),
            out_specs=(
                pl.BlockSpec((block, 3 * piece), lambda i, order: (order[i], 0)),
                summed,
                summed,
            ),
        ),
        out_shape=(jax.ShapeDtypeStruct((length, 3 * piece), BF16), total, total),
        compiler_params=pltpu.CompilerParams(vmem_limit_bytes=60 << 20),
        cost_estimate=TINY,
        name="feed_forward",
    )(order, xb, dy, w, *sums)


def place_kernel(widths, tiles, me_ref, *refs):
    outs = refs[-len(widths) :]
    k, t = pl.program_id(0), pl.program_id(1)
    for n in range(pl.num_programs(0)):
        for m in range(tiles):

            @pl.when((k == n) & (t == m))
            def _():
                start = 0
                for out_ref, width in zip(outs, widths):
                    size = width // tiles
                    at = start + m * size
                    out_ref[...] = refs[n][:, at : at + size].astype(F32)
                    start += width


def place(slots, widths, tiles, first, every, outs, me, count):
    rows = slots[0].shape[0]
    square = by_neighbours(count)

    def out_map(k, t, me_ref):
        member = jnp.bitwise_xor(me_ref[0], k) if square else k
        return 0, member * every + first + t

    any_spec = pl.BlockSpec(memory_space=pl.ANY)
    n = len(slots)
    return pl.pallas_call(
        functools.partial(place_kernel, widths, tiles),
        grid_spec=pltpu.PrefetchScalarGridSpec(
            num_scalar_prefetch=1,
            grid=(count, tiles),
            in_specs=[pl.BlockSpec(s.shape, lambda k, t, me_ref: (0, 0)) for s in slots]
            + [any_spec] * len(outs),
            out_specs=[pl.BlockSpec((rows, w // tiles), out_map) for w in widths],
        ),
        out_shape=[
            jax.ShapeDtypeStruct((rows, w // tiles * every * count), F32) for w in widths
        ],
        input_output_aliases={1 + n + m: m for m in range(len(outs))},
        compiler_params=pltpu.CompilerParams(vmem_limit_bytes=40 << 20),
        name="place",
        cost_estimate=TINY,
    )(jnp.reshape(me, (1,)).astype(jnp.int32), *slots, *outs)


def make_body(counts):
    seq_count, fsdp_count = counts["seq"], counts["fsdp"]

    def body(
        tokens,
        segment_ids,
        input_gain,
        query_weight,
        key_projection_weight,
        value_projection_weight,
        output_weight,
        query_gain,
        key_gain,
        post_gain,
        gate_weight,
        up_weight,
        down_weight,
        cotangent,
    ):
        me = lax.axis_index("seq")
        rows = query_weight.shape[0]
        q_heads = QUERY_HEADS // seq_count
        kv_heads = KEY_VALUE_HEADS // seq_count
        ratio = QUERY_HEADS // KEY_VALUE_HEADS
        q_cols, kv_cols = q_heads * HEAD_SIZE, kv_heads * HEAD_SIZE
        qkv_cols = q_cols + 2 * kv_cols
        f_cols = gate_weight.shape[1] // seq_count
        pieces = (f_cols // 3 * 2, f_cols // 3)
        def share(w, cols, start=0, size=None):
            return lax.dynamic_slice(w, (0, me * cols + start), (rows, size or cols))

        w_attn = gather_weight(
            jnp.concatenate(
                [
                    share(query_weight, q_cols),
                    share(key_projection_weight, kv_cols),
                    share(value_projection_weight, kv_cols),
                    share(output_weight, q_cols),
                ],
                axis=1,
            )
        )
        w_qkv, w_out = w_attn[:, :qkv_cols], w_attn[:, qkv_cols:]
        w_mlp = [
            gather_weight(
                jnp.concatenate(
                    [share(w, f_cols, start, size) for w in (gate_weight, up_weight, down_weight)],
                    axis=1,
                )
            )
            for start, size in zip((0, pieces[0]), pieces)
        ]

        inputs = tokens[0].astype(F32)
        segments = segment_ids[0]
        order = slot_order(seq_count)
        get_dy = Gather(cotangent[0], seq_count)
        get_dy.first()
        get_xa = Gather((inputs * inverse_rms(inputs) * input_gain).astype(BF16), seq_count)
        get_xa.first()
        get_xa.second()
        xa = get_xa.column()

        place_in_document = positions(segments)
        tables = rotary_tables(place_in_document)
        start = (jnp.arange(segments.shape[0], dtype=jnp.int32) - place_in_document)[:, None]
        head_gains = query_gain[None, :], key_gain[None, :]
        qkv = dot(xa, w_qkv).astype(BF16)
        get_dy.second(qkv)
        dy = get_dy.column()
        o = attend(qkv, tables, start, head_gains, q_heads, kv_heads)
        sum_r, _ = scattered_product(after(o, dy), w_out, order, seq_count)
        resid = inputs + sum_r.finish()
        get_xb = Gather((resid * inverse_rms(resid) * post_gain).astype(BF16), seq_count)
        get_xb.first()
        get_xb.second()
        xb = get_xb.column()

        d1, *sums = feed_forward(xb, dy, w_mlp[0], order, (), F32)
        terms1 = weight_terms([(xb, 2), (dy, 1)], d1)
        share1 = sum_terms(terms1)
        xb2 = after(xb, terms1)
        d2, d_xb, out = feed_forward(xb2, dy, w_mlp[1], order, tuple(sums), BF16)
        sum_dxb = Scatter(seq_count)
        sum_dxb.first(d_xb[-1])
        sum_dxb.second(d_xb)
        terms2 = weight_terms([(xb, 2), (dy, 1)], after(d2, *sum_dxb.sent))
        du, post_terms = norm_back(resid, post_gain, after(sum_dxb.finish(), terms2))
        d_resid = cotangent[0].astype(F32) + du
        get_drl = Gather(d_resid.astype(BF16), seq_count)
        get_drl.first()
        get_drl.second()
        drl = get_drl.column()
        share2 = sum_terms(after(terms2, drl))
        sum_out = Scatter(seq_count)
        got = sum_out.first(after(out, drl)[-1])
        d_o = dot(drl, w_out).astype(BF16)
        sum_out.second(after(out, d_o))
        dq, dk, dv, q_terms, k_terms = attend_back(
            qkv, tables, start, head_gains, after(d_o, *sum_out.sent), q_heads, kv_heads
        )
        out = resid + sum_out.finish()
        dq, out = lax.optimization_barrier((dq, out))
        get1 = Gather(after(share1, dq), seq_count)
        near = get1.first()
        d_attn = jnp.concatenate([dq, dk, dv, o], axis=1)
        sum_dxa, got = scattered_product(d_attn[:, :qkv_cols], w_qkv, order, seq_count, *near)
        terms3 = weight_terms([(xa, 2), (drl, 1)], after(d_attn, sum_dxa.last))
        get1.second(*got)
        share3 = sum_terms(after(terms3, share2, *sum_dxa.sent))
        du, in_terms = norm_back(inputs, input_gain, after(sum_dxa.finish(), *get1.slots()))
        d_inputs = d_resid + du

        gains = jnp.concatenate(
            [
                jnp.sum(in_terms, axis=0),
                jnp.sum(post_terms, axis=0),
                jnp.sum(q_terms, axis=(0, 1)),
                jnp.sum(k_terms, axis=(0, 1)),
            ]
        )
        width = post_gain.shape[0]
        get2 = Gather(after(share2, in_terms), seq_count)
        get2.first()
        gains = sum_all(gains, "fsdp", fsdp_count)
        mlp = place(get1.slots(), (pieces[0],) * 3, 2, 0, 3, (), me, seq_count)
        get2.second(gains, *mlp)
        get3 = Gather(after(share3, *get2.slots()), seq_count)
        get3.first()
        mlp = place(get2.slots(), (pieces[1],) * 3, 1, 2, 3, mlp, me, seq_count)
        gains = sum_all(after(gains, *get2.slots()), "seq", seq_count)
        get3.second(gains, *mlp)
        widths = (q_cols, kv_cols, kv_cols, q_cols)
        g_q, g_k, g_v, g_out = place(get3.slots(), widths, 1, 0, 1, (), me, seq_count)
        return (
            out.astype(BF16)[None],
            d_inputs.astype(BF16)[None],
            gains[:width],
            g_q,
            g_k,
            g_v,
            g_out,
            gains[2 * width : 2 * width + HEAD_SIZE],
            gains[2 * width + HEAD_SIZE :],
            gains[width : 2 * width],
            *mlp,
        )

    return body


def solution(mesh):
    rows, acts = P("fsdp", None), P("fsdp", "seq", None)
    return jax.shard_map(
        make_body({"seq": mesh.shape["seq"], "fsdp": mesh.shape["fsdp"]}),
        mesh=mesh,
        in_specs=(
            acts, rows, P(), rows, rows, rows, rows, P(), P(), P(), rows, rows, rows, acts,
        ),
        out_specs=(acts, acts, P(), rows, rows, rows, rows, P(), P(), P(), rows, rows, rows),
        check_vma=False,
    )
```

```python
import functools

import jax
import jax.numpy as jnp
from jax import lax
from jax.experimental import pallas as pl
from jax.experimental.pallas import tpu as pltpu
from jax.sharding import PartitionSpec as P

QUERY_HEADS = 16
KEY_VALUE_HEADS = 8
HEAD_SIZE = 128
NORM_EPSILON = 1e-06
ROPE_BASE = 1000000.0
F32 = jnp.float32
BF16 = jnp.bfloat16
TINY = pl.CostEstimate(flops=1000, bytes_accessed=1000, transcendentals=0)


def dot(a, b):
    return jnp.dot(a, b, preferred_element_type=F32)


def dot_nt(a, b):
    return lax.dot_general(a, b, (((1,), (1,)), ((), ())), preferred_element_type=F32)


def dot_tn(a, b):
    return lax.dot_general(a, b, (((0,), (0,)), ((), ())), preferred_element_type=F32)


def inverse_rms(u):
    return lax.rsqrt(jnp.mean(u * u, axis=-1, keepdims=True) + NORM_EPSILON)


def norm_back(u, gain, e):
    w = inverse_rms(u)
    n = u * w
    t = e * gain
    du = w * (t - n * jnp.mean(n * t, axis=-1, keepdims=True))
    return du, e * n


def positions(segments):
    index = jnp.arange(segments.shape[0], dtype=jnp.int32)
    first = jnp.concatenate([jnp.ones((1,), dtype=jnp.bool_), segments[1:] != segments[:-1]])
    starts = lax.cummax(jnp.where(first, index, jnp.zeros_like(index)), axis=0)
    return index - starts


def rotary_tables(position_index):
    half = HEAD_SIZE // 2
    freq = ROPE_BASE ** (-jnp.arange(half, dtype=F32) * 2.0 / HEAD_SIZE)
    angle = position_index.astype(F32)[:, None] * freq[None, :]
    cosine, sine = jnp.cos(angle), jnp.sin(angle)
    return jnp.concatenate([cosine, cosine], axis=-1), jnp.concatenate([-sine, sine], axis=-1)


def by_neighbours(count):
    return count == 4


def swap(x, side):
    return lax.ppermute(x, "seq", [(s, s ^ side) for s in range(4)])


def put_rows_kernel(count, order_ref, *refs):
    for n in range(count):

        @pl.when(pl.program_id(0) == n)
        def _():
            refs[-1][...] = refs[n][...]


def put_rows(pieces, offsets, parts, out):
    me = lax.axis_index("seq")
    blocks = [(me ^ k) * parts + n % parts for n, k in enumerate(offsets)]
    rows, c = pieces[0].shape
    kept = [] if out is None else [out]
    return pl.pallas_call(
        functools.partial(put_rows_kernel, len(pieces)),
        grid_spec=pltpu.PrefetchScalarGridSpec(
            num_scalar_prefetch=1,
            grid=(len(pieces),),
            in_specs=[pl.BlockSpec((rows, c), lambda n, order: (0, 0))] * len(pieces)
            + [pl.BlockSpec(memory_space=pl.ANY)] * len(kept),
            out_specs=pl.BlockSpec((rows, c), lambda n, order: (order[n], 0)),
        ),
        out_shape=jax.ShapeDtypeStruct((4 * parts * rows, c), pieces[0].dtype),
        input_output_aliases={1 + len(pieces): 0} if kept else {},
        compiler_params=pltpu.CompilerParams(vmem_limit_bytes=60 << 20),
        cost_estimate=TINY,
        name="put_rows",
    )(jnp.stack(blocks).astype(jnp.int32), *pieces, *kept)


class Scatter:
    def __init__(self, count):
        self.square = by_neighbours(count)

    def first(self, last):
        if not self.square:
            return [last]
        half = last.shape[0] // 2
        self.tx, self.ty = swap(last[:half], 1), swap(last[half:], 2)
        return [self.tx, self.ty]

    def second(self, slots):
        self.slots = slots
        if not self.square:
            every = slots.reshape(-1, slots.shape[-1])
            self.sum = lax.psum_scatter(every, "seq", scatter_dimension=0, tiled=True)
            self.sent = [every]
            return [self.sum]
        half = self.tx.shape[0]
        top, low = slots[1, :half], slots[1, half:]
        sx = jnp.concatenate([top, add(low, self.ty)])
        top, low = slots[2, :half], slots[2, half:]
        sy = jnp.concatenate([add(top, self.tx), low])
        self.sent = [sx, sy]
        self.rx, self.ry = swap(sx, 1), swap(sy, 2)
        return [self.rx, self.ry]

    def arrived(self):
        return [self.rx, self.ry] if self.square else [self.sum]

    def finish(self):
        if not self.square:
            return self.sum.astype(F32)
        return self.slots[0].astype(F32) + self.rx.astype(F32) + self.ry.astype(F32)


def add(a, b):
    return (a.astype(F32) + b.astype(F32)).astype(BF16)


def slot_order(count):
    me = lax.axis_index("seq")
    members = [me ^ k if by_neighbours(count) else jnp.int32(k) for k in range(count)]
    return jnp.stack(members).astype(jnp.int32)


def slot_rows(x, order, count, slots):
    rows = x.shape[0] // count
    return jnp.concatenate(
        [lax.dynamic_slice_in_dim(x, order[k] * rows, rows, 0) for k in slots], axis=0
    )


def scattered_product(x, w, order, count, *others, early=True):
    total = Scatter(count)
    rows = x.shape[0] // count
    if not total.square:
        total.last = terms = dot_nt(x, w).astype(BF16)
        total.second(terms.reshape(count, rows, w.shape[0]))
        return total, [terms]
    if early:
        last = dot_nt(slot_rows(x, order, count, (3,)), w).astype(BF16)
        rest = dot_nt(slot_rows(x, order, count, (0, 1, 2)), w).astype(BF16)
        rest = rest.reshape(3, rows, w.shape[0])
    else:
        rest = dot_nt(slot_rows(x, order, count, range(4)), w).astype(BF16)
        rest = rest.reshape(4, rows, w.shape[0])
        last = rest[3]
    total.last = after(last, *others)
    got = total.first(total.last)
    total.second(rest)
    return total, got


class Gather:
    def __init__(self, x, count):
        self.x, self.count = x, count
        self.square = by_neighbours(count)
        self.me = lax.axis_index("seq")

    def first(self):
        if not self.square:
            return [self.x]
        self.bx, self.by = swap(self.x, 1), swap(self.x, 2)
        return [self.bx, self.by]

    def second(self, *others):
        if not self.square:
            self.sent = [self.x]
            return [self.x]
        half = self.x.shape[0] // 2
        ahead, below = self.by[:half], self.bx[half:]
        if others:
            ahead, below, *_ = lax.optimization_barrier((ahead, below, *others))
        self.sent = [ahead, below]
        self.ad, self.bd = swap(ahead, 1), swap(below, 2)
        return [self.ad, self.bd]

    def column(self):
        if not self.square:
            return lax.all_gather(self.x, "seq", axis=0, tiled=True)
        near = put_rows((self.x, self.bx, self.by), (0, 1, 2), 1, None)
        return put_rows((self.ad, self.bd), (3, 3), 2, near)

    def slots(self):
        if not self.square:
            every = lax.all_gather(self.x, "seq", axis=0, tiled=False)
            return [every[k] for k in range(self.count)]
        return [self.x, self.bx, self.by, jnp.concatenate([self.ad, self.bd], axis=0)]


def after(x, *others):
    return lax.optimization_barrier((x, *others))[0]


def in_line(count):
    return count == 8


def gather_weight(w):
    return lax.all_gather(w, "fsdp", axis=0, tiled=True)


def terms_kernel(starts, *refs):
    count = len(starts)
    x_refs, d_ref, out_ref = refs[:count], refs[count], refs[-1]
    j = pl.program_id(0)
    rows = 512
    for n, x_ref in enumerate(x_refs):
        last = starts[n + 1] if n + 1 < count else pl.num_programs(0)

        @pl.when((j >= starts[n]) & (j < last))
        def _():
            for at in range(0, out_ref.shape[0], rows):
                here = slice(at, at + rows)
                out_ref[here, :] = dot_tn(x_ref[:, here], d_ref[...]).astype(BF16)


def weight_terms(xs, d):
    length, columns = xs[0][0].shape
    tiles = sum(n for _, n in xs)
    width = d.shape[1] // tiles
    starts = [sum(n for _, n in xs[:m]) for m in range(len(xs))]
    whole = pl.BlockSpec((length, columns), lambda j: (0, 0), pipeline_mode=pl.Buffered(1))
    return pl.pallas_call(
        functools.partial(terms_kernel, starts),
        grid=(tiles,),
        in_specs=[whole] * len(xs) + [pl.BlockSpec((length, width), lambda j: (0, j))],
        out_specs=pl.BlockSpec((columns, width), lambda j: (0, j)),
        out_shape=jax.ShapeDtypeStruct((columns, d.shape[1]), BF16),
        compiler_params=pltpu.CompilerParams(vmem_limit_bytes=58 << 20),
        cost_estimate=TINY,
        name="weight_terms",
    )(*[x for x, _ in xs], d)


def sum_terms(terms):
    return lax.psum_scatter(terms, "fsdp", scatter_dimension=0, tiled=True)


def sum_all(x, axis, count):
    if count & (count - 1):
        return lax.psum(x, axis)
    bit = 1
    while bit < count:
        x = x + lax.ppermute(x, axis, [(i, i ^ bit) for i in range(count)])
        bit *= 2
    return x


ROWS = 256
FORWARD_ROWS = 128
SCALE = HEAD_SIZE ** (-0.5)
LOG2_E = 1.4426950408889634


def head_norm_rope(u, gain, cosine, sine):
    w = inverse_rms(u)
    t = u * w * gain
    return (t * cosine + pltpu.roll(t, HEAD_SIZE // 2, 1) * sine).astype(BF16)


def head_norm_rope_back(u, gain, cosine, sine, e):
    e = e * cosine - pltpu.roll(e, HEAD_SIZE // 2, 1) * sine
    return norm_back(u, gain, e)


def heads_of(refs, gains, cosine, sine, ratio):
    q_ref, k_ref = refs
    queries = [
        head_norm_rope(
            q_ref[:, h * HEAD_SIZE : (h + 1) * HEAD_SIZE].astype(F32), gains[0], cosine, sine
        )
        for h in range(ratio)
    ]
    return queries, head_norm_rope(k_ref[...].astype(F32), gains[1], cosine, sine)


def softmax_rows(queries, key, start, block, i):
    before, keys = i * block, (i + 1) * block
    stacked = jnp.concatenate([q[before:keys] for q in queries], axis=0)
    s = dot_nt(stacked, key[:keys]) * (SCALE * LOG2_E)
    first = jnp.concatenate([start[before:keys]] * len(queries), axis=0)
    here = (s.shape[0], block)
    place = lax.broadcasted_iota(jnp.int32, here, 0) % block
    index = lax.broadcasted_iota(jnp.int32, here, 1)
    allowed = (index <= place) & (index + before >= first)
    e = jnp.where(allowed, jnp.exp2(s[:, before:]), 0.0)
    if before:
        index = lax.broadcasted_iota(jnp.int32, (s.shape[0], before), 1)
        earlier = jnp.where(index >= first, jnp.exp2(s[:, :before]), 0.0)
        e = jnp.concatenate([earlier, e], axis=1)
    return stacked, e * (1.0 / jnp.sum(e, axis=-1, keepdims=True))


def attend_kernel(
    ratio, q_ref, k_ref, v_ref, cos_ref, sin_ref, start_ref, qg_ref, kg_ref, o_ref
):
    gains = qg_ref[...], kg_ref[...]
    queries, key = heads_of((q_ref, k_ref), gains, cos_ref[...], sin_ref[...], ratio)
    start, block = start_ref[...], FORWARD_ROWS
    for i in range(q_ref.shape[0] // block):
        keys = (i + 1) * block
        _, p = softmax_rows(queries, key, start, block, i)
        o = dot(p.astype(BF16), v_ref[:keys, :]).astype(BF16)
        for h in range(ratio):
            o_ref[i * block : keys, h * HEAD_SIZE : (h + 1) * HEAD_SIZE] = o[
                h * block : (h + 1) * block
            ]


def attend_back_kernel(
    ratio,
    q_ref,
    k_ref,
    v_ref,
    cos_ref,
    sin_ref,
    start_ref,
    qg_ref,
    kg_ref,
    do_ref,
    dq_ref,
    dk_ref,
    dv_ref,
    qgg_ref,
    kgg_ref,
    dq_all,
    dk_all,
    dv_all,
):
    gains = qg_ref[...], kg_ref[...]
    cosine, sine = cos_ref[...], sin_ref[...]
    queries, key = heads_of((q_ref, k_ref), gains, cosine, sine, ratio)
    start = start_ref[...]
    dk_all[...] = jnp.zeros_like(dk_all)
    dv_all[...] = jnp.zeros_like(dv_all)
    for i in range(q_ref.shape[0] // ROWS):
        keys = (i + 1) * ROWS
        stacked, p = softmax_rows(queries, key, start, ROWS, i)
        do = jnp.concatenate(
            [do_ref[i * ROWS : keys, h * HEAD_SIZE : (h + 1) * HEAD_SIZE] for h in range(ratio)],
            axis=0,
        )
        dp = dot_nt(do, v_ref[:keys, :])
        delta = jnp.sum(p * dp, axis=-1, keepdims=True)
        ds = (p * (dp - delta) * SCALE).astype(BF16)
        dq = dot(ds, key[:keys])
        for h in range(ratio):
            dq_all[h, i * ROWS : keys, :] = dq[h * ROWS : (h + 1) * ROWS]
        dk_all[:keys, :] += dot_tn(ds, stacked)
        dv_all[:keys, :] += dot_tn(p.astype(BF16), do)

    q_terms = jnp.zeros((1, HEAD_SIZE), F32)
    for h in range(ratio):
        columns = slice(h * HEAD_SIZE, (h + 1) * HEAD_SIZE)
        du, terms = head_norm_rope_back(
            q_ref[:, columns].astype(F32), gains[0], cosine, sine, dq_all[h]
        )
        dq_ref[:, columns] = du.astype(BF16)
        q_terms = q_terms + jnp.sum(terms, axis=0, keepdims=True)
    du, terms = head_norm_rope_back(k_ref[...].astype(F32), gains[1], cosine, sine, dk_all[...])
    dk_ref[...] = du.astype(BF16)
    dv_ref[...] = dv_all[...].astype(BF16)
    qgg_ref[0] = q_terms
    kgg_ref[0] = jnp.sum(terms, axis=0, keepdims=True)


def attention_specs(length, q_heads, kv_heads):
    ratio = q_heads // kv_heads
    wide = pl.BlockSpec((length, ratio * HEAD_SIZE), lambda g: (0, g))
    narrow = pl.BlockSpec((length, HEAD_SIZE), lambda g: (0, g))
    table = pl.BlockSpec((length, HEAD_SIZE), lambda g: (0, 0))
    gain = pl.BlockSpec((1, HEAD_SIZE), lambda g: (0, 0))
    inputs = [
        wide,
        pl.BlockSpec((length, HEAD_SIZE), lambda g: (0, q_heads + g)),
        pl.BlockSpec((length, HEAD_SIZE), lambda g: (0, q_heads + kv_heads + g)),
        table,
        table,
        pl.BlockSpec((length, 1), lambda g: (0, 0)),
        gain,
        gain,
    ]
    return ratio, wide, narrow, inputs


def attention_cost(length, q_heads, products):
    flops = products * q_heads * length * length * HEAD_SIZE
    return pl.CostEstimate(
        flops=flops, bytes_accessed=16 * length * q_heads * HEAD_SIZE, transcendentals=q_heads * length * length
    )


def attend(qkv, tables, start, gains, q_heads, kv_heads):
    length = qkv.shape[0]
    ratio, wide, _, inputs = attention_specs(length, q_heads, kv_heads)
    return pl.pallas_call(
        functools.partial(attend_kernel, ratio),
        grid=(kv_heads,),
        in_specs=inputs,
        out_specs=wide,
        out_shape=jax.ShapeDtypeStruct((length, q_heads * HEAD_SIZE), BF16),
        compiler_params=pltpu.CompilerParams(vmem_limit_bytes=56 << 20),
        cost_estimate=TINY,
        name="attend",
    )(qkv, qkv, qkv, *tables, start, *gains)


def attend_back(qkv, tables, start, gains, d_o, q_heads, kv_heads):
    length = qkv.shape[0]
    ratio, wide, narrow, inputs = attention_specs(length, q_heads, kv_heads)
    gain_spec = pl.BlockSpec((1, 1, HEAD_SIZE), lambda g: (g, 0, 0))
    gain_shape = jax.ShapeDtypeStruct((kv_heads, 1, HEAD_SIZE), F32)
    kv_shape = jax.ShapeDtypeStruct((length, kv_heads * HEAD_SIZE), BF16)
    return pl.pallas_call(
        functools.partial(attend_back_kernel, ratio),
        grid=(kv_heads,),
        in_specs=inputs + [wide],
        out_specs=(wide, narrow, narrow, gain_spec, gain_spec),
        out_shape=(
            jax.ShapeDtypeStruct((length, q_heads * HEAD_SIZE), BF16),
            kv_shape,
            kv_shape,
            gain_shape,
            gain_shape,
        ),
        scratch_shapes=[
            pltpu.VMEM((ratio, length, HEAD_SIZE), F32),
            pltpu.VMEM((length, HEAD_SIZE), F32),
            pltpu.VMEM((length, HEAD_SIZE), F32),
        ],
        compiler_params=pltpu.CompilerParams(vmem_limit_bytes=56 << 20),
        cost_estimate=TINY,
        name="attend_back",
    )(qkv, qkv, qkv, *tables, start, *gains, d_o)


def feed_forward_kernel(carried, piece, order_ref, xb_ref, dy_ref, w_ref, *refs):
    sums = refs[:2] if carried else (None, None)
    d_ref, dxb_ref, out_ref = refs[-3:]
    xb, dy = xb_ref[...], dy_ref[...]
    gate = dot(xb, w_ref[:, :piece])
    upper = dot(xb, w_ref[:, piece : 2 * piece])
    d_hidden = dot(dy, w_ref[:, 2 * piece :])
    sigma = 1.0 / (1.0 + jnp.exp(-gate))
    silu = gate * sigma
    hidden = (silu * upper).astype(BF16)
    d_gate = (d_hidden * upper * sigma * (1.0 + gate * (1.0 - sigma))).astype(BF16)
    d_up = (d_hidden * silu).astype(BF16)
    d_ref[:, :piece] = d_gate
    d_ref[:, piece : 2 * piece] = d_up
    d_ref[:, 2 * piece :] = hidden
    d_xb = dot_nt(d_gate, w_ref[:, :piece]) + dot_nt(d_up, w_ref[:, piece : 2 * piece])
    out = dot_nt(hidden, w_ref[:, 2 * piece :])
    if carried:
        d_xb = d_xb + sums[0][0]
        out = out + sums[1][0]
    dxb_ref[0] = d_xb.astype(dxb_ref.dtype)
    out_ref[0] = out.astype(out_ref.dtype)


def feed_forward(xb, dy, w, order, sums, kind):
    length, width = xb.shape
    piece = w.shape[1] // 3
    count = order.shape[0]
    block = length // count
    rows = pl.BlockSpec((block, width), lambda i, order: (order[i], 0))
    whole = pl.BlockSpec(w.shape, lambda i, order: (0, 0), pipeline_mode=pl.Buffered(1))
    summed = pl.BlockSpec((1, block, width), lambda i, order: (i, 0, 0))
    total = jax.ShapeDtypeStruct((count, block, width), kind)
    return pl.pallas_call(
        functools.partial(feed_forward_kernel, bool(sums), piece),
        grid_spec=pltpu.PrefetchScalarGridSpec(
            num_scalar_prefetch=1,
            grid=(count,),
            in_specs=[rows, rows, whole] + [summed] * len(sums),
            out_specs=(
                pl.BlockSpec((block, 3 * piece), lambda i, order: (order[i], 0)),
                summed,
                summed,
            ),
        ),
        out_shape=(jax.ShapeDtypeStruct((length, 3 * piece), BF16), total, total),
        compiler_params=pltpu.CompilerParams(vmem_limit_bytes=60 << 20),
        cost_estimate=TINY,
        name="feed_forward",
    )(order, xb, dy, w, *sums)


def place_kernel(widths, tiles, me_ref, *refs):
    outs = refs[-len(widths) :]
    k, t = pl.program_id(0), pl.program_id(1)
    for n in range(pl.num_programs(0)):
        for m in range(tiles):

            @pl.when((k == n) & (t == m))
            def _():
                start = 0
                for out_ref, width in zip(outs, widths):
                    size = width // tiles
                    at = start + m * size
                    out_ref[...] = refs[n][:, at : at + size].astype(F32)
                    start += width


def place(slots, widths, tiles, first, every, outs, me, count):
    rows = slots[0].shape[0]
    square = by_neighbours(count)

    def out_map(k, t, me_ref):
        member = jnp.bitwise_xor(me_ref[0], k) if square else k
        return 0, member * every + first + t

    any_spec = pl.BlockSpec(memory_space=pl.ANY)
    n = len(slots)
    return pl.pallas_call(
        functools.partial(place_kernel, widths, tiles),
        grid_spec=pltpu.PrefetchScalarGridSpec(
            num_scalar_prefetch=1,
            grid=(count, tiles),
            in_specs=[pl.BlockSpec(s.shape, lambda k, t, me_ref: (0, 0)) for s in slots]
            + [any_spec] * len(outs),
            out_specs=[pl.BlockSpec((rows, w // tiles), out_map) for w in widths],
        ),
        out_shape=[
            jax.ShapeDtypeStruct((rows, w // tiles * every * count), F32) for w in widths
        ],
        input_output_aliases={1 + n + m: m for m in range(len(outs))},
        compiler_params=pltpu.CompilerParams(vmem_limit_bytes=40 << 20),
        name="place",
        cost_estimate=TINY,
    )(jnp.reshape(me, (1,)).astype(jnp.int32), *slots, *outs)


def make_body(counts):
    seq_count, fsdp_count = counts["seq"], counts["fsdp"]

    def body(
        tokens,
        segment_ids,
        input_gain,
        query_weight,
        key_projection_weight,
        value_projection_weight,
        output_weight,
        query_gain,
        key_gain,
        post_gain,
        gate_weight,
        up_weight,
        down_weight,
        cotangent,
    ):
        me = lax.axis_index("seq")
        rows = query_weight.shape[0]
        q_heads = QUERY_HEADS // seq_count
        kv_heads = KEY_VALUE_HEADS // seq_count
        ratio = QUERY_HEADS // KEY_VALUE_HEADS
        q_cols, kv_cols = q_heads * HEAD_SIZE, kv_heads * HEAD_SIZE
        qkv_cols = q_cols + 2 * kv_cols
        f_cols = gate_weight.shape[1] // seq_count
        pieces = (f_cols // 3 * 2, f_cols // 3)
        def share(w, cols, start=0, size=None):
            return lax.dynamic_slice(w, (0, me * cols + start), (rows, size or cols))

        w_attn = gather_weight(
            jnp.concatenate(
                [
                    share(query_weight, q_cols),
                    share(key_projection_weight, kv_cols),
                    share(value_projection_weight, kv_cols),
                    share(output_weight, q_cols),
                ],
                axis=1,
            )
        )
        w_qkv, w_out = w_attn[:, :qkv_cols], w_attn[:, qkv_cols:]
        w_mlp = [
            gather_weight(
                jnp.concatenate(
                    [share(w, f_cols, start, size) for w in (gate_weight, up_weight, down_weight)],
                    axis=1,
                )
            )
            for start, size in zip((0, pieces[0]), pieces)
        ]

        inputs = tokens[0].astype(F32)
        segments = segment_ids[0]
        order = slot_order(seq_count)
        get_dy = Gather(cotangent[0], seq_count)
        get_dy.first()
        get_xa = Gather((inputs * inverse_rms(inputs) * input_gain).astype(BF16), seq_count)
        get_xa.first()
        get_xa.second()
        xa = get_xa.column()

        place_in_document = positions(segments)
        tables = rotary_tables(place_in_document)
        start = (jnp.arange(segments.shape[0], dtype=jnp.int32) - place_in_document)[:, None]
        head_gains = query_gain[None, :], key_gain[None, :]
        qkv = dot(xa, w_qkv).astype(BF16)
        get_dy.second(qkv)
        dy = get_dy.column()
        o = attend(qkv, tables, start, head_gains, q_heads, kv_heads)
        sum_r, _ = scattered_product(after(o, dy), w_out, order, seq_count)
        resid = inputs + sum_r.finish()
        get_xb = Gather((resid * inverse_rms(resid) * post_gain).astype(BF16), seq_count)
        get_xb.first()
        get_xb.second()
        xb = get_xb.column()

        d1, *sums = feed_forward(xb, dy, w_mlp[0], order, (), F32)
        terms1 = weight_terms([(xb, 2), (dy, 1)], d1)
        share1 = sum_terms(terms1)
        xb2 = after(xb, terms1)
        d2, d_xb, out = feed_forward(xb2, dy, w_mlp[1], order, tuple(sums), BF16)
        sum_dxb, sum_out = Scatter(seq_count), Scatter(seq_count)
        got = sum_dxb.first(d_xb[-1]) + sum_out.first(out[-1])
        sum_dxb.second(after(d_xb, *got))
        terms2 = weight_terms([(xb, 2), (dy, 1)], after(d2, *sum_dxb.sent))
        du, post_terms = norm_back(resid, post_gain, after(sum_dxb.finish(), terms2))
        d_resid = cotangent[0].astype(F32) + du
        get_drl = Gather(d_resid.astype(BF16), seq_count)
        get_drl.first()
        get_drl.second()
        share2 = sum_terms(after(terms2, *get_drl.sent))
        drl = get_drl.column()
        halves = sum_out.second(after(out, drl))
        d_o = dot(drl, w_out).astype(BF16)
        dq, dk, dv, q_terms, k_terms = attend_back(
            qkv, tables, start, head_gains, after(d_o, *sum_out.sent), q_heads, kv_heads
        )
        dq = after(dq, *halves)
        get1 = Gather(after(share1, dq), seq_count)
        near = get1.first()
        d_attn = jnp.concatenate([dq, dk, dv, o], axis=1)
        terms3 = weight_terms([(xa, 2), (drl, 1)], d_attn)
        d_qkv = after(d_attn, terms3)[:, :qkv_cols]
        sum_dxa, got = scattered_product(
            d_qkv, w_qkv, order, seq_count, *near, early=False
        )
        get1.second(*got)
        out = resid + after(sum_out.finish(), *got)
        share3 = sum_terms(after(terms3, share2, *got))
        du, in_terms = norm_back(inputs, input_gain, after(sum_dxa.finish(), *get1.slots()))
        d_inputs = d_resid + du

        gains = jnp.concatenate(
            [
                jnp.sum(in_terms, axis=0),
                jnp.sum(post_terms, axis=0),
                jnp.sum(q_terms, axis=(0, 1)),
                jnp.sum(k_terms, axis=(0, 1)),
            ]
        )
        width = post_gain.shape[0]
        get2 = Gather(after(share2, *get1.slots(), *sum_dxa.arrived()), seq_count)
        get2.first()
        gains = sum_all(gains, "fsdp", fsdp_count)
        mlp = place(get1.slots(), (pieces[0],) * 3, 2, 0, 3, (), me, seq_count)
        get2.second(gains, *mlp)
        get3 = Gather(after(share3, *get2.slots()), seq_count)
        get3.first()
        mlp = place(get2.slots(), (pieces[1],) * 3, 1, 2, 3, mlp, me, seq_count)
        gains = sum_all(after(gains, *get2.slots()), "seq", seq_count)
        get3.second(gains, *mlp)
        widths = (q_cols, kv_cols, kv_cols, q_cols)
        g_q, g_k, g_v, g_out = place(get3.slots(), widths, 1, 0, 1, (), me, seq_count)
        return (
            out.astype(BF16)[None],
            d_inputs.astype(BF16)[None],
            gains[:width],
            g_q,
            g_k,
            g_v,
            g_out,
            gains[2 * width : 2 * width + HEAD_SIZE],
            gains[2 * width + HEAD_SIZE :],
            gains[width : 2 * width],
            *mlp,
        )

    return body


def solution(mesh):
    rows, acts = P("fsdp", None), P("fsdp", "seq", None)
    return jax.shard_map(
        make_body({"seq": mesh.shape["seq"], "fsdp": mesh.shape["fsdp"]}),
        mesh=mesh,
        in_specs=(
            acts, rows, P(), rows, rows, rows, rows, P(), P(), P(), rows, rows, rows, acts,
        ),
        out_specs=(acts, acts, P(), rows, rows, rows, rows, P(), P(), P(), rows, rows, rows),
        check_vma=False,
    )
```

```python
import functools

import jax
import jax.numpy as jnp
from jax import lax
from jax.experimental import pallas as pl
from jax.experimental.pallas import tpu as pltpu
from jax.sharding import PartitionSpec as P

QUERY_HEADS = 16
KEY_VALUE_HEADS = 8
HEAD_SIZE = 128
NORM_EPSILON = 1e-06
ROPE_BASE = 1000000.0
F32 = jnp.float32
BF16 = jnp.bfloat16
TINY = pl.CostEstimate(flops=1000, bytes_accessed=1000, transcendentals=0)


def dot(a, b):
    return jnp.dot(a, b, preferred_element_type=F32)


def dot_nt(a, b):
    return lax.dot_general(a, b, (((1,), (1,)), ((), ())), preferred_element_type=F32)


def dot_tn(a, b):
    return lax.dot_general(a, b, (((0,), (0,)), ((), ())), preferred_element_type=F32)


def inverse_rms(u):
    return lax.rsqrt(jnp.mean(u * u, axis=-1, keepdims=True) + NORM_EPSILON)


def norm_back(u, gain, e):
    w = inverse_rms(u)
    n = u * w
    t = e * gain
    du = w * (t - n * jnp.mean(n * t, axis=-1, keepdims=True))
    return du, e * n


def positions(segments):
    index = jnp.arange(segments.shape[0], dtype=jnp.int32)
    first = jnp.concatenate([jnp.ones((1,), dtype=jnp.bool_), segments[1:] != segments[:-1]])
    starts = lax.cummax(jnp.where(first, index, jnp.zeros_like(index)), axis=0)
    return index - starts


def rotary_tables(position_index):
    half = HEAD_SIZE // 2
    freq = ROPE_BASE ** (-jnp.arange(half, dtype=F32) * 2.0 / HEAD_SIZE)
    angle = position_index.astype(F32)[:, None] * freq[None, :]
    cosine, sine = jnp.cos(angle), jnp.sin(angle)
    return jnp.concatenate([cosine, cosine], axis=-1), jnp.concatenate([-sine, sine], axis=-1)


def by_neighbours(count):
    return count == 4


def swap(x, side):
    return lax.ppermute(x, "seq", [(s, s ^ side) for s in range(4)])


def put_rows_kernel(count, order_ref, *refs):
    for n in range(count):

        @pl.when(pl.program_id(0) == n)
        def _():
            refs[-1][...] = refs[n][...]


def put_rows(pieces, offsets, parts, out):
    me = lax.axis_index("seq")
    blocks = [(me ^ k) * parts + n % parts for n, k in enumerate(offsets)]
    rows, c = pieces[0].shape
    kept = [] if out is None else [out]
    return pl.pallas_call(
        functools.partial(put_rows_kernel, len(pieces)),
        grid_spec=pltpu.PrefetchScalarGridSpec(
            num_scalar_prefetch=1,
            grid=(len(pieces),),
            in_specs=[pl.BlockSpec((rows, c), lambda n, order: (0, 0))] * len(pieces)
            + [pl.BlockSpec(memory_space=pl.ANY)] * len(kept),
            out_specs=pl.BlockSpec((rows, c), lambda n, order: (order[n], 0)),
        ),
        out_shape=jax.ShapeDtypeStruct((4 * parts * rows, c), pieces[0].dtype),
        input_output_aliases={1 + len(pieces): 0} if kept else {},
        compiler_params=pltpu.CompilerParams(vmem_limit_bytes=60 << 20),
        cost_estimate=TINY,
        name="put_rows",
    )(jnp.stack(blocks).astype(jnp.int32), *pieces, *kept)


class Scatter:
    def __init__(self, count):
        self.square = by_neighbours(count)

    def first(self, top, low):
        if not self.square:
            return [top]
        self.tx, self.ty = swap(top, 1), swap(low, 2)
        return [self.tx, self.ty]

    def second(self, slots):
        self.slots = slots
        if not self.square:
            every = slots.reshape(-1, slots.shape[-1])
            self.sum = lax.psum_scatter(every, "seq", scatter_dimension=0, tiled=True)
            self.sent = [every]
            return [self.sum]
        sx, sy = add_halves(slots, self.tx, self.ty)
        self.sent = [sx, sy]
        self.rx, self.ry = swap(sx, 1), swap(sy, 2)
        return [self.rx, self.ry]

    def arrived(self):
        return [self.rx, self.ry] if self.square else [self.sum]

    def finish(self):
        if not self.square:
            return self.sum.astype(F32)
        return self.slots[0].astype(F32) + self.rx.astype(F32) + self.ry.astype(F32)


def add_halves_kernel(one_ref, two_ref, tx_ref, ty_ref, sx_ref, sy_ref):
    half = tx_ref.shape[0]
    sx_ref[:half] = one_ref[0, :half]
    sx_ref[half:] = (one_ref[0, half:].astype(F32) + ty_ref[...].astype(F32)).astype(BF16)
    sy_ref[:half] = (two_ref[0, :half].astype(F32) + tx_ref[...].astype(F32)).astype(BF16)
    sy_ref[half:] = two_ref[0, half:]


def add_halves(slots, tx, ty):
    _, rows, c = slots.shape
    half = pl.BlockSpec((rows // 2, c), lambda i: (0, 0))
    whole = pl.BlockSpec((rows, c), lambda i: (0, 0))
    return pl.pallas_call(
        add_halves_kernel,
        grid=(1,),
        in_specs=[
            pl.BlockSpec((1, rows, c), lambda i: (1, 0, 0)),
            pl.BlockSpec((1, rows, c), lambda i: (2, 0, 0)),
            half,
            half,
        ],
        out_specs=(whole, whole),
        out_shape=[jax.ShapeDtypeStruct((rows, c), slots.dtype)] * 2,
        compiler_params=pltpu.CompilerParams(vmem_limit_bytes=60 << 20),
        cost_estimate=TINY,
        name="add_halves",
    )(slots, slots, tx, ty)


def slot_order(count):
    me = lax.axis_index("seq")
    members = [me ^ k if by_neighbours(count) else jnp.int32(k) for k in range(count)]
    return jnp.stack(members).astype(jnp.int32)


def slot_rows(x, order, count, slots):
    rows = x.shape[0] // count
    return jnp.concatenate(
        [lax.dynamic_slice_in_dim(x, order[k] * rows, rows, 0) for k in slots], axis=0
    )


def scattered_product(x, w, order, count, *others, early=True):
    total = Scatter(count)
    rows = x.shape[0] // count
    if not total.square:
        total.last = terms = dot_nt(x, w).astype(BF16)
        total.second(terms.reshape(count, rows, w.shape[0]))
        return total, [terms]
    if early:
        last = dot_nt(slot_rows(x, order, count, (3,)), w).astype(BF16)
        rest = dot_nt(slot_rows(x, order, count, (0, 1, 2)), w).astype(BF16)
        rest = rest.reshape(3, rows, w.shape[0])
    else:
        rest = dot_nt(slot_rows(x, order, count, range(4)), w).astype(BF16)
        rest = rest.reshape(4, rows, w.shape[0])
        last = rest[3]
    total.last = after(last, *others)
    got = total.first(total.last[: rows // 2], total.last[rows // 2 :])
    total.second(rest)
    return total, got


class Gather:
    def __init__(self, x, count):
        self.x, self.count = x, count
        self.square = by_neighbours(count)
        self.me = lax.axis_index("seq")
        self.halves = None

    def first(self):
        if not self.square:
            return [self.x]
        self.bx, self.by = swap(self.x, 1), swap(self.x, 2)
        return [self.bx, self.by]

    def cut(self):
        if not self.square:
            return [self.x]
        if not self.halves:
            half = self.x.shape[0] // 2
            self.halves = [self.by[:half], self.bx[half:]]
        return self.halves

    def second(self, *others):
        if not self.square:
            self.sent = [self.x]
            return [self.x]
        ahead, below = self.cut()
        if others:
            ahead, below, *_ = lax.optimization_barrier((ahead, below, *others))
        self.sent = [ahead, below]
        self.ad, self.bd = swap(ahead, 1), swap(below, 2)
        return [self.ad, self.bd]

    def column(self):
        if not self.square:
            return lax.all_gather(self.x, "seq", axis=0, tiled=True)
        near = put_rows((self.x, self.bx, self.by), (0, 1, 2), 1, None)
        return put_rows((self.ad, self.bd), (3, 3), 2, near)

    def arrived(self):
        return [piece for _, rows in self.all() for piece in rows]

    def near(self):
        if not self.square:
            every = lax.all_gather(self.x, "seq", axis=0, tiled=False)
            return [(jnp.int32(k), (every[k],)) for k in range(self.count)]
        return [(self.me ^ k, (x,)) for k, x in enumerate((self.x, self.bx, self.by))]

    def all(self):
        return self.near() + [
            (member, (jnp.concatenate(rows, axis=0),)) for member, rows in self.far()
        ]

    def far(self):
        return [(self.me ^ 3, (self.ad, self.bd))] if self.square else []


def after(x, *others):
    return lax.optimization_barrier((x, *others))[0]


def in_line(count):
    return count == 8


def gather_weight(w):
    return lax.all_gather(w, "fsdp", axis=0, tiled=True)


def other_core(x):
    return lax.ppermute(x, "fsdp", [(f, f ^ 1) for f in range(8)])


def terms_kernel(starts, blocks, stride, parity_ref, *refs):
    count = len(starts)
    x_refs, d_ref, out_ref = refs[:count], refs[count], refs[-1]
    rows = out_ref.shape[0] // blocks
    j = pl.program_id(0)
    for n, x_ref in enumerate(x_refs):
        last = starts[n + 1] if n + 1 < count else pl.num_programs(0)

        @pl.when((j >= starts[n]) & (j < last))
        def _():
            for i in range(blocks):
                at = pl.multiple_of((stride * i + parity_ref[0]) * rows, rows)
                terms = dot_tn(x_ref[:, pl.ds(at, rows)], d_ref[...])
                here = slice(i * rows, (i + 1) * rows)
                if len(refs) == count + 3:
                    terms = terms + refs[count + 1][here].astype(F32)
                out_ref[here] = terms.astype(BF16)


def weight_terms(xs, d, blocks, stride, parity, got=None):
    length, columns = xs[0][0].shape
    tiles = sum(n for _, n in xs)
    width = d.shape[1] // tiles
    starts = [sum(n for _, n in xs[:m]) for m in range(len(xs))]
    whole = pl.BlockSpec(
        (length, columns), lambda j, parity: (0, 0), pipeline_mode=pl.Buffered(1)
    )
    terms = pl.BlockSpec((columns // stride, width), lambda j, parity: (0, j))
    operands = [x for x, _ in xs] + [d] + ([] if got is None else [got])
    return pl.pallas_call(
        functools.partial(terms_kernel, starts, blocks, stride),
        grid_spec=pltpu.PrefetchScalarGridSpec(
            num_scalar_prefetch=1,
            grid=(tiles,),
            in_specs=[whole] * len(xs)
            + [pl.BlockSpec((length, width), lambda j, parity: (0, j))]
            + ([] if got is None else [terms]),
            out_specs=terms,
        ),
        out_shape=jax.ShapeDtypeStruct((columns // stride, d.shape[1]), BF16),
        compiler_params=pltpu.CompilerParams(vmem_limit_bytes=58 << 20),
        cost_estimate=TINY,
        name="weight_terms",
    )(jnp.reshape(parity, (1,)).astype(jnp.int32), *operands)


class Reduction:
    def __init__(self, xs, d, count, by_core=False):
        self.xs, self.d, self.count = xs, d, count
        self.line = by_core and in_line(count)
        self.core = lax.axis_index("fsdp") % 2

    def odd(self, *others):
        d = after(self.d, *others)
        if self.line:
            self.terms = weight_terms(self.xs, d, 4, 2, 1 - self.core)
            self.got = other_core(self.terms)
        else:
            self.terms = self.got = weight_terms(self.xs, d, 4, 1, jnp.int32(0))
        return self.terms

    def even(self, *others):
        if self.line:
            d = after(self.d, *others)
            self.terms = weight_terms(self.xs, d, 4, 2, self.core, self.got)
        return self.terms

    def total(self, *others):
        terms = after(self.terms, *others)
        groups = [[0, 2, 4, 6], [1, 3, 5, 7]] if self.line else None
        return lax.psum_scatter(
            terms, "fsdp", scatter_dimension=0, axis_index_groups=groups, tiled=True
        )


def sum_all(x, axis, count):
    if count & (count - 1):
        return lax.psum(x, axis)
    bit = 1
    while bit < count:
        x = x + lax.ppermute(x, axis, [(i, i ^ bit) for i in range(count)])
        bit *= 2
    return x


BLOCK = 128
SCALE = HEAD_SIZE ** (-0.5)
LOG2_E = 1.4426950408889634


def head_norm_rope(u, gain, cosine, sine):
    w = inverse_rms(u)
    t = u * w * gain
    return (t * cosine + pltpu.roll(t, HEAD_SIZE // 2, 1) * sine).astype(BF16)


def head_norm_rope_back(u, gain, cosine, sine, e):
    e = e * cosine - pltpu.roll(e, HEAD_SIZE // 2, 1) * sine
    return norm_back(u, gain, e)


def heads_of(refs, gains, cosine, sine, ratio):
    q_ref, k_ref = refs
    queries = [
        head_norm_rope(
            q_ref[:, h * HEAD_SIZE : (h + 1) * HEAD_SIZE].astype(F32), gains[0], cosine, sine
        )
        for h in range(ratio)
    ]
    return queries, head_norm_rope(k_ref[...].astype(F32), gains[1], cosine, sine)


def softmax_rows(queries, key, start, block, i):
    before, keys = i * block, (i + 1) * block
    stacked = jnp.concatenate([q[before:keys] for q in queries], axis=0)
    s = dot_nt(stacked, key[:keys]) * (SCALE * LOG2_E)
    first = jnp.concatenate([start[before:keys]] * len(queries), axis=0)
    here = (s.shape[0], block)
    place = lax.broadcasted_iota(jnp.int32, here, 0) % block
    index = lax.broadcasted_iota(jnp.int32, here, 1)
    allowed = (index <= place) & (index + before >= first)
    e = jnp.where(allowed, jnp.exp2(s[:, before:]), 0.0)
    if before:
        index = lax.broadcasted_iota(jnp.int32, (s.shape[0], before), 1)
        earlier = jnp.where(index >= first, jnp.exp2(s[:, :before]), 0.0)
        e = jnp.concatenate([earlier, e], axis=1)
    return stacked, e * (1.0 / jnp.sum(e, axis=-1, keepdims=True))


def attend_kernel(
    ratio, q_ref, k_ref, v_ref, cos_ref, sin_ref, start_ref, qg_ref, kg_ref, o_ref
):
    gains = qg_ref[...], kg_ref[...]
    queries, key = heads_of((q_ref, k_ref), gains, cos_ref[...], sin_ref[...], ratio)
    start, block = start_ref[...], BLOCK
    for i in range(q_ref.shape[0] // block):
        keys = (i + 1) * block
        _, p = softmax_rows(queries, key, start, block, i)
        o = dot(p.astype(BF16), v_ref[:keys, :]).astype(BF16)
        for h in range(ratio):
            o_ref[i * block : keys, h * HEAD_SIZE : (h + 1) * HEAD_SIZE] = o[
                h * block : (h + 1) * block
            ]


def attend_back_kernel(
    ratio,
    q_ref,
    k_ref,
    v_ref,
    cos_ref,
    sin_ref,
    start_ref,
    qg_ref,
    kg_ref,
    do_ref,
    o_ref,
    dq_ref,
    dk_ref,
    dv_ref,
    qgg_ref,
    kgg_ref,
    dq_all,
    dk_all,
    dv_all,
):
    gains = qg_ref[...], kg_ref[...]
    cosine, sine = cos_ref[...], sin_ref[...]
    queries, key = heads_of((q_ref, k_ref), gains, cosine, sine, ratio)
    start = start_ref[...]
    dk_all[...] = jnp.zeros_like(dk_all)
    dv_all[...] = jnp.zeros_like(dv_all)
    products = do_ref[...].astype(F32) * o_ref[...].astype(F32)
    deltas = [
        jnp.sum(products[:, h * HEAD_SIZE : (h + 1) * HEAD_SIZE], axis=-1, keepdims=True)
        for h in range(ratio)
    ]
    for i in range(q_ref.shape[0] // BLOCK):
        before, keys = i * BLOCK, (i + 1) * BLOCK
        stacked, p = softmax_rows(queries, key, start, BLOCK, i)
        do = jnp.concatenate(
            [do_ref[before:keys, h * HEAD_SIZE : (h + 1) * HEAD_SIZE] for h in range(ratio)], axis=0
        )
        delta = jnp.concatenate([x[before:keys] for x in deltas], axis=0)
        ds = (p * (dot_nt(do, v_ref[:keys, :]) - delta)).astype(BF16)
        dq = dot(ds, key[:keys]) * SCALE
        for h in range(ratio):
            dq_all[h, before:keys, :] = dq[h * BLOCK : (h + 1) * BLOCK]
        dk_all[:keys, :] += dot_tn(ds, stacked)
        dv_all[:keys, :] += dot_tn(p.astype(BF16), do)

    q_terms = jnp.zeros((1, HEAD_SIZE), F32)
    for h in range(ratio):
        columns = slice(h * HEAD_SIZE, (h + 1) * HEAD_SIZE)
        du, terms = head_norm_rope_back(
            q_ref[:, columns].astype(F32), gains[0], cosine, sine, dq_all[h]
        )
        dq_ref[:, columns] = du.astype(BF16)
        q_terms = q_terms + jnp.sum(terms, axis=0, keepdims=True)
    du, terms = head_norm_rope_back(
        k_ref[...].astype(F32), gains[1], cosine, sine, dk_all[...] * SCALE
    )
    dk_ref[...] = du.astype(BF16)
    dv_ref[...] = dv_all[...].astype(BF16)
    qgg_ref[0] = q_terms
    kgg_ref[0] = jnp.sum(terms, axis=0, keepdims=True)


def attention_specs(length, q_heads, kv_heads):
    ratio = q_heads // kv_heads
    wide = pl.BlockSpec((length, ratio * HEAD_SIZE), lambda g: (0, g))
    narrow = pl.BlockSpec((length, HEAD_SIZE), lambda g: (0, g))
    table = pl.BlockSpec((length, HEAD_SIZE), lambda g: (0, 0))
    gain = pl.BlockSpec((1, HEAD_SIZE), lambda g: (0, 0))
    inputs = [
        wide,
        pl.BlockSpec((length, HEAD_SIZE), lambda g: (0, q_heads + g)),
        pl.BlockSpec((length, HEAD_SIZE), lambda g: (0, q_heads + kv_heads + g)),
        table,
        table,
        pl.BlockSpec((length, 1), lambda g: (0, 0)),
        gain,
        gain,
    ]
    return ratio, wide, narrow, inputs


def attention_cost(length, q_heads, products):
    flops = products * q_heads * length * length * HEAD_SIZE
    return pl.CostEstimate(
        flops=flops, bytes_accessed=16 * length * q_heads * HEAD_SIZE, transcendentals=q_heads * length * length
    )


def attend(qkv, tables, start, gains, q_heads, kv_heads):
    length = qkv.shape[0]
    ratio, wide, _, inputs = attention_specs(length, q_heads, kv_heads)
    return pl.pallas_call(
        functools.partial(attend_kernel, ratio),
        grid=(kv_heads,),
        in_specs=inputs,
        out_specs=wide,
        out_shape=jax.ShapeDtypeStruct((length, q_heads * HEAD_SIZE), BF16),
        compiler_params=pltpu.CompilerParams(vmem_limit_bytes=56 << 20),
        cost_estimate=TINY,
        name="attend",
    )(qkv, qkv, qkv, *tables, start, *gains)


def attend_back(qkv, tables, start, gains, d_o, o, q_heads, kv_heads):
    length = qkv.shape[0]
    ratio, wide, narrow, inputs = attention_specs(length, q_heads, kv_heads)
    gain_spec = pl.BlockSpec((1, 1, HEAD_SIZE), lambda g: (g, 0, 0))
    gain_shape = jax.ShapeDtypeStruct((kv_heads, 1, HEAD_SIZE), F32)
    kv_shape = jax.ShapeDtypeStruct((length, kv_heads * HEAD_SIZE), BF16)
    return pl.pallas_call(
        functools.partial(attend_back_kernel, ratio),
        grid=(kv_heads,),
        in_specs=inputs + [wide, wide],
        out_specs=(wide, narrow, narrow, gain_spec, gain_spec),
        out_shape=(
            jax.ShapeDtypeStruct((length, q_heads * HEAD_SIZE), BF16),
            kv_shape,
            kv_shape,
            gain_shape,
            gain_shape,
        ),
        scratch_shapes=[
            pltpu.VMEM((ratio, length, HEAD_SIZE), F32),
            pltpu.VMEM((length, HEAD_SIZE), F32),
            pltpu.VMEM((length, HEAD_SIZE), F32),
        ],
        compiler_params=pltpu.CompilerParams(vmem_limit_bytes=56 << 20),
        cost_estimate=TINY,
        name="attend_back",
    )(qkv, qkv, qkv, *tables, start, *gains, d_o, o)


def feed_forward_kernel(carried, piece, order_ref, xb_ref, dy_ref, w_ref, *refs):
    sums = refs[:2] if carried else (None, None)
    d_ref, dxb_ref, out_ref = refs[-3:]
    xb, dy = xb_ref[...], dy_ref[...]
    gate = dot(xb, w_ref[:, :piece])
    upper = dot(xb, w_ref[:, piece : 2 * piece])
    d_hidden = dot(dy, w_ref[:, 2 * piece :])
    sigma = 1.0 / (1.0 + jnp.exp(-gate))
    silu = gate * sigma
    hidden = (silu * upper).astype(BF16)
    d_gate = (d_hidden * upper * sigma * (1.0 + gate * (1.0 - sigma))).astype(BF16)
    d_up = (d_hidden * silu).astype(BF16)
    d_ref[:, :piece] = d_gate
    d_ref[:, piece : 2 * piece] = d_up
    d_ref[:, 2 * piece :] = hidden
    d_xb = dot_nt(d_gate, w_ref[:, :piece]) + dot_nt(d_up, w_ref[:, piece : 2 * piece])
    out = dot_nt(hidden, w_ref[:, 2 * piece :])
    if carried:
        d_xb = d_xb + sums[0][0]
        out = out + sums[1][0]
    dxb_ref[0] = d_xb.astype(dxb_ref.dtype)
    out_ref[0] = out.astype(out_ref.dtype)


def feed_forward(xb, dy, w, order, sums, kind):
    length, width = xb.shape
    piece = w.shape[1] // 3
    count = order.shape[0]
    block = length // count
    rows = pl.BlockSpec((block, width), lambda i, order: (order[i], 0))
    whole = pl.BlockSpec(w.shape, lambda i, order: (0, 0), pipeline_mode=pl.Buffered(1))
    summed = pl.BlockSpec((1, block, width), lambda i, order: (i, 0, 0))
    total = jax.ShapeDtypeStruct((count, block, width), kind)
    return pl.pallas_call(
        functools.partial(feed_forward_kernel, bool(sums), piece),
        grid_spec=pltpu.PrefetchScalarGridSpec(
            num_scalar_prefetch=1,
            grid=(count,),
            in_specs=[rows, rows, whole] + [summed] * len(sums),
            out_specs=(
                pl.BlockSpec((block, 3 * piece), lambda i, order: (order[i], 0)),
                summed,
                summed,
            ),
        ),
        out_shape=(jax.ShapeDtypeStruct((length, 3 * piece), BF16), total, total),
        compiler_params=pltpu.CompilerParams(vmem_limit_bytes=60 << 20),
        cost_estimate=TINY,
        name="feed_forward",
    )(order, xb, dy, w, *sums)


def place_kernel(widths, tiles, pieces, order_ref, *refs):
    outs = refs[-len(widths) :]
    k, t = pl.program_id(0), pl.program_id(1)
    for n in range(pl.num_programs(0)):
        mine = refs[sum(pieces[:n]) : sum(pieces[: n + 1])]
        for m in range(tiles):

            @pl.when((k == n) & (t == m))
            def _():
                start = 0
                for out_ref, width in zip(outs, widths):
                    size = width // tiles
                    at, row = start + m * size, 0
                    for piece in mine:
                        rows = piece.shape[0]
                        out_ref[row : row + rows, :] = piece[:, at : at + size].astype(F32)
                        row += rows
                    start += width


def place(blocks, widths, tiles, first, every, outs, count):
    pieces = [piece for _, rows in blocks for piece in rows]
    rows = sum(piece.shape[0] for piece in blocks[0][1])

    def out_map(k, t, order_ref):
        return 0, order_ref[k] * every + first + t

    any_spec = pl.BlockSpec(memory_space=pl.ANY)
    n = len(pieces)
    return pl.pallas_call(
        functools.partial(place_kernel, widths, tiles, [len(x) for _, x in blocks]),
        grid_spec=pltpu.PrefetchScalarGridSpec(
            num_scalar_prefetch=1,
            grid=(len(blocks), tiles),
            in_specs=[pl.BlockSpec(x.shape, lambda k, t, order_ref: (0, 0)) for x in pieces]
            + [any_spec] * len(outs),
            out_specs=[pl.BlockSpec((rows, w // tiles), out_map) for w in widths],
        ),
        out_shape=[
            jax.ShapeDtypeStruct((rows, w // tiles * every * count), F32) for w in widths
        ],
        input_output_aliases={1 + n + m: m for m in range(len(outs))},
        compiler_params=pltpu.CompilerParams(vmem_limit_bytes=40 << 20),
        name="place",
        cost_estimate=TINY,
    )(jnp.stack([k for k, _ in blocks]).astype(jnp.int32), *pieces, *outs)


def make_body(counts):
    seq_count, fsdp_count = counts["seq"], counts["fsdp"]

    def body(
        tokens,
        segment_ids,
        input_gain,
        query_weight,
        key_projection_weight,
        value_projection_weight,
        output_weight,
        query_gain,
        key_gain,
        post_gain,
        gate_weight,
        up_weight,
        down_weight,
        cotangent,
    ):
        me = lax.axis_index("seq")
        rows = query_weight.shape[0]
        q_heads = QUERY_HEADS // seq_count
        kv_heads = KEY_VALUE_HEADS // seq_count
        ratio = QUERY_HEADS // KEY_VALUE_HEADS
        q_cols, kv_cols = q_heads * HEAD_SIZE, kv_heads * HEAD_SIZE
        qkv_cols = q_cols + 2 * kv_cols
        f_cols = gate_weight.shape[1] // seq_count
        pieces = (f_cols // 3 * 2, f_cols // 3)
        def share(w, cols, start=0, size=None):
            return lax.dynamic_slice(w, (0, me * cols + start), (rows, size or cols))

        w_attn = gather_weight(
            jnp.concatenate(
                [
                    share(query_weight, q_cols),
                    share(key_projection_weight, kv_cols),
                    share(value_projection_weight, kv_cols),
                    share(output_weight, q_cols),
                ],
                axis=1,
            )
        )
        w_qkv, w_out = w_attn[:, :qkv_cols], w_attn[:, qkv_cols:]
        w_mlp = [
            gather_weight(
                jnp.concatenate(
                    [share(w, f_cols, start, size) for w in (gate_weight, up_weight, down_weight)],
                    axis=1,
                )
            )
            for start, size in zip((0, pieces[0]), pieces)
        ]

        inputs = tokens[0].astype(F32)
        segments = segment_ids[0]
        order = slot_order(seq_count)
        get_dy = Gather(cotangent[0], seq_count)
        get_dy.first()
        get_xa = Gather((inputs * inverse_rms(inputs) * input_gain).astype(BF16), seq_count)
        get_xa.first()
        get_xa.second()
        xa = get_xa.column()

        place_in_document = positions(segments)
        tables = rotary_tables(place_in_document)
        start = (jnp.arange(segments.shape[0], dtype=jnp.int32) - place_in_document)[:, None]
        head_gains = query_gain[None, :], key_gain[None, :]
        qkv = dot(xa, w_qkv).astype(BF16)
        get_dy.second(qkv)
        dy = get_dy.column()
        o = attend(qkv, tables, start, head_gains, q_heads, kv_heads)
        sum_r, _ = scattered_product(after(o, dy), w_out, order, seq_count)
        resid = inputs + sum_r.finish()
        get_xb = Gather((resid * inverse_rms(resid) * post_gain).astype(BF16), seq_count)
        get_xb.first()
        get_xb.second()
        xb = get_xb.column()

        d1, *sums = feed_forward(xb, dy, w_mlp[0], order, (), F32)
        red1 = Reduction([(xb, 2), (dy, 1)], d1, fsdp_count)
        terms1 = red1.odd()
        share1 = red1.total()
        xb2 = after(xb, terms1)
        d2, d_xb, out = feed_forward(xb2, dy, w_mlp[1], order, tuple(sums), BF16)
        sum_dxb, sum_out = Scatter(seq_count), Scatter(seq_count)
        half = d_xb.shape[1] // 2
        got = sum_dxb.first(d_xb[-1, :half], d_xb[-1, half:])
        got += sum_out.first(out[-1, :half], out[-1, half:])
        sum_dxb.second(after(d_xb, *got))
        red2 = Reduction([(xb, 2), (dy, 1)], d2, fsdp_count)
        terms2 = red2.odd(*sum_dxb.sent)
        du, post_terms = norm_back(resid, post_gain, after(sum_dxb.finish(), terms2))
        d_resid = cotangent[0].astype(F32) + du
        get_drl = Gather(d_resid.astype(BF16), seq_count)
        get_drl.first()
        get_drl.second()
        share2 = red2.total(*get_drl.sent)
        drl = get_drl.column()
        halves = sum_out.second(after(out, drl))
        d_o = dot(drl, w_out).astype(BF16)
        dq, dk, dv, q_terms, k_terms = attend_back(
            qkv, tables, start, head_gains, after(d_o, *sum_out.sent), o, q_heads, kv_heads
        )
        dq = after(dq, *halves)
        get1 = Gather(after(share1, dq), seq_count)
        near = get1.first()
        d_attn = jnp.concatenate([dq, dk, dv, o], axis=1)
        red3 = Reduction([(xa, 2), (drl, 1)], d_attn, fsdp_count)
        terms3 = red3.odd()
        d_qkv = after(d_attn, terms3)[:, :qkv_cols]
        sum_dxa, got = scattered_product(
            d_qkv, w_qkv, order, seq_count, *near, *get1.cut(), early=False
        )
        get1.second(*got)
        out = resid + after(sum_out.finish(), *got)
        share3 = red3.total(share2, *got)
        du, in_terms = norm_back(inputs, input_gain, after(sum_dxa.finish(), *get1.arrived()))
        d_inputs = d_resid + du

        gains = jnp.concatenate(
            [
                jnp.sum(in_terms, axis=0),
                jnp.sum(post_terms, axis=0),
                jnp.sum(q_terms, axis=(0, 1)),
                jnp.sum(k_terms, axis=(0, 1)),
            ]
        )
        width = post_gain.shape[0]
        get2 = Gather(after(share2, *get1.arrived(), *sum_dxa.arrived()), seq_count)
        get2.first()
        gains = sum_all(gains, "fsdp", fsdp_count)
        mlp = place(get1.all(), (pieces[0],) * 3, 2, 0, 3, (), seq_count)
        get2.second(gains, *mlp)
        get3 = Gather(after(share3, *get2.arrived()), seq_count)
        get3.first()
        mlp = place(get2.all(), (pieces[1],) * 3, 1, 2, 3, mlp, seq_count)
        gains = sum_all(after(gains, *get2.arrived()), "seq", seq_count)
        get3.second(gains, *mlp)
        widths = (q_cols, kv_cols, kv_cols, q_cols)
        attn = place(get3.near(), widths, 1, 0, 1, (), seq_count)
        if get3.far():
            attn = place(get3.far(), widths, 1, 0, 1, attn, seq_count)
        g_q, g_k, g_v, g_out = attn
        return (
            out.astype(BF16)[None],
            d_inputs.astype(BF16)[None],
            gains[:width],
            g_q,
            g_k,
            g_v,
            g_out,
            gains[2 * width : 2 * width + HEAD_SIZE],
            gains[2 * width + HEAD_SIZE :],
            gains[width : 2 * width],
            *mlp,
        )

    return body


def solution(mesh):
    rows, acts = P("fsdp", None), P("fsdp", "seq", None)
    return jax.shard_map(
        make_body({"seq": mesh.shape["seq"], "fsdp": mesh.shape["fsdp"]}),
        mesh=mesh,
        in_specs=(
            acts, rows, P(), rows, rows, rows, rows, P(), P(), P(), rows, rows, rows, acts,
        ),
        out_specs=(acts, acts, P(), rows, rows, rows, rows, P(), P(), P(), rows, rows, rows),
        check_vma=False,
    )
```

```python
import functools

import jax
import jax.numpy as jnp
from jax import lax
from jax.experimental import pallas as pl
from jax.experimental.pallas import tpu as pltpu
from jax.sharding import PartitionSpec as P

QUERY_HEADS = 16
KEY_VALUE_HEADS = 8
HEAD_SIZE = 128
NORM_EPSILON = 1e-06
ROPE_BASE = 1000000.0
F32 = jnp.float32
BF16 = jnp.bfloat16
TINY = pl.CostEstimate(flops=1000, bytes_accessed=1000, transcendentals=0)


def dot(a, b):
    return jnp.dot(a, b, preferred_element_type=F32)


def dot_nt(a, b):
    return lax.dot_general(a, b, (((1,), (1,)), ((), ())), preferred_element_type=F32)


def dot_tn(a, b):
    return lax.dot_general(a, b, (((0,), (0,)), ((), ())), preferred_element_type=F32)


def inverse_rms(u):
    return lax.rsqrt(jnp.mean(u * u, axis=-1, keepdims=True) + NORM_EPSILON)


def norm_back(u, gain, e):
    w = inverse_rms(u)
    n = u * w
    t = e * gain
    du = w * (t - n * jnp.mean(n * t, axis=-1, keepdims=True))
    return du, e * n


def positions(segments):
    index = jnp.arange(segments.shape[0], dtype=jnp.int32)
    first = jnp.concatenate([jnp.ones((1,), dtype=jnp.bool_), segments[1:] != segments[:-1]])
    starts = lax.cummax(jnp.where(first, index, jnp.zeros_like(index)), axis=0)
    return index - starts


def rotary_tables(position_index):
    half = HEAD_SIZE // 2
    freq = ROPE_BASE ** (-jnp.arange(half, dtype=F32) * 2.0 / HEAD_SIZE)
    angle = position_index.astype(F32)[:, None] * freq[None, :]
    cosine, sine = jnp.cos(angle), jnp.sin(angle)
    return jnp.concatenate([cosine, cosine], axis=-1), jnp.concatenate([-sine, sine], axis=-1)


def by_neighbours(count):
    return count == 4


def swap(x, side):
    return lax.ppermute(x, "seq", [(s, s ^ side) for s in range(4)])


def put_rows_kernel(count, order_ref, *refs):
    for n in range(count):

        @pl.when(pl.program_id(0) == n)
        def _():
            refs[-1][...] = refs[n][...]


def put_rows(pieces, offsets, parts, out):
    me = lax.axis_index("seq")
    blocks = [(me ^ k) * parts + n % parts for n, k in enumerate(offsets)]
    rows, c = pieces[0].shape
    kept = [] if out is None else [out]
    return pl.pallas_call(
        functools.partial(put_rows_kernel, len(pieces)),
        grid_spec=pltpu.PrefetchScalarGridSpec(
            num_scalar_prefetch=1,
            grid=(len(pieces),),
            in_specs=[pl.BlockSpec((rows, c), lambda n, order: (0, 0))] * len(pieces)
            + [pl.BlockSpec(memory_space=pl.ANY)] * len(kept),
            out_specs=pl.BlockSpec((rows, c), lambda n, order: (order[n], 0)),
        ),
        out_shape=jax.ShapeDtypeStruct((4 * parts * rows, c), pieces[0].dtype),
        input_output_aliases={1 + len(pieces): 0} if kept else {},
        compiler_params=pltpu.CompilerParams(vmem_limit_bytes=60 << 20),
        cost_estimate=TINY,
        name="put_rows",
    )(jnp.stack(blocks).astype(jnp.int32), *pieces, *kept)


class Scatter:
    def __init__(self, count):
        self.square = by_neighbours(count)

    def first(self, top, low):
        if not self.square:
            return [top]
        self.tx, self.ty = swap(top, 1), swap(low, 2)
        return [self.tx, self.ty]

    def second(self, slots, *others):
        self.slots = slots
        if not self.square:
            every = after(slots, *others).reshape(-1, slots.shape[-1])
            self.sum = lax.psum_scatter(every, "seq", scatter_dimension=0, tiled=True)
            self.sent = [every]
            return [self.sum]
        sx, sy = add_halves(slots, self.tx, self.ty)
        if others:
            sx, sy, *_ = lax.optimization_barrier((sx, sy, *others))
        self.sent = [sx, sy]
        self.rx, self.ry = swap(sx, 1), swap(sy, 2)
        return [self.rx, self.ry]

    def arrived(self):
        return [self.rx, self.ry] if self.square else [self.sum]

    def finish(self):
        if not self.square:
            return self.sum.astype(F32)
        return self.slots[0].astype(F32) + self.rx.astype(F32) + self.ry.astype(F32)


def add_halves_kernel(one_ref, two_ref, tx_ref, ty_ref, sx_ref, sy_ref):
    half = tx_ref.shape[0]
    sx_ref[:half] = one_ref[0, :half]
    sx_ref[half:] = (one_ref[0, half:].astype(F32) + ty_ref[...].astype(F32)).astype(BF16)
    sy_ref[:half] = (two_ref[0, :half].astype(F32) + tx_ref[...].astype(F32)).astype(BF16)
    sy_ref[half:] = two_ref[0, half:]


def add_halves(slots, tx, ty):
    _, rows, c = slots.shape
    half = pl.BlockSpec((rows // 2, c), lambda i: (0, 0))
    whole = pl.BlockSpec((rows, c), lambda i: (0, 0))
    return pl.pallas_call(
        add_halves_kernel,
        grid=(1,),
        in_specs=[
            pl.BlockSpec((1, rows, c), lambda i: (1, 0, 0)),
            pl.BlockSpec((1, rows, c), lambda i: (2, 0, 0)),
            half,
            half,
        ],
        out_specs=(whole, whole),
        out_shape=[jax.ShapeDtypeStruct((rows, c), slots.dtype)] * 2,
        compiler_params=pltpu.CompilerParams(vmem_limit_bytes=60 << 20),
        cost_estimate=TINY,
        name="add_halves",
    )(slots, slots, tx, ty)


def slot_order(count):
    me = lax.axis_index("seq")
    members = [me ^ k if by_neighbours(count) else jnp.int32(k) for k in range(count)]
    return jnp.stack(members).astype(jnp.int32)


def slot_rows(x, order, count, slots):
    rows = x.shape[0] // count
    return jnp.concatenate(
        [lax.dynamic_slice_in_dim(x, order[k] * rows, rows, 0) for k in slots], axis=0
    )


def scattered_product(x, w, order, count, *others, early=True):
    total = Scatter(count)
    rows = x.shape[0] // count
    if not total.square:
        total.last = terms = dot_nt(x, w).astype(BF16)
        total.second(terms.reshape(count, rows, w.shape[0]))
        return total, [terms]
    if early:
        last = dot_nt(slot_rows(x, order, count, (3,)), w).astype(BF16)
        rest = dot_nt(slot_rows(x, order, count, (0, 1, 2)), w).astype(BF16)
        rest = rest.reshape(3, rows, w.shape[0])
    else:
        rest = dot_nt(slot_rows(x, order, count, range(4)), w).astype(BF16)
        rest = rest.reshape(4, rows, w.shape[0])
        last = rest[3]
    total.last = after(last, *others)
    got = total.first(total.last[: rows // 2], total.last[rows // 2 :])
    total.second(rest)
    return total, got


class Gather:
    def __init__(self, x, count):
        self.x, self.count = x, count
        self.square = by_neighbours(count)
        self.me = lax.axis_index("seq")
        self.halves = None

    def first(self):
        if not self.square:
            return [self.x]
        self.bx, self.by = swap(self.x, 1), swap(self.x, 2)
        return [self.bx, self.by]

    def cut(self):
        if not self.square:
            return [self.x]
        if not self.halves:
            half = self.x.shape[0] // 2
            self.halves = [self.by[:half], self.bx[half:]]
        return self.halves

    def second(self, *others):
        if not self.square:
            self.sent = [self.x]
            return [self.x]
        ahead, below = self.cut()
        if others:
            ahead, below, *_ = lax.optimization_barrier((ahead, below, *others))
        self.sent = [ahead, below]
        self.ad, self.bd = swap(ahead, 1), swap(below, 2)
        return [self.ad, self.bd]

    def column(self):
        if not self.square:
            return lax.all_gather(self.x, "seq", axis=0, tiled=True)
        near = put_rows((self.x, self.bx, self.by), (0, 1, 2), 1, None)
        return put_rows((self.ad, self.bd), (3, 3), 2, near)

    def arrived(self):
        return [piece for _, rows in self.all() for piece in rows]

    def near(self):
        if not self.square:
            every = lax.all_gather(self.x, "seq", axis=0, tiled=False)
            return [(jnp.int32(k), (every[k],)) for k in range(self.count)]
        return [(self.me ^ k, (x,)) for k, x in enumerate((self.x, self.bx, self.by))]

    def all(self):
        return self.near() + [
            (member, (jnp.concatenate(rows, axis=0),)) for member, rows in self.far()
        ]

    def far(self):
        return [(self.me ^ 3, (self.ad, self.bd))] if self.square else []


def after(x, *others):
    return lax.optimization_barrier((x, *others))[0]


def in_line(count):
    return count == 8


def gather_weight(w):
    return lax.all_gather(w, "fsdp", axis=0, tiled=True)


def other_core(x):
    return lax.ppermute(x, "fsdp", [(f, f ^ 1) for f in range(8)])


def terms_kernel(starts, blocks, stride, parity_ref, *refs):
    count = len(starts)
    x_refs, d_ref, out_ref = refs[:count], refs[count], refs[-1]
    rows = out_ref.shape[0] // blocks
    j = pl.program_id(0)
    for n, x_ref in enumerate(x_refs):
        last = starts[n + 1] if n + 1 < count else pl.num_programs(0)

        @pl.when((j >= starts[n]) & (j < last))
        def _():
            for i in range(blocks):
                at = pl.multiple_of((stride * i + parity_ref[0]) * rows, rows)
                terms = dot_tn(x_ref[:, pl.ds(at, rows)], d_ref[...])
                here = slice(i * rows, (i + 1) * rows)
                if len(refs) == count + 3:
                    terms = terms + refs[count + 1][here].astype(F32)
                out_ref[here] = terms.astype(BF16)


def weight_terms(xs, d, blocks, stride, parity, got=None):
    length, columns = xs[0][0].shape
    tiles = sum(n for _, n in xs)
    width = d.shape[1] // tiles
    starts = [sum(n for _, n in xs[:m]) for m in range(len(xs))]
    whole = pl.BlockSpec(
        (length, columns), lambda j, parity: (0, 0), pipeline_mode=pl.Buffered(1)
    )
    terms = pl.BlockSpec((columns // stride, width), lambda j, parity: (0, j))
    operands = [x for x, _ in xs] + [d] + ([] if got is None else [got])
    return pl.pallas_call(
        functools.partial(terms_kernel, starts, blocks, stride),
        grid_spec=pltpu.PrefetchScalarGridSpec(
            num_scalar_prefetch=1,
            grid=(tiles,),
            in_specs=[whole] * len(xs)
            + [pl.BlockSpec((length, width), lambda j, parity: (0, j))]
            + ([] if got is None else [terms]),
            out_specs=terms,
        ),
        out_shape=jax.ShapeDtypeStruct((columns // stride, d.shape[1]), BF16),
        compiler_params=pltpu.CompilerParams(vmem_limit_bytes=58 << 20),
        cost_estimate=TINY,
        name="weight_terms",
    )(jnp.reshape(parity, (1,)).astype(jnp.int32), *operands)


class Reduction:
    def __init__(self, xs, d, count, by_core=False):
        self.xs, self.d, self.count = xs, d, count
        self.line = by_core and in_line(count)
        self.core = lax.axis_index("fsdp") % 2

    def odd(self, *others):
        d = after(self.d, *others)
        if self.line:
            self.terms = weight_terms(self.xs, d, 4, 2, 1 - self.core)
            self.got = other_core(self.terms)
        else:
            self.terms = self.got = weight_terms(self.xs, d, 4, 1, jnp.int32(0))
        return self.terms

    def even(self, *others):
        if self.line:
            d = after(self.d, *others)
            self.terms = weight_terms(self.xs, d, 4, 2, self.core, self.got)
        return self.terms

    def total(self, *others):
        terms = after(self.terms, *others)
        groups = [[0, 2, 4, 6], [1, 3, 5, 7]] if self.line else None
        return lax.psum_scatter(
            terms, "fsdp", scatter_dimension=0, axis_index_groups=groups, tiled=True
        )


def sum_all(x, axis, count):
    if count & (count - 1):
        return lax.psum(x, axis)
    bit = 1
    while bit < count:
        x = x + lax.ppermute(x, axis, [(i, i ^ bit) for i in range(count)])
        bit *= 2
    return x


BLOCK = 128
SCALE = HEAD_SIZE ** (-0.5)
LOG2_E = 1.4426950408889634


def head_norm_rope(u, gain, cosine, sine):
    w = inverse_rms(u)
    t = u * w * gain
    return (t * cosine + pltpu.roll(t, HEAD_SIZE // 2, 1) * sine).astype(BF16)


def head_norm_rope_back(u, gain, cosine, sine, e):
    e = e * cosine - pltpu.roll(e, HEAD_SIZE // 2, 1) * sine
    return norm_back(u, gain, e)


def heads_of(refs, gains, cosine, sine, ratio):
    q_ref, k_ref = refs
    queries = [
        head_norm_rope(
            q_ref[:, h * HEAD_SIZE : (h + 1) * HEAD_SIZE].astype(F32), gains[0], cosine, sine
        )
        for h in range(ratio)
    ]
    return queries, head_norm_rope(k_ref[...].astype(F32), gains[1], cosine, sine)


def softmax_rows(queries, key, start, block, i):
    before, keys = i * block, (i + 1) * block
    stacked = jnp.concatenate([q[before:keys] for q in queries], axis=0)
    s = dot_nt(stacked, key[:keys]) * (SCALE * LOG2_E)
    first = jnp.concatenate([start[before:keys]] * len(queries), axis=0)
    here = (s.shape[0], block)
    place = lax.broadcasted_iota(jnp.int32, here, 0) % block
    index = lax.broadcasted_iota(jnp.int32, here, 1)
    allowed = (index <= place) & (index + before >= first)
    e = jnp.where(allowed, jnp.exp2(s[:, before:]), 0.0)
    if before:
        index = lax.broadcasted_iota(jnp.int32, (s.shape[0], before), 1)
        earlier = jnp.where(index >= first, jnp.exp2(s[:, :before]), 0.0)
        e = jnp.concatenate([earlier, e], axis=1)
    return stacked, e * (1.0 / jnp.sum(e, axis=-1, keepdims=True))


def attend_kernel(
    ratio, q_ref, k_ref, v_ref, cos_ref, sin_ref, start_ref, qg_ref, kg_ref, o_ref
):
    gains = qg_ref[...], kg_ref[...]
    queries, key = heads_of((q_ref, k_ref), gains, cos_ref[...], sin_ref[...], ratio)
    start, block = start_ref[...], BLOCK
    for i in range(q_ref.shape[0] // block):
        keys = (i + 1) * block
        _, p = softmax_rows(queries, key, start, block, i)
        o = dot(p.astype(BF16), v_ref[:keys, :]).astype(BF16)
        for h in range(ratio):
            o_ref[i * block : keys, h * HEAD_SIZE : (h + 1) * HEAD_SIZE] = o[
                h * block : (h + 1) * block
            ]


def attend_back_kernel(
    ratio,
    q_ref,
    k_ref,
    v_ref,
    cos_ref,
    sin_ref,
    start_ref,
    qg_ref,
    kg_ref,
    do_ref,
    o_ref,
    dq_ref,
    dk_ref,
    dv_ref,
    qgg_ref,
    kgg_ref,
    dq_all,
    dk_all,
    dv_all,
):
    gains = qg_ref[...], kg_ref[...]
    cosine, sine = cos_ref[...], sin_ref[...]
    queries, key = heads_of((q_ref, k_ref), gains, cosine, sine, ratio)
    start = start_ref[...]
    dk_all[...] = jnp.zeros_like(dk_all)
    dv_all[...] = jnp.zeros_like(dv_all)
    products = do_ref[...].astype(F32) * o_ref[...].astype(F32)
    deltas = [
        jnp.sum(products[:, h * HEAD_SIZE : (h + 1) * HEAD_SIZE], axis=-1, keepdims=True)
        for h in range(ratio)
    ]
    for i in range(q_ref.shape[0] // BLOCK):
        before, keys = i * BLOCK, (i + 1) * BLOCK
        stacked, p = softmax_rows(queries, key, start, BLOCK, i)
        do = jnp.concatenate(
            [do_ref[before:keys, h * HEAD_SIZE : (h + 1) * HEAD_SIZE] for h in range(ratio)], axis=0
        )
        delta = jnp.concatenate([x[before:keys] for x in deltas], axis=0)
        ds = (p * (dot_nt(do, v_ref[:keys, :]) - delta)).astype(BF16)
        dq = dot(ds, key[:keys]) * SCALE
        for h in range(ratio):
            dq_all[h, before:keys, :] = dq[h * BLOCK : (h + 1) * BLOCK]
        dk_all[:keys, :] += dot_tn(ds, stacked)
        dv_all[:keys, :] += dot_tn(p.astype(BF16), do)

    q_terms = jnp.zeros((1, HEAD_SIZE), F32)
    for h in range(ratio):
        columns = slice(h * HEAD_SIZE, (h + 1) * HEAD_SIZE)
        du, terms = head_norm_rope_back(
            q_ref[:, columns].astype(F32), gains[0], cosine, sine, dq_all[h]
        )
        dq_ref[:, columns] = du.astype(BF16)
        q_terms = q_terms + jnp.sum(terms, axis=0, keepdims=True)
    du, terms = head_norm_rope_back(
        k_ref[...].astype(F32), gains[1], cosine, sine, dk_all[...] * SCALE
    )
    dk_ref[...] = du.astype(BF16)
    dv_ref[...] = dv_all[...].astype(BF16)
    qgg_ref[0] = q_terms
    kgg_ref[0] = jnp.sum(terms, axis=0, keepdims=True)


def attention_specs(length, q_heads, kv_heads):
    ratio = q_heads // kv_heads
    wide = pl.BlockSpec((length, ratio * HEAD_SIZE), lambda g: (0, g))
    narrow = pl.BlockSpec((length, HEAD_SIZE), lambda g: (0, g))
    table = pl.BlockSpec((length, HEAD_SIZE), lambda g: (0, 0))
    gain = pl.BlockSpec((1, HEAD_SIZE), lambda g: (0, 0))
    inputs = [
        wide,
        pl.BlockSpec((length, HEAD_SIZE), lambda g: (0, q_heads + g)),
        pl.BlockSpec((length, HEAD_SIZE), lambda g: (0, q_heads + kv_heads + g)),
        table,
        table,
        pl.BlockSpec((length, 1), lambda g: (0, 0)),
        gain,
        gain,
    ]
    return ratio, wide, narrow, inputs


def attention_cost(length, q_heads, products):
    flops = products * q_heads * length * length * HEAD_SIZE
    return pl.CostEstimate(
        flops=flops, bytes_accessed=16 * length * q_heads * HEAD_SIZE, transcendentals=q_heads * length * length
    )


def attend(qkv, tables, start, gains, q_heads, kv_heads):
    length = qkv.shape[0]
    ratio, wide, _, inputs = attention_specs(length, q_heads, kv_heads)
    return pl.pallas_call(
        functools.partial(attend_kernel, ratio),
        grid=(kv_heads,),
        in_specs=inputs,
        out_specs=wide,
        out_shape=jax.ShapeDtypeStruct((length, q_heads * HEAD_SIZE), BF16),
        compiler_params=pltpu.CompilerParams(vmem_limit_bytes=56 << 20),
        cost_estimate=TINY,
        name="attend",
    )(qkv, qkv, qkv, *tables, start, *gains)


def attend_back(qkv, tables, start, gains, d_o, o, q_heads, kv_heads):
    length = qkv.shape[0]
    ratio, wide, narrow, inputs = attention_specs(length, q_heads, kv_heads)
    gain_spec = pl.BlockSpec((1, 1, HEAD_SIZE), lambda g: (g, 0, 0))
    gain_shape = jax.ShapeDtypeStruct((kv_heads, 1, HEAD_SIZE), F32)
    kv_shape = jax.ShapeDtypeStruct((length, kv_heads * HEAD_SIZE), BF16)
    return pl.pallas_call(
        functools.partial(attend_back_kernel, ratio),
        grid=(kv_heads,),
        in_specs=inputs + [wide, wide],
        out_specs=(wide, narrow, narrow, gain_spec, gain_spec),
        out_shape=(
            jax.ShapeDtypeStruct((length, q_heads * HEAD_SIZE), BF16),
            kv_shape,
            kv_shape,
            gain_shape,
            gain_shape,
        ),
        scratch_shapes=[
            pltpu.VMEM((ratio, length, HEAD_SIZE), F32),
            pltpu.VMEM((length, HEAD_SIZE), F32),
            pltpu.VMEM((length, HEAD_SIZE), F32),
        ],
        compiler_params=pltpu.CompilerParams(vmem_limit_bytes=56 << 20),
        cost_estimate=TINY,
        name="attend_back",
    )(qkv, qkv, qkv, *tables, start, *gains, d_o, o)


def feed_forward_kernel(carried, piece, order_ref, xb_ref, dy_ref, w_ref, *refs):
    sums = refs[:2] if carried else (None, None)
    d_ref, dxb_ref, out_ref = refs[-3:]
    xb, dy = xb_ref[...], dy_ref[...]
    gate = dot(xb, w_ref[:, :piece])
    upper = dot(xb, w_ref[:, piece : 2 * piece])
    d_hidden = dot(dy, w_ref[:, 2 * piece :])
    sigma = 1.0 / (1.0 + jnp.exp(-gate))
    silu = gate * sigma
    hidden = (silu * upper).astype(BF16)
    d_gate = (d_hidden * upper * sigma * (1.0 + gate * (1.0 - sigma))).astype(BF16)
    d_up = (d_hidden * silu).astype(BF16)
    d_ref[:, :piece] = d_gate
    d_ref[:, piece : 2 * piece] = d_up
    d_ref[:, 2 * piece :] = hidden
    d_xb = dot_nt(d_gate, w_ref[:, :piece]) + dot_nt(d_up, w_ref[:, piece : 2 * piece])
    out = dot_nt(hidden, w_ref[:, 2 * piece :])
    if carried:
        d_xb = d_xb + sums[0][0]
        out = out + sums[1][0]
    dxb_ref[0] = d_xb.astype(dxb_ref.dtype)
    out_ref[0] = out.astype(out_ref.dtype)


def feed_forward(xb, dy, w, order, sums, kind):
    length, width = xb.shape
    piece = w.shape[1] // 3
    count = order.shape[0]
    block = length // count
    rows = pl.BlockSpec((block, width), lambda i, order: (order[i], 0))
    whole = pl.BlockSpec(w.shape, lambda i, order: (0, 0), pipeline_mode=pl.Buffered(1))
    summed = pl.BlockSpec((1, block, width), lambda i, order: (i, 0, 0))
    total = jax.ShapeDtypeStruct((count, block, width), kind)
    return pl.pallas_call(
        functools.partial(feed_forward_kernel, bool(sums), piece),
        grid_spec=pltpu.PrefetchScalarGridSpec(
            num_scalar_prefetch=1,
            grid=(count,),
            in_specs=[rows, rows, whole] + [summed] * len(sums),
            out_specs=(
                pl.BlockSpec((block, 3 * piece), lambda i, order: (order[i], 0)),
                summed,
                summed,
            ),
        ),
        out_shape=(jax.ShapeDtypeStruct((length, 3 * piece), BF16), total, total),
        compiler_params=pltpu.CompilerParams(vmem_limit_bytes=60 << 20),
        cost_estimate=TINY,
        name="feed_forward",
    )(order, xb, dy, w, *sums)


def place_kernel(widths, tiles, pieces, order_ref, *refs):
    outs = refs[-len(widths) :]
    k, t = pl.program_id(0), pl.program_id(1)
    for n in range(pl.num_programs(0)):
        mine = refs[sum(pieces[:n]) : sum(pieces[: n + 1])]
        for m in range(tiles):

            @pl.when((k == n) & (t == m))
            def _():
                start = 0
                for out_ref, width in zip(outs, widths):
                    size = width // tiles
                    at, row = start + m * size, 0
                    for piece in mine:
                        rows = piece.shape[0]
                        out_ref[row : row + rows, :] = piece[:, at : at + size].astype(F32)
                        row += rows
                    start += width


def place(blocks, widths, tiles, first, every, outs, count):
    pieces = [piece for _, rows in blocks for piece in rows]
    rows = sum(piece.shape[0] for piece in blocks[0][1])

    def out_map(k, t, order_ref):
        return 0, order_ref[k] * every + first + t

    any_spec = pl.BlockSpec(memory_space=pl.ANY)
    n = len(pieces)
    return pl.pallas_call(
        functools.partial(place_kernel, widths, tiles, [len(x) for _, x in blocks]),
        grid_spec=pltpu.PrefetchScalarGridSpec(
            num_scalar_prefetch=1,
            grid=(len(blocks), tiles),
            in_specs=[pl.BlockSpec(x.shape, lambda k, t, order_ref: (0, 0)) for x in pieces]
            + [any_spec] * len(outs),
            out_specs=[pl.BlockSpec((rows, w // tiles), out_map) for w in widths],
        ),
        out_shape=[
            jax.ShapeDtypeStruct((rows, w // tiles * every * count), F32) for w in widths
        ],
        input_output_aliases={1 + n + m: m for m in range(len(outs))},
        compiler_params=pltpu.CompilerParams(vmem_limit_bytes=40 << 20),
        name="place",
        cost_estimate=TINY,
    )(jnp.stack([k for k, _ in blocks]).astype(jnp.int32), *pieces, *outs)


def make_body(counts):
    seq_count, fsdp_count = counts["seq"], counts["fsdp"]

    def body(
        tokens,
        segment_ids,
        input_gain,
        query_weight,
        key_projection_weight,
        value_projection_weight,
        output_weight,
        query_gain,
        key_gain,
        post_gain,
        gate_weight,
        up_weight,
        down_weight,
        cotangent,
    ):
        me = lax.axis_index("seq")
        rows = query_weight.shape[0]
        q_heads = QUERY_HEADS // seq_count
        kv_heads = KEY_VALUE_HEADS // seq_count
        ratio = QUERY_HEADS // KEY_VALUE_HEADS
        q_cols, kv_cols = q_heads * HEAD_SIZE, kv_heads * HEAD_SIZE
        qkv_cols = q_cols + 2 * kv_cols
        f_cols = gate_weight.shape[1] // seq_count
        pieces = (f_cols // 3 * 2, f_cols // 3)
        def share(w, cols, start=0, size=None):
            return lax.dynamic_slice(w, (0, me * cols + start), (rows, size or cols))

        w_attn = gather_weight(
            jnp.concatenate(
                [
                    share(query_weight, q_cols),
                    share(key_projection_weight, kv_cols),
                    share(value_projection_weight, kv_cols),
                    share(output_weight, q_cols),
                ],
                axis=1,
            )
        )
        w_qkv, w_out = w_attn[:, :qkv_cols], w_attn[:, qkv_cols:]
        w_mlp = [
            gather_weight(
                jnp.concatenate(
                    [share(w, f_cols, start, size) for w in (gate_weight, up_weight, down_weight)],
                    axis=1,
                )
            )
            for start, size in zip((0, pieces[0]), pieces)
        ]

        inputs = tokens[0].astype(F32)
        segments = segment_ids[0]
        order = slot_order(seq_count)
        get_dy = Gather(cotangent[0], seq_count)
        get_dy.first()
        get_xa = Gather((inputs * inverse_rms(inputs) * input_gain).astype(BF16), seq_count)
        get_xa.first()
        get_xa.second()
        xa = get_xa.column()

        place_in_document = positions(segments)
        tables = rotary_tables(place_in_document)
        start = (jnp.arange(segments.shape[0], dtype=jnp.int32) - place_in_document)[:, None]
        head_gains = query_gain[None, :], key_gain[None, :]
        qkv = dot(xa, w_qkv).astype(BF16)
        get_dy.second(qkv)
        dy = get_dy.column()
        o = attend(qkv, tables, start, head_gains, q_heads, kv_heads)
        sum_r, _ = scattered_product(after(o, dy), w_out, order, seq_count)
        resid = inputs + sum_r.finish()
        get_xb = Gather((resid * inverse_rms(resid) * post_gain).astype(BF16), seq_count)
        get_xb.first()
        get_xb.second()
        xb = get_xb.column()

        d1, *sums = feed_forward(xb, dy, w_mlp[0], order, (), F32)
        red1 = Reduction([(xb, 2), (dy, 1)], d1, fsdp_count)
        terms1 = red1.odd()
        share1 = red1.total()
        xb2 = after(xb, terms1)
        d2, d_xb, out = feed_forward(xb2, dy, w_mlp[1], order, tuple(sums), BF16)
        sum_dxb, sum_out = Scatter(seq_count), Scatter(seq_count)
        half = d_xb.shape[1] // 2
        got = sum_dxb.first(d_xb[-1, :half], d_xb[-1, half:])
        got += sum_out.first(out[-1, :half], out[-1, half:])
        sum_dxb.second(after(d_xb, *got))
        red2 = Reduction([(xb, 2), (dy, 1)], d2, fsdp_count)
        terms2 = red2.odd(*sum_dxb.sent)
        du, post_terms = norm_back(resid, post_gain, after(sum_dxb.finish(), terms2))
        d_resid = cotangent[0].astype(F32) + du
        get_drl = Gather(d_resid.astype(BF16), seq_count)
        get_drl.first()
        get_drl.second()
        share2 = red2.total(*get_drl.sent)
        drl = get_drl.column()
        halves = sum_out.second(out, drl)
        d_o = dot(drl, w_out).astype(BF16)
        dq, dk, dv, q_terms, k_terms = attend_back(
            qkv, tables, start, head_gains, after(d_o, *sum_out.sent), o, q_heads, kv_heads
        )
        dq = after(dq, *halves)
        get1 = Gather(after(share1, dq), seq_count)
        near = get1.first()
        d_attn = jnp.concatenate([dq, dk, dv, o], axis=1)
        red3 = Reduction([(xa, 2), (drl, 1)], d_attn, fsdp_count)
        terms3 = red3.odd()
        d_qkv = after(d_attn, terms3)[:, :qkv_cols]
        sum_dxa, got = scattered_product(
            d_qkv, w_qkv, order, seq_count, *near, *get1.cut(), early=False
        )
        get1.second(*got)
        out = resid + after(sum_out.finish(), *got)
        share3 = red3.total(share2, *got)
        du, in_terms = norm_back(inputs, input_gain, after(sum_dxa.finish(), *get1.arrived()))
        d_inputs = d_resid + du

        gains = jnp.concatenate(
            [
                jnp.sum(in_terms, axis=0),
                jnp.sum(post_terms, axis=0),
                jnp.sum(q_terms, axis=(0, 1)),
                jnp.sum(k_terms, axis=(0, 1)),
            ]
        )
        width = post_gain.shape[0]
        get2 = Gather(after(share2, *get1.arrived(), *sum_dxa.arrived()), seq_count)
        get2.first()
        gains = sum_all(gains, "fsdp", fsdp_count)
        mlp = place(get1.all(), (pieces[0],) * 3, 2, 0, 3, (), seq_count)
        get2.second(*mlp)
        get3 = Gather(after(share3, *get2.arrived()), seq_count)
        get3.first()
        mlp = place(get2.all(), (pieces[1],) * 3, 1, 2, 3, mlp, seq_count)
        gains = sum_all(after(gains, *get2.arrived()), "seq", seq_count)
        get3.second(gains, *mlp)
        widths = (q_cols, kv_cols, kv_cols, q_cols)
        attn = place(get3.near(), widths, 1, 0, 1, (), seq_count)
        if get3.far():
            attn = place(get3.far(), widths, 1, 0, 1, attn, seq_count)
        g_q, g_k, g_v, g_out = attn
        return (
            out.astype(BF16)[None],
            d_inputs.astype(BF16)[None],
            gains[:width],
            g_q,
            g_k,
            g_v,
            g_out,
            gains[2 * width : 2 * width + HEAD_SIZE],
            gains[2 * width + HEAD_SIZE :],
            gains[width : 2 * width],
            *mlp,
        )

    return body


def solution(mesh):
    rows, acts = P("fsdp", None), P("fsdp", "seq", None)
    return jax.shard_map(
        make_body({"seq": mesh.shape["seq"], "fsdp": mesh.shape["fsdp"]}),
        mesh=mesh,
        in_specs=(
            acts, rows, P(), rows, rows, rows, rows, P(), P(), P(), rows, rows, rows, acts,
        ),
        out_specs=(acts, acts, P(), rows, rows, rows, rows, P(), P(), P(), rows, rows, rows),
        check_vma=False,
    )
```

```python
import functools

import jax
import jax.numpy as jnp
from jax import lax
from jax.experimental import pallas as pl
from jax.experimental.pallas import tpu as pltpu
from jax.sharding import PartitionSpec as P

QUERY_HEADS = 16
KEY_VALUE_HEADS = 8
HEAD_SIZE = 128
NORM_EPSILON = 1e-06
ROPE_BASE = 1000000.0
F32 = jnp.float32
BF16 = jnp.bfloat16
TINY = pl.CostEstimate(flops=1000, bytes_accessed=1000, transcendentals=0)


def dot(a, b):
    return jnp.dot(a, b, preferred_element_type=F32)


def dot_nt(a, b):
    return lax.dot_general(a, b, (((1,), (1,)), ((), ())), preferred_element_type=F32)


def dot_tn(a, b):
    return lax.dot_general(a, b, (((0,), (0,)), ((), ())), preferred_element_type=F32)


def inverse_rms(u):
    return lax.rsqrt(jnp.mean(u * u, axis=-1, keepdims=True) + NORM_EPSILON)


def norm_back(u, gain, e):
    w = inverse_rms(u)
    n = u * w
    t = e * gain
    du = w * (t - n * jnp.mean(n * t, axis=-1, keepdims=True))
    return du, e * n


def positions(segments):
    index = jnp.arange(segments.shape[0], dtype=jnp.int32)
    first = jnp.concatenate([jnp.ones((1,), dtype=jnp.bool_), segments[1:] != segments[:-1]])
    starts = lax.cummax(jnp.where(first, index, jnp.zeros_like(index)), axis=0)
    return index - starts


def rotary_tables(position_index):
    half = HEAD_SIZE // 2
    freq = ROPE_BASE ** (-jnp.arange(half, dtype=F32) * 2.0 / HEAD_SIZE)
    angle = position_index.astype(F32)[:, None] * freq[None, :]
    cosine, sine = jnp.cos(angle), jnp.sin(angle)
    return jnp.concatenate([cosine, cosine], axis=-1), jnp.concatenate([-sine, sine], axis=-1)


def by_neighbours(count):
    return count == 4


def swap(x, side):
    return lax.ppermute(x, "seq", [(s, s ^ side) for s in range(4)])


def put_rows_kernel(count, order_ref, *refs):
    for n in range(count):

        @pl.when(pl.program_id(0) == n)
        def _():
            refs[-1][...] = refs[n][...]


def put_rows(pieces, offsets, parts, out):
    me = lax.axis_index("seq")
    blocks = [(me ^ k) * parts + n % parts for n, k in enumerate(offsets)]
    rows, c = pieces[0].shape
    kept = [] if out is None else [out]
    return pl.pallas_call(
        functools.partial(put_rows_kernel, len(pieces)),
        grid_spec=pltpu.PrefetchScalarGridSpec(
            num_scalar_prefetch=1,
            grid=(len(pieces),),
            in_specs=[pl.BlockSpec((rows, c), lambda n, order: (0, 0))] * len(pieces)
            + [pl.BlockSpec(memory_space=pl.ANY)] * len(kept),
            out_specs=pl.BlockSpec((rows, c), lambda n, order: (order[n], 0)),
        ),
        out_shape=jax.ShapeDtypeStruct((4 * parts * rows, c), pieces[0].dtype),
        input_output_aliases={1 + len(pieces): 0} if kept else {},
        compiler_params=pltpu.CompilerParams(vmem_limit_bytes=60 << 20),
        cost_estimate=TINY,
        name="put_rows",
    )(jnp.stack(blocks).astype(jnp.int32), *pieces, *kept)


class Scatter:
    def __init__(self, count):
        self.square = by_neighbours(count)

    def first(self, top, low):
        if not self.square:
            return [top]
        self.tx, self.ty = swap(top, 1), swap(low, 2)
        return [self.tx, self.ty]

    def second(self, slots, *others):
        self.slots = slots
        if not self.square:
            every = after(slots, *others).reshape(-1, slots.shape[-1])
            self.sum = lax.psum_scatter(every, "seq", scatter_dimension=0, tiled=True)
            self.sent = [every]
            return [self.sum]
        sx, sy = add_halves(slots, self.tx, self.ty)
        if others:
            sx, sy, *_ = lax.optimization_barrier((sx, sy, *others))
        self.sent = [sx, sy]
        self.rx, self.ry = swap(sx, 1), swap(sy, 2)
        return [self.rx, self.ry]

    def arrived(self):
        return [self.rx, self.ry] if self.square else [self.sum]

    def finish(self):
        if not self.square:
            return self.sum.astype(F32)
        return self.slots[0].astype(F32) + self.rx.astype(F32) + self.ry.astype(F32)


def add_halves_kernel(one_ref, two_ref, tx_ref, ty_ref, sx_ref, sy_ref):
    half = tx_ref.shape[0]
    sx_ref[:half] = one_ref[0, :half]
    sx_ref[half:] = (one_ref[0, half:].astype(F32) + ty_ref[...].astype(F32)).astype(BF16)
    sy_ref[:half] = (two_ref[0, :half].astype(F32) + tx_ref[...].astype(F32)).astype(BF16)
    sy_ref[half:] = two_ref[0, half:]


def add_halves(slots, tx, ty):
    _, rows, c = slots.shape
    half = pl.BlockSpec((rows // 2, c), lambda i: (0, 0))
    whole = pl.BlockSpec((rows, c), lambda i: (0, 0))
    return pl.pallas_call(
        add_halves_kernel,
        grid=(1,),
        in_specs=[
            pl.BlockSpec((1, rows, c), lambda i: (1, 0, 0)),
            pl.BlockSpec((1, rows, c), lambda i: (2, 0, 0)),
            half,
            half,
        ],
        out_specs=(whole, whole),
        out_shape=[jax.ShapeDtypeStruct((rows, c), slots.dtype)] * 2,
        compiler_params=pltpu.CompilerParams(vmem_limit_bytes=60 << 20),
        cost_estimate=TINY,
        name="add_halves",
    )(slots, slots, tx, ty)


def slot_order(count):
    me = lax.axis_index("seq")
    members = [me ^ k if by_neighbours(count) else jnp.int32(k) for k in range(count)]
    return jnp.stack(members).astype(jnp.int32)


def slot_rows(x, order, count, slots):
    rows = x.shape[0] // count
    return jnp.concatenate(
        [lax.dynamic_slice_in_dim(x, order[k] * rows, rows, 0) for k in slots], axis=0
    )


def scattered_product(x, w, order, count, *others, early=True):
    total = Scatter(count)
    rows = x.shape[0] // count
    if not total.square:
        total.last = terms = dot_nt(x, w).astype(BF16)
        total.second(terms.reshape(count, rows, w.shape[0]))
        return total, [terms]
    if early:
        last = dot_nt(slot_rows(x, order, count, (3,)), w).astype(BF16)
        rest = dot_nt(slot_rows(x, order, count, (0, 1, 2)), w).astype(BF16)
        rest = rest.reshape(3, rows, w.shape[0])
    else:
        rest = dot_nt(slot_rows(x, order, count, range(4)), w).astype(BF16)
        rest = rest.reshape(4, rows, w.shape[0])
        last = rest[3]
    total.last = after(last, *others)
    got = total.first(total.last[: rows // 2], total.last[rows // 2 :])
    total.second(rest)
    return total, got


class Gather:
    def __init__(self, x, count):
        self.x, self.count = x, count
        self.square = by_neighbours(count)
        self.me = lax.axis_index("seq")
        self.halves = None

    def first(self):
        if not self.square:
            return [self.x]
        self.bx, self.by = swap(self.x, 1), swap(self.x, 2)
        return [self.bx, self.by]

    def cut(self):
        if not self.square:
            return [self.x]
        if not self.halves:
            half = self.x.shape[0] // 2
            self.halves = [self.by[:half], self.bx[half:]]
        return self.halves

    def second(self, *others):
        if not self.square:
            self.sent = [self.x]
            return [self.x]
        ahead, below = self.cut()
        if others:
            ahead, below, *_ = lax.optimization_barrier((ahead, below, *others))
        self.sent = [ahead, below]
        self.ad, self.bd = swap(ahead, 1), swap(below, 2)
        return [self.ad, self.bd]

    def column(self):
        if not self.square:
            return lax.all_gather(self.x, "seq", axis=0, tiled=True)
        near = put_rows((self.x, self.bx, self.by), (0, 1, 2), 1, None)
        return put_rows((self.ad, self.bd), (3, 3), 2, near)

    def arrived(self):
        return [piece for _, rows in self.all() for piece in rows]

    def near(self):
        if not self.square:
            every = lax.all_gather(self.x, "seq", axis=0, tiled=False)
            return [(jnp.int32(k), (every[k],)) for k in range(self.count)]
        return [(self.me ^ k, (x,)) for k, x in enumerate((self.x, self.bx, self.by))]

    def all(self):
        return self.near() + [
            (member, (jnp.concatenate(rows, axis=0),)) for member, rows in self.far()
        ]

    def far(self):
        return [(self.me ^ 3, (self.ad, self.bd))] if self.square else []


def after(x, *others):
    return lax.optimization_barrier((x, *others))[0]


def in_line(count):
    return count == 8


def gather_weight(w):
    return lax.all_gather(w, "fsdp", axis=0, tiled=True)


def other_core(x):
    return lax.ppermute(x, "fsdp", [(f, f ^ 1) for f in range(8)])


def terms_kernel(starts, blocks, stride, parity_ref, *refs):
    count = len(starts)
    x_refs, d_ref, out_ref = refs[:count], refs[count], refs[-1]
    rows = out_ref.shape[0] // blocks
    j = pl.program_id(0)
    for n, x_ref in enumerate(x_refs):
        last = starts[n + 1] if n + 1 < count else pl.num_programs(0)

        @pl.when((j >= starts[n]) & (j < last))
        def _():
            for i in range(blocks):
                at = pl.multiple_of((stride * i + parity_ref[0]) * rows, rows)
                terms = dot_tn(x_ref[:, pl.ds(at, rows)], d_ref[...])
                here = slice(i * rows, (i + 1) * rows)
                if len(refs) == count + 3:
                    terms = terms + refs[count + 1][here].astype(F32)
                out_ref[here] = terms.astype(BF16)


def weight_terms(xs, d, blocks, stride, parity, got=None):
    length, columns = xs[0][0].shape
    tiles = sum(n for _, n in xs)
    width = d.shape[1] // tiles
    starts = [sum(n for _, n in xs[:m]) for m in range(len(xs))]
    whole = pl.BlockSpec(
        (length, columns), lambda j, parity: (0, 0), pipeline_mode=pl.Buffered(1)
    )
    terms = pl.BlockSpec((columns // stride, width), lambda j, parity: (0, j))
    operands = [x for x, _ in xs] + [d] + ([] if got is None else [got])
    return pl.pallas_call(
        functools.partial(terms_kernel, starts, blocks, stride),
        grid_spec=pltpu.PrefetchScalarGridSpec(
            num_scalar_prefetch=1,
            grid=(tiles,),
            in_specs=[whole] * len(xs)
            + [pl.BlockSpec((length, width), lambda j, parity: (0, j))]
            + ([] if got is None else [terms]),
            out_specs=terms,
        ),
        out_shape=jax.ShapeDtypeStruct((columns // stride, d.shape[1]), BF16),
        compiler_params=pltpu.CompilerParams(vmem_limit_bytes=58 << 20),
        cost_estimate=TINY,
        name="weight_terms",
    )(jnp.reshape(parity, (1,)).astype(jnp.int32), *operands)


class Reduction:
    def __init__(self, xs, d, count, by_core=False):
        self.xs, self.d, self.count = xs, d, count
        self.line = by_core and in_line(count)
        self.core = lax.axis_index("fsdp") % 2

    def odd(self, *others):
        d = after(self.d, *others)
        if self.line:
            self.terms = weight_terms(self.xs, d, 4, 2, 1 - self.core)
            self.got = other_core(self.terms)
        else:
            self.terms = self.got = weight_terms(self.xs, d, 4, 1, jnp.int32(0))
        return self.terms

    def even(self, *others):
        if self.line:
            d = after(self.d, *others)
            self.terms = weight_terms(self.xs, d, 4, 2, self.core, self.got)
        return self.terms

    def total(self, *others):
        terms = after(self.terms, *others)
        groups = [[0, 2, 4, 6], [1, 3, 5, 7]] if self.line else None
        return lax.psum_scatter(
            terms, "fsdp", scatter_dimension=0, axis_index_groups=groups, tiled=True
        )


def sum_all(x, axis, count):
    if count & (count - 1):
        return lax.psum(x, axis)
    bit = 1
    while bit < count:
        x = x + lax.ppermute(x, axis, [(i, i ^ bit) for i in range(count)])
        bit *= 2
    return x


BLOCK = 128
SCALE = HEAD_SIZE ** (-0.5)
LOG2_E = 1.4426950408889634


def head_norm_rope(u, gain, cosine, sine):
    w = inverse_rms(u)
    t = u * w * gain
    return (t * cosine + pltpu.roll(t, HEAD_SIZE // 2, 1) * sine).astype(BF16)


def head_norm_rope_back(u, gain, cosine, sine, e):
    e = e * cosine - pltpu.roll(e, HEAD_SIZE // 2, 1) * sine
    return norm_back(u, gain, e)


def heads_of(refs, gains, cosine, sine, ratio):
    q_ref, k_ref = refs
    queries = [
        head_norm_rope(
            q_ref[:, h * HEAD_SIZE : (h + 1) * HEAD_SIZE].astype(F32), gains[0], cosine, sine
        )
        for h in range(ratio)
    ]
    return queries, head_norm_rope(k_ref[...].astype(F32), gains[1], cosine, sine)


def softmax_rows(queries, key, start, block, i):
    before, keys = i * block, (i + 1) * block
    stacked = jnp.concatenate([q[before:keys] for q in queries], axis=0)
    s = dot_nt(stacked, key[:keys]) * (SCALE * LOG2_E)
    first = jnp.concatenate([start[before:keys]] * len(queries), axis=0)
    here = (s.shape[0], block)
    place = lax.broadcasted_iota(jnp.int32, here, 0) % block
    index = lax.broadcasted_iota(jnp.int32, here, 1)
    allowed = (index <= place) & (index + before >= first)
    e = jnp.where(allowed, jnp.exp2(s[:, before:]), 0.0)
    if before:
        index = lax.broadcasted_iota(jnp.int32, (s.shape[0], before), 1)
        earlier = jnp.where(index >= first, jnp.exp2(s[:, :before]), 0.0)
        e = jnp.concatenate([earlier, e], axis=1)
    return stacked, e * (1.0 / jnp.sum(e, axis=-1, keepdims=True))


def attend_kernel(
    ratio, q_ref, k_ref, v_ref, cos_ref, sin_ref, start_ref, qg_ref, kg_ref, o_ref
):
    gains = qg_ref[...], kg_ref[...]
    queries, key = heads_of((q_ref, k_ref), gains, cos_ref[...], sin_ref[...], ratio)
    start, block = start_ref[...], BLOCK
    for i in range(q_ref.shape[0] // block):
        keys = (i + 1) * block
        _, p = softmax_rows(queries, key, start, block, i)
        o = dot(p.astype(BF16), v_ref[:keys, :]).astype(BF16)
        for h in range(ratio):
            o_ref[i * block : keys, h * HEAD_SIZE : (h + 1) * HEAD_SIZE] = o[
                h * block : (h + 1) * block
            ]


def attend_back_kernel(
    ratio,
    q_ref,
    k_ref,
    v_ref,
    cos_ref,
    sin_ref,
    start_ref,
    qg_ref,
    kg_ref,
    do_ref,
    o_ref,
    dq_ref,
    dk_ref,
    dv_ref,
    qgg_ref,
    kgg_ref,
    dq_all,
    dk_all,
    dv_all,
):
    gains = qg_ref[...], kg_ref[...]
    cosine, sine = cos_ref[...], sin_ref[...]
    queries, key = heads_of((q_ref, k_ref), gains, cosine, sine, ratio)
    start = start_ref[...]
    dk_all[...] = jnp.zeros_like(dk_all)
    dv_all[...] = jnp.zeros_like(dv_all)
    products = do_ref[...].astype(F32) * o_ref[...].astype(F32)
    deltas = [
        jnp.sum(products[:, h * HEAD_SIZE : (h + 1) * HEAD_SIZE], axis=-1, keepdims=True)
        for h in range(ratio)
    ]
    for i in range(q_ref.shape[0] // BLOCK):
        before, keys = i * BLOCK, (i + 1) * BLOCK
        stacked, p = softmax_rows(queries, key, start, BLOCK, i)
        do = jnp.concatenate(
            [do_ref[before:keys, h * HEAD_SIZE : (h + 1) * HEAD_SIZE] for h in range(ratio)], axis=0
        )
        delta = jnp.concatenate([x[before:keys] for x in deltas], axis=0)
        ds = (p * (dot_nt(do, v_ref[:keys, :]) - delta)).astype(BF16)
        dq = dot(ds, key[:keys]) * SCALE
        for h in range(ratio):
            dq_all[h, before:keys, :] = dq[h * BLOCK : (h + 1) * BLOCK]
        dk_all[:keys, :] += dot_tn(ds, stacked)
        dv_all[:keys, :] += dot_tn(p.astype(BF16), do)

    q_terms = jnp.zeros((1, HEAD_SIZE), F32)
    for h in range(ratio):
        columns = slice(h * HEAD_SIZE, (h + 1) * HEAD_SIZE)
        du, terms = head_norm_rope_back(
            q_ref[:, columns].astype(F32), gains[0], cosine, sine, dq_all[h]
        )
        dq_ref[:, columns] = du.astype(BF16)
        q_terms = q_terms + jnp.sum(terms, axis=0, keepdims=True)
    du, terms = head_norm_rope_back(
        k_ref[...].astype(F32), gains[1], cosine, sine, dk_all[...] * SCALE
    )
    dk_ref[...] = du.astype(BF16)
    dv_ref[...] = dv_all[...].astype(BF16)
    qgg_ref[0] = q_terms
    kgg_ref[0] = jnp.sum(terms, axis=0, keepdims=True)


def attention_specs(length, q_heads, kv_heads):
    ratio = q_heads // kv_heads
    wide = pl.BlockSpec((length, ratio * HEAD_SIZE), lambda g: (0, g))
    narrow = pl.BlockSpec((length, HEAD_SIZE), lambda g: (0, g))
    table = pl.BlockSpec((length, HEAD_SIZE), lambda g: (0, 0))
    gain = pl.BlockSpec((1, HEAD_SIZE), lambda g: (0, 0))
    inputs = [
        wide,
        pl.BlockSpec((length, HEAD_SIZE), lambda g: (0, q_heads + g)),
        pl.BlockSpec((length, HEAD_SIZE), lambda g: (0, q_heads + kv_heads + g)),
        table,
        table,
        pl.BlockSpec((length, 1), lambda g: (0, 0)),
        gain,
        gain,
    ]
    return ratio, wide, narrow, inputs


def attention_cost(length, q_heads, products):
    flops = products * q_heads * length * length * HEAD_SIZE
    return pl.CostEstimate(
        flops=flops, bytes_accessed=16 * length * q_heads * HEAD_SIZE, transcendentals=q_heads * length * length
    )


def attend(qkv, tables, start, gains, q_heads, kv_heads):
    length = qkv.shape[0]
    ratio, wide, _, inputs = attention_specs(length, q_heads, kv_heads)
    return pl.pallas_call(
        functools.partial(attend_kernel, ratio),
        grid=(kv_heads,),
        in_specs=inputs,
        out_specs=wide,
        out_shape=jax.ShapeDtypeStruct((length, q_heads * HEAD_SIZE), BF16),
        compiler_params=pltpu.CompilerParams(vmem_limit_bytes=56 << 20),
        cost_estimate=TINY,
        name="attend",
    )(qkv, qkv, qkv, *tables, start, *gains)


def attend_back(qkv, tables, start, gains, d_o, o, q_heads, kv_heads):
    length = qkv.shape[0]
    ratio, wide, narrow, inputs = attention_specs(length, q_heads, kv_heads)
    gain_spec = pl.BlockSpec((1, 1, HEAD_SIZE), lambda g: (g, 0, 0))
    gain_shape = jax.ShapeDtypeStruct((kv_heads, 1, HEAD_SIZE), F32)
    kv_shape = jax.ShapeDtypeStruct((length, kv_heads * HEAD_SIZE), BF16)
    return pl.pallas_call(
        functools.partial(attend_back_kernel, ratio),
        grid=(kv_heads,),
        in_specs=inputs + [wide, wide],
        out_specs=(wide, narrow, narrow, gain_spec, gain_spec),
        out_shape=(
            jax.ShapeDtypeStruct((length, q_heads * HEAD_SIZE), BF16),
            kv_shape,
            kv_shape,
            gain_shape,
            gain_shape,
        ),
        scratch_shapes=[
            pltpu.VMEM((ratio, length, HEAD_SIZE), F32),
            pltpu.VMEM((length, HEAD_SIZE), F32),
            pltpu.VMEM((length, HEAD_SIZE), F32),
        ],
        compiler_params=pltpu.CompilerParams(vmem_limit_bytes=56 << 20),
        cost_estimate=TINY,
        name="attend_back",
    )(qkv, qkv, qkv, *tables, start, *gains, d_o, o)


def feed_forward_kernel(carried, piece, order_ref, xb_ref, dy_ref, w_ref, *refs):
    sums = refs[:2] if carried else (None, None)
    d_ref, dxb_ref, out_ref = refs[-3:]
    xb, dy = xb_ref[...], dy_ref[...]
    gate = dot(xb, w_ref[:, :piece])
    upper = dot(xb, w_ref[:, piece : 2 * piece])
    d_hidden = dot(dy, w_ref[:, 2 * piece :])
    sigma = 1.0 / (1.0 + jnp.exp(-gate))
    silu = gate * sigma
    hidden = (silu * upper).astype(BF16)
    d_gate = (d_hidden * upper * sigma * (1.0 + gate * (1.0 - sigma))).astype(BF16)
    d_up = (d_hidden * silu).astype(BF16)
    d_ref[:, :piece] = d_gate
    d_ref[:, piece : 2 * piece] = d_up
    d_ref[:, 2 * piece :] = hidden
    d_xb = dot_nt(d_gate, w_ref[:, :piece]) + dot_nt(d_up, w_ref[:, piece : 2 * piece])
    out = dot_nt(hidden, w_ref[:, 2 * piece :])
    if carried:
        d_xb = d_xb + sums[0][0]
        out = out + sums[1][0]
    dxb_ref[0] = d_xb.astype(dxb_ref.dtype)
    out_ref[0] = out.astype(out_ref.dtype)


def feed_forward(xb, dy, w, order, sums, kind):
    length, width = xb.shape
    piece = w.shape[1] // 3
    count = order.shape[0]
    block = length // count
    rows = pl.BlockSpec((block, width), lambda i, order: (order[i], 0))
    whole = pl.BlockSpec(w.shape, lambda i, order: (0, 0), pipeline_mode=pl.Buffered(1))
    summed = pl.BlockSpec((1, block, width), lambda i, order: (i, 0, 0))
    total = jax.ShapeDtypeStruct((count, block, width), kind)
    return pl.pallas_call(
        functools.partial(feed_forward_kernel, bool(sums), piece),
        grid_spec=pltpu.PrefetchScalarGridSpec(
            num_scalar_prefetch=1,
            grid=(count,),
            in_specs=[rows, rows, whole] + [summed] * len(sums),
            out_specs=(
                pl.BlockSpec((block, 3 * piece), lambda i, order: (order[i], 0)),
                summed,
                summed,
            ),
        ),
        out_shape=(jax.ShapeDtypeStruct((length, 3 * piece), BF16), total, total),
        compiler_params=pltpu.CompilerParams(vmem_limit_bytes=60 << 20),
        cost_estimate=TINY,
        name="feed_forward",
    )(order, xb, dy, w, *sums)


def place_kernel(widths, tiles, pieces, order_ref, *refs):
    outs = refs[-len(widths) :]
    k, t = pl.program_id(0), pl.program_id(1)
    for n in range(pl.num_programs(0)):
        mine = refs[sum(pieces[:n]) : sum(pieces[: n + 1])]
        for m in range(tiles):

            @pl.when((k == n) & (t == m))
            def _():
                start = 0
                for out_ref, width in zip(outs, widths):
                    size = width // tiles
                    at, row = start + m * size, 0
                    for piece in mine:
                        rows = piece.shape[0]
                        out_ref[row : row + rows, :] = piece[:, at : at + size].astype(F32)
                        row += rows
                    start += width


def place(blocks, widths, tiles, first, every, outs, count):
    pieces = [piece for _, rows in blocks for piece in rows]
    rows = sum(piece.shape[0] for piece in blocks[0][1])

    def out_map(k, t, order_ref):
        return 0, order_ref[k] * every + first + t

    any_spec = pl.BlockSpec(memory_space=pl.ANY)
    n = len(pieces)
    return pl.pallas_call(
        functools.partial(place_kernel, widths, tiles, [len(x) for _, x in blocks]),
        grid_spec=pltpu.PrefetchScalarGridSpec(
            num_scalar_prefetch=1,
            grid=(len(blocks), tiles),
            in_specs=[pl.BlockSpec(x.shape, lambda k, t, order_ref: (0, 0)) for x in pieces]
            + [any_spec] * len(outs),
            out_specs=[pl.BlockSpec((rows, w // tiles), out_map) for w in widths],
        ),
        out_shape=[
            jax.ShapeDtypeStruct((rows, w // tiles * every * count), F32) for w in widths
        ],
        input_output_aliases={1 + n + m: m for m in range(len(outs))},
        compiler_params=pltpu.CompilerParams(vmem_limit_bytes=40 << 20),
        name="place",
        cost_estimate=TINY,
    )(jnp.stack([k for k, _ in blocks]).astype(jnp.int32), *pieces, *outs)


def make_body(counts):
    seq_count, fsdp_count = counts["seq"], counts["fsdp"]

    def body(
        tokens,
        segment_ids,
        input_gain,
        query_weight,
        key_projection_weight,
        value_projection_weight,
        output_weight,
        query_gain,
        key_gain,
        post_gain,
        gate_weight,
        up_weight,
        down_weight,
        cotangent,
    ):
        me = lax.axis_index("seq")
        rows = query_weight.shape[0]
        q_heads = QUERY_HEADS // seq_count
        kv_heads = KEY_VALUE_HEADS // seq_count
        ratio = QUERY_HEADS // KEY_VALUE_HEADS
        q_cols, kv_cols = q_heads * HEAD_SIZE, kv_heads * HEAD_SIZE
        qkv_cols = q_cols + 2 * kv_cols
        f_cols = gate_weight.shape[1] // seq_count
        pieces = (f_cols // 3 * 2, f_cols // 3)
        def share(w, cols, start=0, size=None):
            return lax.dynamic_slice(w, (0, me * cols + start), (rows, size or cols))

        w_attn = gather_weight(
            jnp.concatenate(
                [
                    share(query_weight, q_cols),
                    share(key_projection_weight, kv_cols),
                    share(value_projection_weight, kv_cols),
                    share(output_weight, q_cols),
                ],
                axis=1,
            )
        )
        w_qkv, w_out = w_attn[:, :qkv_cols], w_attn[:, qkv_cols:]
        w_mlp = [
            gather_weight(
                jnp.concatenate(
                    [share(w, f_cols, start, size) for w in (gate_weight, up_weight, down_weight)],
                    axis=1,
                )
            )
            for start, size in zip((0, pieces[0]), pieces)
        ]

        inputs = tokens[0].astype(F32)
        segments = segment_ids[0]
        order = slot_order(seq_count)
        get_dy = Gather(cotangent[0], seq_count)
        get_dy.first()
        get_xa = Gather((inputs * inverse_rms(inputs) * input_gain).astype(BF16), seq_count)
        get_xa.first()
        get_xa.second()
        xa = get_xa.column()

        place_in_document = positions(segments)
        tables = rotary_tables(place_in_document)
        start = (jnp.arange(segments.shape[0], dtype=jnp.int32) - place_in_document)[:, None]
        head_gains = query_gain[None, :], key_gain[None, :]
        qkv = dot(xa, w_qkv).astype(BF16)
        get_dy.second(qkv)
        dy = get_dy.column()
        o = attend(qkv, tables, start, head_gains, q_heads, kv_heads)
        sum_r, _ = scattered_product(after(o, dy), w_out, order, seq_count)
        resid = inputs + sum_r.finish()
        get_xb = Gather((resid * inverse_rms(resid) * post_gain).astype(BF16), seq_count)
        get_xb.first()
        get_xb.second()
        xb = get_xb.column()

        d1, *sums = feed_forward(xb, dy, w_mlp[0], order, (), F32)
        red1 = Reduction([(xb, 2), (dy, 1)], d1, fsdp_count)
        terms1 = red1.odd()
        share1 = red1.total()
        xb2 = after(xb, terms1)
        d2, d_xb, out = feed_forward(xb2, dy, w_mlp[1], order, tuple(sums), BF16)
        sum_dxb, sum_out = Scatter(seq_count), Scatter(seq_count)
        half = d_xb.shape[1] // 2
        got = sum_dxb.first(d_xb[-1, :half], d_xb[-1, half:])
        got += sum_out.first(out[-1, :half], out[-1, half:])
        sum_dxb.second(after(d_xb, *got))
        red2 = Reduction([(xb, 2), (dy, 1)], d2, fsdp_count)
        terms2 = red2.odd(*sum_dxb.sent)
        du, post_terms = norm_back(resid, post_gain, after(sum_dxb.finish(), terms2))
        d_resid = cotangent[0].astype(F32) + du
        get_drl = Gather(d_resid.astype(BF16), seq_count)
        get_drl.first()
        get_drl.second()
        share2 = red2.total(*get_drl.sent)
        drl = get_drl.column()
        halves = sum_out.second(out, drl)
        d_o = dot(drl, w_out).astype(BF16)
        dq, dk, dv, q_terms, k_terms = attend_back(
            qkv, tables, start, head_gains, after(d_o, *sum_out.sent), o, q_heads, kv_heads
        )
        dq = after(dq, *halves)
        get1 = Gather(after(share1, dq), seq_count)
        near = get1.first()
        d_attn = jnp.concatenate([dq, dk, dv, o], axis=1)
        red3 = Reduction([(xa, 2), (drl, 1)], d_attn, fsdp_count)
        terms3 = red3.odd()
        d_qkv = after(d_attn, terms3)[:, :qkv_cols]
        sum_dxa, got = scattered_product(
            d_qkv, w_qkv, order, seq_count, *near, *get1.cut(), early=False
        )
        get1.second(*got)
        out = resid + after(sum_out.finish(), *got)
        share3 = red3.total(share2, *sum_dxa.sent)
        du, in_terms = norm_back(inputs, input_gain, after(sum_dxa.finish(), *get1.arrived()))
        d_inputs = d_resid + du

        gains = jnp.concatenate(
            [
                jnp.sum(in_terms, axis=0),
                jnp.sum(post_terms, axis=0),
                jnp.sum(q_terms, axis=(0, 1)),
                jnp.sum(k_terms, axis=(0, 1)),
            ]
        )
        width = post_gain.shape[0]
        get2 = Gather(after(share2, *get1.arrived(), *sum_dxa.arrived()), seq_count)
        get2.first()
        gains = sum_all(gains, "fsdp", fsdp_count)
        mlp = place(get1.all(), (pieces[0],) * 3, 2, 0, 3, (), seq_count)
        get2.second(*mlp)
        get3 = Gather(after(share3, *get2.arrived()), seq_count)
        get3.first()
        mlp = place(get2.all(), (pieces[1],) * 3, 1, 2, 3, mlp, seq_count)
        gains = sum_all(after(gains, *get2.arrived()), "seq", seq_count)
        get3.second(gains, *mlp)
        widths = (q_cols, kv_cols, kv_cols, q_cols)
        attn = place(get3.near(), widths, 1, 0, 1, (), seq_count)
        if get3.far():
            attn = place(get3.far(), widths, 1, 0, 1, attn, seq_count)
        g_q, g_k, g_v, g_out = attn
        return (
            out.astype(BF16)[None],
            d_inputs.astype(BF16)[None],
            gains[:width],
            g_q,
            g_k,
            g_v,
            g_out,
            gains[2 * width : 2 * width + HEAD_SIZE],
            gains[2 * width + HEAD_SIZE :],
            gains[width : 2 * width],
            *mlp,
        )

    return body


def solution(mesh):
    rows, acts = P("fsdp", None), P("fsdp", "seq", None)
    return jax.shard_map(
        make_body({"seq": mesh.shape["seq"], "fsdp": mesh.shape["fsdp"]}),
        mesh=mesh,
        in_specs=(
            acts, rows, P(), rows, rows, rows, rows, P(), P(), P(), rows, rows, rows, acts,
        ),
        out_specs=(acts, acts, P(), rows, rows, rows, rows, P(), P(), P(), rows, rows, rows),
        check_vma=False,
    )
```
